256 devices in a mesh: rep: 32 (over z, x), section: 4 (over y), tp: 2 (over core).
Axes of the slice: x: 4, y: 4, z: 8, core: 2. Of those that a mesh axis runs over, the one named last changes fastest.
Arguments:
- inputs: bfloat16 [4, 16384, 768], P('section', 'rep', 'tp'), may hold values from -6 to 6
- loss_grad: bfloat16 [16384, 768], P('rep', 'tp'), may hold values from -6 to 6
- w_in: bfloat16 [32, 4, 3072, 768], P('rep', 'section', 'tp'), may hold values from -6 to 6
- w_out: bfloat16 [32, 4, 3072, 768], P('rep', 'section', 'tp'), may hold values from -6 to 6
- mixing: float32 [32, 32], replicated, may hold values from 0 to 1, as said below
Outputs:
- input_grads: bfloat16 [4, 16384, 768], P('section', 'rep', 'tp')
- mixed_in: bfloat16 [32, 4, 3072, 768], P('rep', 'section', 'tp')
- mixed_out: bfloat16 [32, 4, 3072, 768], P('rep', 'section', 'tp')
The draws below stay inside these ranges and needn't reach their ends.
Inputs may be any that keep to these rules, and one draw needn't show every extreme that they name: `mixing`: every row and every column sums to one; every entry is positive.
All inputs are finite; a program needn't handle non-finite values.
Results may differ from the reference program's by a relative error of at most 0.023.
Values may be sent and summed in bfloat16 or wider, within the bound.
No kernel may reach another device: no remote copies, remote signals or barrier semaphores. Data moves between devices by JAX's collectives and lax.ppermute only.
A program may use at most 128 MiB of HBM per device.

```python
import jax
import jax.numpy as jnp
from jax import lax

D = 768
FF = 3072
TOK_DEV = 512
WIN_DEV = 1536
REP = 32
SECTIONS = 4
TOKENS = 16384
N_REP = 32
N_SECTION = 4
N_TP = 2


def draw_mixing(key, part):
    key = jax.random.fold_in(key, 11)
    subkeys = jax.random.split(key, 6)
    replicas = N_REP
    matrix_sum = jnp.zeros((replicas, replicas), jnp.float32)
    for member in range(2):
        weights = jax.random.uniform(subkeys[3 * member], (replicas,), jnp.float32, 0.2, 1.0)
        weights = weights / jnp.sum(weights)
        first_perm = jax.random.permutation(subkeys[3 * member + 1], replicas)
        second_perm = jax.random.permutation(subkeys[3 * member + 2], replicas)
        offsets = (second_perm[None, :] - first_perm[:, None]) % replicas
        matrix_sum = matrix_sum + 0.5 * weights[offsets]
    return matrix_sum


def block_levels(stream_key, extent, shards, low, top_value):
    def one(axis_at, blocks):
        steps = jax.random.uniform(jax.random.fold_in(jax.random.fold_in(stream_key, 6), axis_at), (blocks,), jnp.float32, low / len(shards), top_value / len(shards))
        return jnp.repeat(jnp.exp(steps), extent[axis_at] // blocks).reshape((-1,) + (1,) * (len(extent) - axis_at - 1))

    gain = one(*shards[0])
    for cut in shards[1:]:
        gain = gain * one(*cut)
    return gain


def bell_draw(stream_key, shape, width, reach, shards=(), held_as=jnp.bfloat16):
    level = block_levels(stream_key, shape, shards, -0.22, 0.18) if shards else 1.0
    values = jax.random.normal(stream_key, shape, jnp.float32) * width * level
    return jnp.minimum(jnp.maximum(values, -reach), reach).astype(held_as)


def setup_inputs(seed: int = 0) -> dict:
    splits = jax.random.split(jax.random.key(seed), 6)
    inputs = bell_draw(splits[0], (SECTIONS, TOKENS, D), 1.0, 6.0, ((0, 4), (1, 32), (2, 2)))
    loss_grad = bell_draw(splits[1], (TOKENS, D), 1.0, 6.0, ((0, 32), (1, 2)))
    w_in = bell_draw(splits[2], (REP, SECTIONS, FF, D), 1.0, 6.0, ((0, 32), (1, 4), (2, 2)))
    w_out = bell_draw(splits[3], (REP, SECTIONS, FF, D), 1.0, 6.0, ((0, 32), (1, 4), (2, 2)))
    mixing = draw_mixing(jax.random.fold_in(splits[5], 71), 0)
    return dict(inputs=inputs, loss_grad=loss_grad, w_in=w_in, w_out=w_out, mixing=mixing)


step_size = 4.0
root_half = 0.7071067811865476
inv_root_two_pi = 0.3989422804014327


def gelu_parts(preact):
    normal_cdf = 0.5 * (1.0 + lax.erf(preact * root_half))
    density = jnp.exp(-0.5 * preact * preact) * inv_root_two_pi
    return preact * normal_cdf, normal_cdf + preact * density


def layer_back(operands):
    x_rows, dy_rows, weight_in, weight_out = operands
    in_scale = D ** -0.5
    out_scale = FF ** -0.5
    preact = jnp.dot(x_rows, weight_in.T, preferred_element_type=jnp.float32) * in_scale
    values, slopes = gelu_parts(preact)
    backward = jnp.dot(dy_rows, weight_out.T, preferred_element_type=jnp.float32) * out_scale
    delta_rows = (slopes * backward).astype(jnp.bfloat16)
    groups = delta_rows.reshape(TOK_DEV, N_TP, WIN_DEV).astype(jnp.float32)
    slab_rows = weight_in.reshape(N_TP, WIN_DEV, D).astype(jnp.float32)
    partial_value = (jnp.einsum("mtw,twd->tmd", groups, slab_rows) * in_scale).astype(jnp.bfloat16)
    branch = jnp.sum(partial_value.astype(jnp.float32), axis=0)
    result = (dy_rows.astype(jnp.float32) + branch).astype(jnp.bfloat16)
    grad_in = jnp.dot(delta_rows.T, x_rows, preferred_element_type=jnp.float32) * in_scale
    grad_out = jnp.dot(values.astype(jnp.bfloat16).T, dy_rows, preferred_element_type=jnp.float32) * out_scale
    return result, grad_in, grad_out


def mix_slabs(matrix, slabs):
    mixed = jnp.einsum("rq,qhd->rhd", matrix, slabs.astype(jnp.float32), precision=lax.Precision.HIGHEST)
    return mixed.astype(jnp.bfloat16)


def reference(inputs, loss_grad, w_in, w_out, mixing):
    x_all = inputs.reshape(N_SECTION, N_REP, TOK_DEV, D)
    carried = loss_grad.reshape(N_REP, TOK_DEV, D)
    results = []
    new_ins = []
    new_outs = []
    for segment_pos in range(N_SECTION - 1, -1, -1):
        result, grad_in, grad_out = lax.map(layer_back, (x_all[segment_pos], carried, w_in[:, segment_pos], w_out[:, segment_pos]))
        updated_in = (w_in[:, segment_pos].astype(jnp.float32) - step_size * grad_in).astype(jnp.bfloat16)
        updated_out = (w_out[:, segment_pos].astype(jnp.float32) - step_size * grad_out).astype(jnp.bfloat16)
        new_ins.append(mix_slabs(mixing, updated_in))
        new_outs.append(mix_slabs(mixing, updated_out))
        results.append(result.reshape(TOKENS, D))
        carried = result
    results = results[::-1]
    new_ins = new_ins[::-1]
    new_outs = new_outs[::-1]
    return jnp.stack(results, axis=0), jnp.stack(new_ins, axis=1), jnp.stack(new_outs, axis=1)
```

```python
import jax
import jax.numpy as jnp
from jax import lax
from jax.experimental import pallas as pl
from jax.experimental.pallas import tpu as pltpu
from jax.sharding import PartitionSpec as P

D = 768
FF = 3072
BF = jnp.bfloat16
F32 = jnp.float32

step_size = 4.0
root_half = 0.7071067811865476
inv_root_two_pi = 0.3989422804014327
in_scale = D ** (-0.5)
out_scale = FF ** (-0.5)

CHUNKS = 2
BLOCK = 512
MIB = 1024 * 1024
VMEM = pl.BlockSpec(memory_space=pltpu.VMEM)
HBM = pl.BlockSpec(memory_space=pltpu.HBM)
ANY = pl.BlockSpec(memory_space=pl.ANY)


def params(mib=20):
    return pltpu.CompilerParams(vmem_limit_bytes=mib * MIB)


def cost(flops, nbytes, trans=0):
    return pl.CostEstimate(flops=flops, bytes_accessed=nbytes, transcendentals=trans)


def nt(left, right):
    return lax.dot_general(left, right, (((1,), (1,)), ((), ())), preferred_element_type=F32)


def nn(left, right):
    return lax.dot_general(left, right, (((1,), (0,)), ((), ())), preferred_element_type=F32)


def gelu_parts(preact):
    normal_cdf = 0.5 * (1.0 + lax.erf(preact * root_half))
    density = jnp.exp(-0.5 * preact * preact) * inv_root_two_pi
    return preact * normal_cdf, normal_cdf + preact * density


def blocks(h):
    return [pl.ds(i * BLOCK, BLOCK) for i in range(h // BLOCK)]


def token_slopes_kernel(x_ref, w_ref, s_ref):
    x = x_ref[...]
    for at in blocks(w_ref.shape[0]):
        s_ref[at, :] = gelu_parts(nt(w_ref[at, :], x) * in_scale)[1]


def token_slopes(x_rows, weight_in):
    m, h = x_rows.shape[0], weight_in.shape[0]
    return pl.pallas_call(
        token_slopes_kernel,
        out_shape=jax.ShapeDtypeStruct((h, m), F32),
        in_specs=[VMEM, VMEM],
        out_specs=VMEM,
        compiler_params=params(),
        cost_estimate=cost(2 * m * h * D, 2 * h * D + 4 * m * h, 2 * m * h),
        name="token_slopes",
    )(x_rows, weight_in)


def unit_parts_kernel(w_ref, x_ref, a_ref, s_ref):
    x = x_ref[...]
    for at in blocks(w_ref.shape[0]):
        values, slopes = gelu_parts(nt(w_ref[at, :], x) * in_scale)
        a_ref[at, :] = values.astype(BF)
        s_ref[at, :] = slopes


def unit_parts(weight_in, x_rows):
    m, h = x_rows.shape[0], weight_in.shape[0]
    return pl.pallas_call(
        unit_parts_kernel,
        out_shape=[jax.ShapeDtypeStruct((h, m), BF), jax.ShapeDtypeStruct((h, m), F32)],
        in_specs=[VMEM, VMEM],
        out_specs=[VMEM, VMEM],
        compiler_params=params(),
        cost_estimate=cost(2 * m * h * D, 2 * h * D + 6 * m * h, 2 * m * h),
        name="unit_parts",
    )(weight_in, x_rows)


def turn_kernel(row0, c_ref, wo0_ref, wo1_ref, wi0_ref, wi1_ref, s0_ref, s1_ref, after_ref, o_ref):
    m = c_ref.shape[0]
    cot_t = jnp.transpose(c_ref[...])
    total = c_ref[...].astype(F32)
    branch = None
    for wo_ref, wi_ref, s_ref in ((wo0_ref, wi0_ref, s0_ref), (wo1_ref, wi1_ref, s1_ref)):
        acc = None
        for at in blocks(wo_ref.shape[0]):
            backward = nn(wo_ref[at, :], cot_t) * out_scale
            delta = jnp.transpose(s_ref[at, pl.ds(row0, m)] * backward).astype(BF)
            part = nn(delta, wi_ref[at, :])
            acc = part if acc is None else acc + part
        partial = (acc * in_scale).astype(BF).astype(F32)
        branch = partial if branch is None else branch + partial
    o_ref[...] = (total + branch).astype(BF)


def turn(cot, wouts, wins, slopes, row0, after):
    m = cot.shape[0]
    h = wouts[0].shape[0]
    return pl.pallas_call(
        lambda *refs: turn_kernel(row0, *refs),
        out_shape=jax.ShapeDtypeStruct((m, D), BF),
        in_specs=[VMEM] * 7 + [ANY],
        out_specs=VMEM,
        compiler_params=params(),
        cost_estimate=cost(8 * m * h * D, 8 * h * D + 8 * m * h),
        name="turn",
    )(cot, wouts[0], wouts[1], wins[0], wins[1], slopes[0], slopes[1], after)


def copies_out(scratch, o_ref, sems, i):
    at = pl.ds(i * BLOCK, BLOCK)
    return pltpu.make_async_copy(scratch.at[at, :], o_ref.at[at, :], sems.at[i])


def update_out_kernel(a_ref, c_ref, w_ref, o_ref, scratch, sems):
    cot = c_ref[...]
    parts = blocks(a_ref.shape[0])
    for i, at in enumerate(parts):
        grad = nn(a_ref[at, :], cot) * out_scale
        scratch[at, :] = (w_ref[at, :].astype(F32) - step_size * grad).astype(BF)
        copies_out(scratch, o_ref, sems, i).start()
    for i in range(len(parts)):
        copies_out(scratch, o_ref, sems, i).wait()


def update_out(act_t, cot, weight_out):
    h, m = act_t.shape
    return pl.pallas_call(
        update_out_kernel,
        out_shape=pltpu.HBM((h, D), BF),
        in_specs=[VMEM] * 3,
        out_specs=HBM,
        scratch_shapes=[pltpu.VMEM((h, D), BF), pltpu.SemaphoreType.DMA((h // BLOCK,))],
        compiler_params=params(),
        cost_estimate=cost(2 * m * h * D, 2 * m * h + 4 * h * D),
        name="update_out",
    )(act_t, cot, weight_out)


def update_in_kernel(s_ref, c_ref, x_ref, wo_ref, wi_ref, after_ref, o_ref, scratch, sems):
    cot, x = c_ref[...], x_ref[...]
    parts = blocks(s_ref.shape[0])
    for i, at in enumerate(parts):
        backward = nt(wo_ref[at, :], cot) * out_scale
        delta = (s_ref[at, :] * backward).astype(BF)
        grad = nn(delta, x) * in_scale
        scratch[at, :] = (wi_ref[at, :].astype(F32) - step_size * grad).astype(BF)
        copies_out(scratch, o_ref, sems, i).start()
    for i in range(len(parts)):
        copies_out(scratch, o_ref, sems, i).wait()


def update_in(slopes_t, cot, x_rows, weight_out, weight_in, after):
    h, m = slopes_t.shape
    return pl.pallas_call(
        update_in_kernel,
        out_shape=pltpu.HBM((h, D), BF),
        in_specs=[VMEM] * 5 + [ANY],
        out_specs=HBM,
        scratch_shapes=[pltpu.VMEM((h, D), BF), pltpu.SemaphoreType.DMA((h // BLOCK,))],
        compiler_params=params(),
        cost_estimate=cost(4 * m * h * D, 4 * m * h + 6 * h * D),
        name="update_in",
    )(slopes_t, cot, x_rows, weight_out, weight_in, after)


def mix_kernel(hi_ref, lo_ref, u_ref, o_ref):
    replicas, rows, width = u_ref.shape
    u = u_ref[...].reshape(replicas * rows, width)
    mixed = nn(hi_ref[...], u) + nn(lo_ref[...], u)
    o_ref[...] = mixed.astype(BF).reshape(replicas, rows, width)


def mix(hi, lo, pieces):
    replicas, rows, width = pieces.shape
    block = 16
    n = hi.shape[0]
    matrix = pl.BlockSpec((n, n), lambda i: (0, 0))
    piece = pl.BlockSpec((replicas, block, width), lambda i: (0, i, 0))
    return pl.pallas_call(
        mix_kernel,
        grid=(rows // block,),
        out_shape=pltpu.HBM(pieces.shape, BF),
        in_specs=[matrix, matrix, piece],
        out_specs=piece,
        compiler_params=params(),
        cost_estimate=cost(4 * n * n * width * rows // block, 4 * pieces.size + 4 * n * n),
        name="mix",
    )(hi, lo, pieces)


def spread_kernel(m_ref, hi_ref, lo_ref):
    n, replicas = hi_ref.shape[0], m_ref.shape[0]
    narrow = n // replicas

    def chosen(shape, along):
        group = lax.broadcasted_iota(jnp.int32, shape, along) // narrow
        return jnp.where(lax.broadcasted_iota(jnp.int32, shape, 1 - along) == group, 1.0, 0.0).astype(BF)

    rows, columns = chosen((n, replicas), 0), chosen((replicas, n), 1)
    same = lax.broadcasted_iota(jnp.int32, (n, n), 0) % narrow == lax.broadcasted_iota(jnp.int32, (n, n), 1) % narrow
    left = m_ref[...]
    for ref in (hi_ref, lo_ref):
        part = left.astype(BF)
        left = left - part.astype(F32)
        ref[...] = jnp.where(same, nn(nn(rows, part).astype(BF), columns), 0.0).astype(BF)


def spread_matrix(matrix):
    n = 16 * matrix.shape[0]
    return pl.pallas_call(
        spread_kernel,
        out_shape=[jax.ShapeDtypeStruct((n, n), BF)] * 2,
        in_specs=[VMEM],
        out_specs=[VMEM, VMEM],
        compiler_params=params(),
        cost_estimate=cost(2 * n * n * matrix.shape[0], 4 * n * n),
        name="spread",
    )(matrix)


def landed_kernel(u_ref, o_ref):
    o_ref[...] = u_ref[...]


def landed(array):
    h = array.shape[0]
    rows = pl.BlockSpec((h // 4, D), lambda i: (i, 0))
    return pl.pallas_call(
        landed_kernel,
        grid=(4,),
        out_shape=pltpu.HBM(array.shape, BF),
        in_specs=[rows],
        out_specs=rows,
        compiler_params=params(),
        cost_estimate=cost(0, 4 * h * D),
        name="landed",
    )(array)


def passed_along(shard):
    length = lax.axis_size("section")
    return lax.ppermute(shard, "section", [(i, i - 1) for i in range(1, length)])


def other_core(shard):
    return lax.ppermute(shard, "tp", [(0, 1), (1, 0)])


def sent_out(block):
    return lax.all_to_all(block, "rep", split_axis=0, concat_axis=0, tiled=True)


def shards(inputs, loss_grad, w_in, w_out, mixing):
    segments = lax.axis_size("section")
    segment_index = lax.axis_index("section")
    core = lax.axis_index("tp")
    replicas = lax.axis_size("rep")
    weight_in = w_in[0, 0]
    weight_out = w_out[0, 0]
    units = weight_in.shape[0]
    tokens = loss_grad.shape[0]
    own = tokens // 2

    other_in = other_core(weight_in)
    other_out = other_core(weight_out)
    x_rows = lax.all_gather(inputs[0], "tp", axis=1, tiled=True)
    x_own = lax.dynamic_slice_in_dim(x_rows, core * own, own, 0)
    cot = lax.dynamic_slice_in_dim(lax.all_gather(loss_grad, "tp", axis=1, tiled=True), core * own, own, 0)
    cot = jnp.where(segment_index == segments - 1, cot, jnp.zeros_like(cot))
    slopes = (token_slopes(x_own, weight_in), token_slopes(x_own, other_in))
    wouts, wins = (weight_out, other_out), (weight_in, other_in)

    act_t, slopes_t = unit_parts(weight_in, x_rows)
    hi, lo = spread_matrix(mixing)

    rows = own // CHUNKS
    cots = [cot[c * rows:(c + 1) * rows] for c in range(CHUNKS)]
    kept_cot = []
    kept_result = []
    for turn_index in range(segments - 1):
        results = [turn(cots[c], wouts, wins, slopes, c * rows, mixing) for c in range(CHUNKS)]
        kept_cot.append(cots)
        kept_result.append(results)
        cots = [passed_along(r) for r in results]
    kept_cot.append(cots)

    def summed(kept):
        parts = []
        for c in range(CHUNKS):
            total = kept[0][c]
            for t in range(1, segments):
                total = total + kept[t][c]
            parts.append(total)
        return jnp.concatenate(parts, axis=0)

    cot_rows = lax.all_gather(summed(kept_cot), "tp", axis=0, tiled=True)
    updated_out = update_out(act_t, cot_rows, weight_out)
    pieces_out = sent_out(updated_out.reshape(replicas, units // replicas, D))
    updated_in = update_in(slopes_t, cot_rows, x_rows, weight_out, weight_in, updated_out)
    pieces_in = sent_out(updated_in.reshape(replicas, units // replicas, D))
    kept_result.append([turn(cots[c], wouts, wins, slopes, c * rows, updated_in) for c in range(CHUNKS)])
    back_out = sent_out(mix(hi, lo, pieces_out))
    back_in = sent_out(mix(hi, lo, pieces_in))
    mixed_out = landed(back_out.reshape(units, D))[None, None]
    mixed_in = back_in.reshape(1, 1, units, D)

    result = summed(kept_result)
    width = D // 2
    mine = lax.dynamic_slice_in_dim(result, core * width, width, 1)
    theirs = other_core(lax.dynamic_slice_in_dim(result, (1 - core) * width, width, 1))
    dx = jnp.where(core == 0, jnp.concatenate([mine, theirs], axis=0), jnp.concatenate([theirs, mine], axis=0))
    return dx[None], mixed_in, mixed_out


def solution(mesh):
    in_specs = (
        P("section", "rep", "tp"),
        P("rep", "tp"),
        P("rep", "section", "tp", None),
        P("rep", "section", "tp", None),
        P(),
    )
    out_specs = (
        P("section", "rep", "tp"),
        P("rep", "section", "tp", None),
        P("rep", "section", "tp", None),
    )
    return jax.shard_map(shards, mesh=mesh, in_specs=in_specs, out_specs=out_specs, check_vma=False)
```

```python
import jax
import jax.numpy as jnp
from jax import lax
from jax.experimental import pallas as pl
from jax.experimental.pallas import tpu as pltpu
from jax.sharding import PartitionSpec as P

D = 768
FF = 3072
BF = jnp.bfloat16
F32 = jnp.float32

step_size = 4.0
root_half = 0.7071067811865476
inv_root_two_pi = 0.3989422804014327
in_scale = D ** (-0.5)
out_scale = FF ** (-0.5)

CHUNKS = 2
BLOCK = 512
MIB = 1024 * 1024
VMEM = pl.BlockSpec(memory_space=pltpu.VMEM)
HBM = pl.BlockSpec(memory_space=pltpu.HBM)
ANY = pl.BlockSpec(memory_space=pl.ANY)
SMEM = pl.BlockSpec(memory_space=pltpu.SMEM)


def params(mib=20):
    return pltpu.CompilerParams(vmem_limit_bytes=mib * MIB)


def cost(flops, nbytes, trans=0):
    return pl.CostEstimate(flops=flops, bytes_accessed=nbytes, transcendentals=trans)


def nt(left, right):
    return lax.dot_general(left, right, (((1,), (1,)), ((), ())), preferred_element_type=F32)


def nn(left, right):
    return lax.dot_general(left, right, (((1,), (0,)), ((), ())), preferred_element_type=F32)


def gelu_parts(preact):
    normal_cdf = 0.5 * (1.0 + lax.erf(preact * root_half))
    density = jnp.exp(-0.5 * preact * preact) * inv_root_two_pi
    return preact * normal_cdf, normal_cdf + preact * density


def blocks(h):
    return [pl.ds(i * BLOCK, BLOCK) for i in range(h // BLOCK)]


def joined(core, mine, theirs):
    return jnp.where(core == 0, jnp.concatenate([mine, theirs], axis=1), jnp.concatenate([theirs, mine], axis=1))


def entering_kernel(at, x_ref, other_x_ref, dy_ref, other_dy_ref, whole_ref, own_ref, *outs):
    core = at[0]
    own, m = own_ref.shape[0], outs[0].shape[1]
    whole_ref[...] = joined(core, x_ref[...], other_x_ref[...])
    start = pl.multiple_of(core * own, own)
    own_ref[...] = whole_ref[pl.ds(start, own), :]
    dy = joined(core, dy_ref[pl.ds(start, own), :], other_dy_ref[...])
    dy = jnp.transpose(jnp.where(at[1] == 1, dy, jnp.zeros_like(dy)))
    for c, o_ref in enumerate(outs):
        o_ref[...] = dy[:, c * m : (c + 1) * m]


def entering(at, x, other_x, dy, other_dy):
    own = dy.shape[0] // 2
    shapes = [(2 * own, D), (own, D)] + [(D, own // CHUNKS)] * CHUNKS
    return pl.pallas_call(
        entering_kernel,
        out_shape=[jax.ShapeDtypeStruct(s, BF) for s in shapes],
        in_specs=[SMEM] + [VMEM] * 4,
        out_specs=[VMEM] * len(shapes),
        compiler_params=params(),
        cost_estimate=cost(0, 16 * own * D),
        name="entering",
    )(at, x, other_x, dy, other_dy)


def token_slopes_kernel(x_ref, w_ref, s_ref, t_ref):
    x = x_ref[...]
    for at in blocks(w_ref.shape[0]):
        weight = w_ref[at, :]
        s_ref[at, :] = gelu_parts(nt(weight, x) * in_scale)[1]
        t_ref[:, at] = jnp.transpose(weight)


def token_slopes(x_rows, weight_in):
    m, h = x_rows.shape[0], weight_in.shape[0]
    return pl.pallas_call(
        token_slopes_kernel,
        out_shape=[jax.ShapeDtypeStruct((h, m), F32), jax.ShapeDtypeStruct((D, h), BF)],
        in_specs=[VMEM, VMEM],
        out_specs=[VMEM, VMEM],
        compiler_params=params(),
        cost_estimate=cost(2 * m * h * D, 4 * h * D + 4 * m * h, 2 * m * h),
        name="token_slopes",
    )(x_rows, weight_in)


def kept_kernel(w_ref, o_ref, sems):
    copy = pltpu.make_async_copy(w_ref, o_ref, sems.at[0])
    copy.start()
    copy.wait()


def kept(array):
    return pl.pallas_call(
        kept_kernel,
        out_shape=pltpu.VMEM(array.shape, BF),
        in_specs=[ANY],
        out_specs=VMEM,
        scratch_shapes=[pltpu.SemaphoreType.DMA((1,))],
        compiler_params=params(),
        cost_estimate=cost(0, 4 * array.size),
        name="kept",
    )(array)


def unit_parts_kernel(w_ref, x_ref, a_ref, s_ref):
    x = x_ref[...]
    for at in blocks(w_ref.shape[0]):
        values, slopes = gelu_parts(nt(w_ref[at, :], x) * in_scale)
        a_ref[at, :] = values.astype(BF)
        s_ref[at, :] = slopes


def unit_parts(weight_in, x_rows):
    m, h = x_rows.shape[0], weight_in.shape[0]
    return pl.pallas_call(
        unit_parts_kernel,
        out_shape=[jax.ShapeDtypeStruct((h, m), BF), jax.ShapeDtypeStruct((h, m), F32)],
        in_specs=[VMEM, VMEM],
        out_specs=[VMEM, VMEM],
        compiler_params=params(),
        cost_estimate=cost(2 * m * h * D, 2 * h * D + 6 * m * h, 2 * m * h),
        name="unit_parts",
    )(weight_in, x_rows)


def turn_kernel(col0, c_ref, wo0_ref, wo1_ref, wt0_ref, wt1_ref, s0_ref, s1_ref, after_ref, o_ref, delta):
    cot = c_ref[...]
    m = cot.shape[1]
    branch = None
    for wo_ref, wt_ref, s_ref in ((wo0_ref, wt0_ref, s0_ref), (wo1_ref, wt1_ref, s1_ref)):
        for at in blocks(wo_ref.shape[0]):
            backward = nn(wo_ref[at, :], cot) * out_scale
            delta[at, :] = (s_ref[at, pl.ds(col0, m)] * backward).astype(BF)
        partial = (nn(wt_ref[...], delta[...]) * in_scale).astype(BF).astype(F32)
        branch = partial if branch is None else branch + partial
    o_ref[...] = (cot.astype(F32) + branch).astype(BF)


def turn(cot, wouts, wins_t, slopes, col0, after):
    m = cot.shape[1]
    h = wouts[0].shape[0]
    return pl.pallas_call(
        lambda *refs: turn_kernel(col0, *refs),
        out_shape=jax.ShapeDtypeStruct((D, m), BF),
        in_specs=[VMEM] * 7 + [ANY],
        out_specs=VMEM,
        scratch_shapes=[pltpu.VMEM((h, m), BF)],
        compiler_params=params(),
        cost_estimate=cost(8 * m * h * D, 8 * h * D + 8 * m * h),
        name="turn",
    )(cot, wouts[0], wouts[1], wins_t[0], wins_t[1], slopes[0], slopes[1], after)


def leaving_kernel(core, mine_ref, theirs_ref, o_ref):
    own = mine_ref.shape[1]
    o_ref[pl.ds(pl.multiple_of(core[0] * own, own), own), :] = jnp.transpose(mine_ref[...])
    o_ref[pl.ds(pl.multiple_of((1 - core[0]) * own, own), own), :] = jnp.transpose(theirs_ref[...])


def leaving(core, mine, theirs):
    width, own = mine.shape
    return pl.pallas_call(
        leaving_kernel,
        out_shape=jax.ShapeDtypeStruct((2 * own, width), BF),
        in_specs=[SMEM, VMEM, VMEM],
        out_specs=VMEM,
        compiler_params=params(),
        cost_estimate=cost(0, 8 * own * width),
        name="leaving",
    )(core, mine, theirs)


def copies_out(scratch, o_ref, sems, i):
    at = pl.ds(i * BLOCK, BLOCK)
    return pltpu.make_async_copy(scratch.at[at, :], o_ref.at[at, :], sems.at[i])


def update_out_kernel(a_ref, c_ref, w_ref, o_ref, scratch, sems):
    cot = jnp.transpose(c_ref[...])
    parts = blocks(a_ref.shape[0])
    for i, at in enumerate(parts):
        grad = nn(a_ref[at, :], cot) * out_scale
        scratch[at, :] = (w_ref[at, :].astype(F32) - step_size * grad).astype(BF)
        copies_out(scratch, o_ref, sems, i).start()
    for i in range(len(parts)):
        copies_out(scratch, o_ref, sems, i).wait()


def update_out(act_t, cot, weight_out):
    h, m = act_t.shape
    return pl.pallas_call(
        update_out_kernel,
        out_shape=pltpu.HBM((h, D), BF),
        in_specs=[VMEM] * 3,
        out_specs=HBM,
        scratch_shapes=[pltpu.VMEM((h, D), BF), pltpu.SemaphoreType.DMA((h // BLOCK,))],
        compiler_params=params(),
        cost_estimate=cost(2 * m * h * D, 2 * m * h + 4 * h * D),
        name="update_out",
    )(act_t, cot, weight_out)


def update_in_kernel(s_ref, c_ref, x_ref, wo_ref, wi_ref, o_ref, scratch, sems):
    cot, x = c_ref[...], x_ref[...]
    parts = blocks(s_ref.shape[0])
    for i, at in enumerate(parts):
        backward = nn(wo_ref[at, :], cot) * out_scale
        delta = (s_ref[at, :] * backward).astype(BF)
        grad = nn(delta, x) * in_scale
        scratch[at, :] = (wi_ref[at, :].astype(F32) - step_size * grad).astype(BF)
        copies_out(scratch, o_ref, sems, i).start()
    for i in range(len(parts)):
        copies_out(scratch, o_ref, sems, i).wait()


def update_in(slopes_t, cot, x_rows, weight_out, weight_in):
    h, m = slopes_t.shape
    return pl.pallas_call(
        update_in_kernel,
        out_shape=pltpu.HBM((h, D), BF),
        in_specs=[VMEM] * 5,
        out_specs=HBM,
        scratch_shapes=[pltpu.VMEM((h, D), BF), pltpu.SemaphoreType.DMA((h // BLOCK,))],
        compiler_params=params(),
        cost_estimate=cost(4 * m * h * D, 4 * m * h + 6 * h * D),
        name="update_in",
    )(slopes_t, cot, x_rows, weight_out, weight_in)


def mix_kernel(hi_ref, lo_ref, u_ref, after_ref, o_ref):
    replicas, rows, width = u_ref.shape
    u = u_ref[...].reshape(replicas * rows, width)
    mixed = nn(hi_ref[...], u) + nn(lo_ref[...], u)
    o_ref[...] = mixed.astype(BF).reshape(replicas, rows, width)


def mix(hi, lo, pieces, after):
    replicas, rows, width = pieces.shape
    block = 16
    n = hi.shape[0]
    matrix = pl.BlockSpec((n, n), lambda i: (0, 0))
    piece = pl.BlockSpec((replicas, block, width), lambda i: (0, i, 0))
    return pl.pallas_call(
        mix_kernel,
        grid=(rows // block,),
        out_shape=pltpu.HBM(pieces.shape, BF),
        in_specs=[matrix, matrix, piece, ANY],
        out_specs=piece,
        compiler_params=params(),
        cost_estimate=cost(4 * n * n * width * rows // block, 4 * pieces.size + 4 * n * n),
        name="mix",
    )(hi, lo, pieces, after)


def spread_kernel(m_ref, hi_ref, lo_ref):
    n, replicas = hi_ref.shape[0], m_ref.shape[0]
    narrow = n // replicas

    def chosen(shape, along):
        group = lax.broadcasted_iota(jnp.int32, shape, along) // narrow
        return jnp.where(lax.broadcasted_iota(jnp.int32, shape, 1 - along) == group, 1.0, 0.0).astype(BF)

    rows, columns = chosen((n, replicas), 0), chosen((replicas, n), 1)
    same = lax.broadcasted_iota(jnp.int32, (n, n), 0) % narrow == lax.broadcasted_iota(jnp.int32, (n, n), 1) % narrow
    left = m_ref[...]
    for ref in (hi_ref, lo_ref):
        part = left.astype(BF)
        left = left - part.astype(F32)
        ref[...] = jnp.where(same, nn(nn(rows, part).astype(BF), columns), 0.0).astype(BF)


def spread_matrix(matrix):
    n = 16 * matrix.shape[0]
    return pl.pallas_call(
        spread_kernel,
        out_shape=[jax.ShapeDtypeStruct((n, n), BF)] * 2,
        in_specs=[VMEM],
        out_specs=[VMEM, VMEM],
        compiler_params=params(),
        cost_estimate=cost(2 * n * n * matrix.shape[0], 4 * n * n),
        name="spread",
    )(matrix)


LANDINGS = 6


def landed_kernel(u_ref, o_ref, held, into, out_of):
    rows = u_ref.shape[0] // LANDINGS
    at = [pl.ds(i * rows, rows) for i in range(LANDINGS)]
    loads = [pltpu.make_async_copy(u_ref.at[at[i], :], held.at[at[i], :], into.at[i]) for i in range(LANDINGS)]
    stores = [pltpu.make_async_copy(held.at[at[i], :], o_ref.at[at[i], :], out_of.at[i]) for i in range(LANDINGS)]
    for load in loads:
        load.start()
    for load, store in zip(loads, stores):
        load.wait()
        store.start()
    for store in stores:
        store.wait()


def landed(array):
    return pl.pallas_call(
        landed_kernel,
        out_shape=pltpu.HBM(array.shape, BF),
        in_specs=[ANY],
        out_specs=HBM,
        scratch_shapes=[
            pltpu.VMEM(array.shape, BF),
            pltpu.SemaphoreType.DMA((LANDINGS,)),
            pltpu.SemaphoreType.DMA((LANDINGS,)),
        ],
        compiler_params=params(),
        cost_estimate=cost(0, 4 * array.size),
        name="landed",
    )(array)


def passed_along(shard):
    length = lax.axis_size("section")
    return lax.ppermute(shard, "section", [(i, i - 1) for i in range(1, length)])


def other_core(shard):
    return lax.ppermute(shard, "tp", [(0, 1), (1, 0)])


def sent_out(block):
    return lax.all_to_all(block, "rep", split_axis=0, concat_axis=0, tiled=True)


def shards(inputs, loss_grad, w_in, w_out, mixing):
    segments = lax.axis_size("section")
    segment_index = lax.axis_index("section")
    core = lax.axis_index("tp")
    replicas = lax.axis_size("rep")
    weight_in = w_in[0, 0]
    weight_out = w_out[0, 0]
    units = weight_in.shape[0]
    tokens = loss_grad.shape[0]
    own = tokens // 2

    core_at = jnp.reshape(core, (1,)).astype(jnp.int32)
    last = (segment_index == segments - 1).astype(jnp.int32)
    other_x = other_core(inputs[0])
    other_dy = other_core(lax.dynamic_slice_in_dim(loss_grad, (1 - core) * own, own, 0))
    other_in = other_core(weight_in)
    other_out = other_core(weight_out)
    at = jnp.stack([core.astype(jnp.int32), last])
    x_rows, x_own, *cots = entering(at, inputs[0], other_x, loss_grad, other_dy)
    own_slopes, own_in_t = token_slopes(x_own, weight_in)
    other_slopes, other_in_t = token_slopes(x_own, other_in)
    slopes, wouts, wins_t = (own_slopes, other_slopes), (weight_out, kept(other_out)), (own_in_t, other_in_t)

    act_t, slopes_t = unit_parts(weight_in, x_rows)
    hi, lo = spread_matrix(mixing)

    columns = own // CHUNKS
    kept_cot = []
    kept_result = []
    for turn_index in range(segments - 1):
        results = [turn(cots[c], wouts, wins_t, slopes, c * columns, mixing) for c in range(CHUNKS)]
        kept_cot.append(cots)
        kept_result.append(results)
        cots = [passed_along(r) for r in results]
    kept_cot.append(cots)

    def summed(kept):
        parts = []
        for c in range(CHUNKS):
            total = kept[0][c]
            for t in range(1, segments):
                total = total + kept[t][c]
            parts.append(total)
        return jnp.concatenate(parts, axis=1)

    cot_t = lax.all_gather(summed(kept_cot), "tp", axis=1, tiled=True)
    updated_in = update_in(slopes_t, cot_t, x_rows, weight_out, weight_in)
    pieces_in = sent_out(updated_in.reshape(replicas, units // replicas, D))
    updated_out = update_out(act_t, cot_t, weight_out)
    pieces_out = sent_out(updated_out.reshape(replicas, units // replicas, D))
    mixture_in = mix(hi, lo, pieces_in, mixing)
    back_in = sent_out(mixture_in)
    back_out = sent_out(mix(hi, lo, pieces_out, mixture_in))
    mixed_in = landed(back_in.reshape(units, D))
    mixed_out = landed(back_out.reshape(units, D))

    kept_result.append([turn(cots[c], wouts, wins_t, slopes, c * columns, mixed_in) for c in range(CHUNKS)])
    result = summed(kept_result)
    width = D // 2
    mine = lax.dynamic_slice_in_dim(result, core * width, width, 0)
    theirs = other_core(lax.dynamic_slice_in_dim(result, (1 - core) * width, width, 0))
    dx = leaving(core_at, mine, theirs)
    return dx[None], mixed_in[None, None], mixed_out[None, None]


def solution(mesh):
    in_specs = (
        P("section", "rep", "tp"),
        P("rep", "tp"),
        P("rep", "section", "tp", None),
        P("rep", "section", "tp", None),
        P(),
    )
    out_specs = (
        P("section", "rep", "tp"),
        P("rep", "section", "tp", None),
        P("rep", "section", "tp", None),
    )
    return jax.shard_map(shards, mesh=mesh, in_specs=in_specs, out_specs=out_specs, check_vma=False)
```

```python
import jax
import jax.numpy as jnp
from jax import lax
from jax.experimental import pallas as pl
from jax.experimental.pallas import tpu as pltpu
from jax.sharding import PartitionSpec as P

D = 768
FF = 3072
BF = jnp.bfloat16
F32 = jnp.float32

step_size = 4.0
root_half = 0.7071067811865476
inv_root_two_pi = 0.3989422804014327
in_scale = D ** (-0.5)
out_scale = FF ** (-0.5)

CHUNKS = 2
BLOCK = 512
MIB = 1024 * 1024
VMEM = pl.BlockSpec(memory_space=pltpu.VMEM)
HBM = pl.BlockSpec(memory_space=pltpu.HBM)
ANY = pl.BlockSpec(memory_space=pl.ANY)
SMEM = pl.BlockSpec(memory_space=pltpu.SMEM)


def params(mib=20):
    return pltpu.CompilerParams(vmem_limit_bytes=mib * MIB)


def cost(flops, nbytes, trans=0):
    return pl.CostEstimate(flops=flops, bytes_accessed=nbytes, transcendentals=trans)


def nt(left, right):
    return lax.dot_general(left, right, (((1,), (1,)), ((), ())), preferred_element_type=F32)


def nn(left, right):
    return lax.dot_general(left, right, (((1,), (0,)), ((), ())), preferred_element_type=F32)


def gelu_parts(preact):
    normal_cdf = 0.5 * (1.0 + lax.erf(preact * root_half))
    density = jnp.exp(-0.5 * preact * preact) * inv_root_two_pi
    return preact * normal_cdf, normal_cdf + preact * density


def blocks(h):
    return [pl.ds(i * BLOCK, BLOCK) for i in range(h // BLOCK)]


def joined(core, mine, theirs):
    return jnp.where(core == 0, jnp.concatenate([mine, theirs], axis=1), jnp.concatenate([theirs, mine], axis=1))


def entering_kernel(at, x_ref, other_x_ref, dy_ref, other_dy_ref, whole_ref, own_ref, cot_ref):
    core = at[0]
    own = own_ref.shape[0]
    whole_ref[...] = joined(core, x_ref[...], other_x_ref[...])
    own_ref[...] = whole_ref[pl.ds(pl.multiple_of(core * own, own), own), :]
    dy = joined(core, dy_ref[...], other_dy_ref[...])
    cot_ref[...] = jnp.transpose(jnp.where(at[1] == 1, dy, jnp.zeros_like(dy)))


def entering(at, x, other_x, dy, other_dy):
    own = dy.shape[0] // 2
    shapes = [(2 * own, D), (own, D), (D, 2 * own)]
    return pl.pallas_call(
        entering_kernel,
        out_shape=[jax.ShapeDtypeStruct(s, BF) for s in shapes],
        in_specs=[SMEM] + [VMEM] * 4,
        out_specs=[VMEM] * len(shapes),
        compiler_params=params(),
        cost_estimate=cost(0, 16 * own * D),
        name="entering",
    )(at, x, other_x, dy, other_dy)


def first_turn_kernel(chunk, m, at, c_ref, wo_ref, wt_ref, s_ref, cot_ref, mine_ref, theirs_ref, delta):
    own = c_ref.shape[1] // 2
    lanes = [pl.ds(pl.multiple_of(side * own + chunk * m, m), m) for side in (at[0], 1 - at[0])]
    cot = jnp.concatenate([c_ref[:, lane] for lane in lanes], axis=1)
    for at_rows in blocks(wo_ref.shape[0]):
        backward = nn(wo_ref[at_rows, :], cot) * out_scale
        slopes = jnp.concatenate([s_ref[at_rows, lane] for lane in lanes], axis=1)
        delta[at_rows, :] = (slopes * backward).astype(BF)
    partial = (nn(wt_ref[...], delta[...]) * in_scale).astype(BF)
    cot_ref[...] = cot[:, :m]
    mine_ref[...] = partial[:, :m]
    theirs_ref[...] = partial[:, m:]


def first_turn(at, chunk, cot, weight_out, weight_in_t, slopes):
    h, tokens = slopes.shape
    m = tokens // 2 // CHUNKS
    return pl.pallas_call(
        lambda *refs: first_turn_kernel(chunk, m, *refs),
        out_shape=[jax.ShapeDtypeStruct((D, m), BF)] * 3,
        in_specs=[SMEM] + [VMEM] * 4,
        out_specs=[VMEM] * 3,
        scratch_shapes=[pltpu.VMEM((h, 2 * m), BF)],
        compiler_params=params(),
        cost_estimate=cost(8 * m * h * D, 4 * h * D + 8 * m * h),
        name="first_turn",
    )(at, cot, weight_out, weight_in_t, slopes)


def both_parts_kernel(c_ref, mine_ref, theirs_ref, o_ref):
    branch = mine_ref[...].astype(F32) + theirs_ref[...].astype(F32)
    o_ref[...] = (c_ref[...].astype(F32) + branch).astype(BF)


def both_parts(cot, mine, theirs):
    return pl.pallas_call(
        both_parts_kernel,
        out_shape=jax.ShapeDtypeStruct(cot.shape, BF),
        in_specs=[VMEM] * 3,
        out_specs=VMEM,
        compiler_params=params(),
        cost_estimate=cost(0, 8 * cot.size),
        name="both_parts",
    )(cot, mine, theirs)


def token_slopes_kernel(x_ref, w_ref, s_ref, t_ref):
    x = x_ref[...]
    for at in blocks(w_ref.shape[0]):
        weight = w_ref[at, :]
        s_ref[at, :] = gelu_parts(nt(weight, x) * in_scale)[1]
        t_ref[:, at] = jnp.transpose(weight)


def token_slopes(x_rows, weight_in):
    m, h = x_rows.shape[0], weight_in.shape[0]
    return pl.pallas_call(
        token_slopes_kernel,
        out_shape=[jax.ShapeDtypeStruct((h, m), F32), jax.ShapeDtypeStruct((D, h), BF)],
        in_specs=[VMEM, VMEM],
        out_specs=[VMEM, VMEM],
        compiler_params=params(),
        cost_estimate=cost(2 * m * h * D, 4 * h * D + 4 * m * h, 2 * m * h),
        name="token_slopes",
    )(x_rows, weight_in)


def kept_kernel(w_ref, o_ref, sems):
    copy = pltpu.make_async_copy(w_ref, o_ref, sems.at[0])
    copy.start()
    copy.wait()


def kept(array):
    return pl.pallas_call(
        kept_kernel,
        out_shape=pltpu.VMEM(array.shape, BF),
        in_specs=[ANY],
        out_specs=VMEM,
        scratch_shapes=[pltpu.SemaphoreType.DMA((1,))],
        compiler_params=params(),
        cost_estimate=cost(0, 4 * array.size),
        name="kept",
    )(array)


def unit_parts_kernel(w_ref, x_ref, a_ref, s_ref, t_ref):
    x = x_ref[...]
    for at in blocks(w_ref.shape[0]):
        weight = w_ref[at, :]
        values, slopes = gelu_parts(nt(weight, x) * in_scale)
        a_ref[at, :] = values.astype(BF)
        s_ref[at, :] = slopes
        t_ref[:, at] = jnp.transpose(weight)


def unit_parts(weight_in, x_rows):
    m, h = x_rows.shape[0], weight_in.shape[0]
    return pl.pallas_call(
        unit_parts_kernel,
        out_shape=[
            jax.ShapeDtypeStruct((h, m), BF),
            jax.ShapeDtypeStruct((h, m), F32),
            jax.ShapeDtypeStruct((D, h), BF),
        ],
        in_specs=[VMEM, VMEM],
        out_specs=[VMEM] * 3,
        compiler_params=params(),
        cost_estimate=cost(2 * m * h * D, 2 * h * D + 6 * m * h, 2 * m * h),
        name="unit_parts",
    )(weight_in, x_rows)


def turn_kernel(col0, at_ref, c_ref, wo0_ref, wo1_ref, wt0_ref, wt1_ref, s0_ref, s1_ref, after_ref, o_ref, delta):
    cot = c_ref[...]
    m = cot.shape[1]
    own = pl.ds(pl.multiple_of(at_ref[0] * s1_ref.shape[1] + col0, m), m)
    branch = None
    for wo_ref, wt_ref, s_ref, lane in (
        (wo0_ref, wt0_ref, s0_ref, own),
        (wo1_ref, wt1_ref, s1_ref, pl.ds(col0, m)),
    ):
        for at in blocks(wo_ref.shape[0]):
            backward = nn(wo_ref[at, :], cot) * out_scale
            delta[at, :] = (s_ref[at, lane] * backward).astype(BF)
        partial = (nn(wt_ref[...], delta[...]) * in_scale).astype(BF).astype(F32)
        branch = partial if branch is None else branch + partial
    o_ref[...] = (cot.astype(F32) + branch).astype(BF)


def turn(at, cot, wouts, wins_t, slopes, col0, after):
    m = cot.shape[1]
    h = wouts[0].shape[0]
    return pl.pallas_call(
        lambda *refs: turn_kernel(col0, *refs),
        out_shape=jax.ShapeDtypeStruct((D, m), BF),
        in_specs=[SMEM] + [VMEM] * 7 + [ANY],
        out_specs=VMEM,
        scratch_shapes=[pltpu.VMEM((h, m), BF)],
        compiler_params=params(),
        cost_estimate=cost(8 * m * h * D, 8 * h * D + 8 * m * h),
        name="turn",
    )(at, cot, wouts[0], wouts[1], wins_t[0], wins_t[1], slopes[0], slopes[1], after)


def leaving_kernel(core, mine_ref, theirs_ref, o_ref):
    own = mine_ref.shape[1]
    o_ref[pl.ds(pl.multiple_of(core[0] * own, own), own), :] = jnp.transpose(mine_ref[...])
    o_ref[pl.ds(pl.multiple_of((1 - core[0]) * own, own), own), :] = jnp.transpose(theirs_ref[...])


def leaving(core, mine, theirs):
    width, own = mine.shape
    return pl.pallas_call(
        leaving_kernel,
        out_shape=jax.ShapeDtypeStruct((2 * own, width), BF),
        in_specs=[SMEM, VMEM, VMEM],
        out_specs=VMEM,
        compiler_params=params(),
        cost_estimate=cost(0, 8 * own * width),
        name="leaving",
    )(core, mine, theirs)


def copies_out(scratch, o_ref, sems, i):
    at = pl.ds(i * BLOCK, BLOCK)
    return pltpu.make_async_copy(scratch.at[at, :], o_ref.at[at, :], sems.at[i])


def update_out_kernel(a_ref, c_ref, w_ref, o_ref, scratch, sems):
    cot = jnp.transpose(c_ref[...])
    parts = blocks(a_ref.shape[0])
    for i, at in enumerate(parts):
        grad = nn(a_ref[at, :], cot) * out_scale
        scratch[at, :] = (w_ref[at, :].astype(F32) - step_size * grad).astype(BF)
        copies_out(scratch, o_ref, sems, i).start()
    for i in range(len(parts)):
        copies_out(scratch, o_ref, sems, i).wait()


def update_out(act_t, cot, weight_out):
    h, m = act_t.shape
    return pl.pallas_call(
        update_out_kernel,
        out_shape=pltpu.HBM((h, D), BF),
        in_specs=[VMEM] * 3,
        out_specs=HBM,
        scratch_shapes=[pltpu.VMEM((h, D), BF), pltpu.SemaphoreType.DMA((h // BLOCK,))],
        compiler_params=params(),
        cost_estimate=cost(2 * m * h * D, 2 * m * h + 4 * h * D),
        name="update_out",
    )(act_t, cot, weight_out)


def update_in_kernel(s_ref, c_ref, x_ref, wo_ref, wi_ref, o_ref, scratch, sems):
    cot, x = c_ref[...], x_ref[...]
    parts = blocks(s_ref.shape[0])
    for i, at in enumerate(parts):
        backward = nn(wo_ref[at, :], cot) * out_scale
        delta = (s_ref[at, :] * backward).astype(BF)
        grad = nn(delta, x) * in_scale
        scratch[at, :] = (wi_ref[at, :].astype(F32) - step_size * grad).astype(BF)
        copies_out(scratch, o_ref, sems, i).start()
    for i in range(len(parts)):
        copies_out(scratch, o_ref, sems, i).wait()


def update_in(slopes_t, cot, x_rows, weight_out, weight_in):
    h, m = slopes_t.shape
    return pl.pallas_call(
        update_in_kernel,
        out_shape=pltpu.HBM((h, D), BF),
        in_specs=[VMEM] * 5,
        out_specs=HBM,
        scratch_shapes=[pltpu.VMEM((h, D), BF), pltpu.SemaphoreType.DMA((h // BLOCK,))],
        compiler_params=params(),
        cost_estimate=cost(4 * m * h * D, 4 * m * h + 6 * h * D),
        name="update_in",
    )(slopes_t, cot, x_rows, weight_out, weight_in)


def mix_kernel(hi_ref, lo_ref, u_ref, after_ref, o_ref):
    replicas, rows, width = u_ref.shape
    u = u_ref[...].reshape(replicas * rows, width)
    mixed = nn(hi_ref[...], u) + nn(lo_ref[...], u)
    o_ref[...] = mixed.astype(BF).reshape(replicas, rows, width)


def mix(hi, lo, pieces, after):
    replicas, rows, width = pieces.shape
    block = 16
    n = hi.shape[0]
    matrix = pl.BlockSpec((n, n), lambda i: (0, 0))
    piece = pl.BlockSpec((replicas, block, width), lambda i: (0, i, 0))
    return pl.pallas_call(
        mix_kernel,
        grid=(rows // block,),
        out_shape=pltpu.HBM(pieces.shape, BF),
        in_specs=[matrix, matrix, piece, ANY],
        out_specs=piece,
        compiler_params=params(),
        cost_estimate=cost(4 * n * n * width * rows // block, 4 * pieces.size + 4 * n * n),
        name="mix",
    )(hi, lo, pieces, after)


def spread_kernel(m_ref, hi_ref, lo_ref):
    n, replicas = hi_ref.shape[0], m_ref.shape[0]
    narrow = n // replicas

    def chosen(shape, along):
        group = lax.broadcasted_iota(jnp.int32, shape, along) // narrow
        return jnp.where(lax.broadcasted_iota(jnp.int32, shape, 1 - along) == group, 1.0, 0.0).astype(BF)

    rows, columns = chosen((n, replicas), 0), chosen((replicas, n), 1)
    same = lax.broadcasted_iota(jnp.int32, (n, n), 0) % narrow == lax.broadcasted_iota(jnp.int32, (n, n), 1) % narrow
    left = m_ref[...]
    for ref in (hi_ref, lo_ref):
        part = left.astype(BF)
        left = left - part.astype(F32)
        ref[...] = jnp.where(same, nn(nn(rows, part).astype(BF), columns), 0.0).astype(BF)


def spread_matrix(matrix):
    n = 16 * matrix.shape[0]
    return pl.pallas_call(
        spread_kernel,
        out_shape=[jax.ShapeDtypeStruct((n, n), BF)] * 2,
        in_specs=[VMEM],
        out_specs=[VMEM, VMEM],
        compiler_params=params(),
        cost_estimate=cost(2 * n * n * matrix.shape[0], 4 * n * n),
        name="spread",
    )(matrix)


LANDINGS = 6


def landed_kernel(u_ref, after_ref, o_ref, held, into, out_of):
    rows = u_ref.shape[0] // LANDINGS
    at = [pl.ds(i * rows, rows) for i in range(LANDINGS)]
    loads = [pltpu.make_async_copy(u_ref.at[at[i], :], held.at[at[i], :], into.at[i]) for i in range(LANDINGS)]
    stores = [pltpu.make_async_copy(held.at[at[i], :], o_ref.at[at[i], :], out_of.at[i]) for i in range(LANDINGS)]
    for load in loads:
        load.start()
    for load, store in zip(loads, stores):
        load.wait()
        store.start()
    for store in stores:
        store.wait()


def landed(array, after):
    return pl.pallas_call(
        landed_kernel,
        out_shape=pltpu.HBM(array.shape, BF),
        in_specs=[ANY, ANY],
        out_specs=HBM,
        scratch_shapes=[
            pltpu.VMEM(array.shape, BF),
            pltpu.SemaphoreType.DMA((LANDINGS,)),
            pltpu.SemaphoreType.DMA((LANDINGS,)),
        ],
        compiler_params=params(),
        cost_estimate=cost(0, 4 * array.size),
        name="landed",
    )(array, after)


def passed_along(shard):
    length = lax.axis_size("section")
    return lax.ppermute(shard, "section", [(i, i - 1) for i in range(1, length)])


def other_core(shard):
    return lax.ppermute(shard, "tp", [(0, 1), (1, 0)])


def sent_out(block):
    return lax.all_to_all(block, "rep", split_axis=0, concat_axis=0, tiled=True)


def shards(inputs, loss_grad, w_in, w_out, mixing):
    segments = lax.axis_size("section")
    segment_index = lax.axis_index("section")
    core = lax.axis_index("tp")
    replicas = lax.axis_size("rep")
    weight_in = w_in[0, 0]
    weight_out = w_out[0, 0]
    units = weight_in.shape[0]
    tokens = loss_grad.shape[0]
    own = tokens // 2

    core_at = jnp.reshape(core, (1,)).astype(jnp.int32)
    last = (segment_index == segments - 1).astype(jnp.int32)
    other_x = other_core(inputs[0])
    other_dy = other_core(loss_grad)
    late_in, late_out, other_x, other_dy = lax.optimization_barrier((weight_in, weight_out, other_x, other_dy))
    other_in = other_core(late_in)
    other_out = other_core(late_out)
    at = jnp.stack([core.astype(jnp.int32), last])
    x_rows, x_own, cot = entering(at, inputs[0], other_x, loss_grad, other_dy)
    act_t, slopes_t, own_in_t = unit_parts(weight_in, x_rows)
    hi, lo = spread_matrix(mixing)

    columns = own // CHUNKS
    halves = [first_turn(at, c, cot, weight_out, own_in_t, slopes_t) for c in range(CHUNKS)]
    kept_cot = [[half[0] for half in halves]]
    kept_result = [[both_parts(half[0], half[1], other_core(half[2])) for half in halves]]
    cots = [passed_along(r) for r in kept_result[0]]

    other_slopes, other_in_t = token_slopes(x_own, other_in)
    slopes, wouts, wins_t = (slopes_t, other_slopes), (weight_out, kept(other_out)), (own_in_t, other_in_t)
    for turn_index in range(1, segments - 1):
        results = [turn(at, cots[c], wouts, wins_t, slopes, c * columns, mixing) for c in range(CHUNKS)]
        kept_cot.append(cots)
        kept_result.append(results)
        cots = [passed_along(r) for r in results]
    kept_cot.append(cots)

    def summed(kept):
        parts = []
        for c in range(CHUNKS):
            total = kept[0][c]
            for t in range(1, segments):
                total = total + kept[t][c]
            parts.append(total)
        return jnp.concatenate(parts, axis=1)

    cot_t = lax.all_gather(summed(kept_cot), "tp", axis=1, tiled=True)
    updated_in = update_in(slopes_t, cot_t, x_rows, weight_out, weight_in)
    pieces_in = sent_out(updated_in.reshape(replicas, units // replicas, D))
    updated_out = update_out(act_t, cot_t, weight_out)
    pieces_out = sent_out(updated_out.reshape(replicas, units // replicas, D))
    mixture_in = mix(hi, lo, pieces_in, mixing)
    back_in = sent_out(mixture_in)
    back_out = sent_out(mix(hi, lo, pieces_out, mixture_in))
    mixed_in = landed(back_in.reshape(units, D), mixing)

    kept_result.append([turn(at, cots[c], wouts, wins_t, slopes, c * columns, mixed_in) for c in range(CHUNKS)])
    result = summed(kept_result)
    width = D // 2
    mine = lax.dynamic_slice_in_dim(result, core * width, width, 0)
    theirs = other_core(lax.dynamic_slice_in_dim(result, (1 - core) * width, width, 0))
    dx = leaving(core_at, mine, theirs)
    mixed_out = landed(back_out.reshape(units, D), dx)
    return dx[None], mixed_in[None, None], mixed_out[None, None]


def solution(mesh):
    in_specs = (
        P("section", "rep", "tp"),
        P("rep", "tp"),
        P("rep", "section", "tp", None),
        P("rep", "section", "tp", None),
        P(),
    )
    out_specs = (
        P("section", "rep", "tp"),
        P("rep", "section", "tp", None),
        P("rep", "section", "tp", None),
    )
    return jax.shard_map(shards, mesh=mesh, in_specs=in_specs, out_specs=out_specs, check_vma=False)
```

```python
import jax
import jax.numpy as jnp
from jax import lax
from jax.experimental import pallas as pl
from jax.experimental.pallas import tpu as pltpu
from jax.sharding import PartitionSpec as P

D = 768
FF = 3072
BF = jnp.bfloat16
F32 = jnp.float32

step_size = 4.0
root_half = 0.7071067811865476
inv_root_two_pi = 0.3989422804014327
in_scale = D ** (-0.5)
out_scale = FF ** (-0.5)

CHUNKS = 2
BLOCK = 512
MIB = 1024 * 1024
VMEM = pl.BlockSpec(memory_space=pltpu.VMEM)
HBM = pl.BlockSpec(memory_space=pltpu.HBM)
ANY = pl.BlockSpec(memory_space=pl.ANY)
SMEM = pl.BlockSpec(memory_space=pltpu.SMEM)


def params(mib=20):
    return pltpu.CompilerParams(vmem_limit_bytes=mib * MIB)


def cost(flops, nbytes, trans=0):
    return pl.CostEstimate(flops=flops, bytes_accessed=nbytes, transcendentals=trans)


def nt(left, right):
    return lax.dot_general(left, right, (((1,), (1,)), ((), ())), preferred_element_type=F32)


def nn(left, right):
    return lax.dot_general(left, right, (((1,), (0,)), ((), ())), preferred_element_type=F32)


def gelu_parts(preact):
    normal_cdf = 0.5 * (1.0 + lax.erf(preact * root_half))
    density = jnp.exp(-0.5 * preact * preact) * inv_root_two_pi
    return preact * normal_cdf, normal_cdf + preact * density


def blocks(h):
    return [pl.ds(i * BLOCK, BLOCK) for i in range(h // BLOCK)]


def joined(core, mine, theirs):
    return jnp.where(core == 0, jnp.concatenate([mine, theirs], axis=1), jnp.concatenate([theirs, mine], axis=1))


def entering_kernel(at, x_ref, other_x_ref, dy_ref, other_dy_ref, whole_ref, own_ref, cot_ref):
    core = at[0]
    own = own_ref.shape[0]
    whole_ref[...] = joined(core, x_ref[...], other_x_ref[...])
    own_ref[...] = whole_ref[pl.ds(pl.multiple_of(core * own, own), own), :]
    dy = joined(core, dy_ref[...], other_dy_ref[...])
    cot_ref[...] = jnp.transpose(jnp.where(at[1] == 1, dy, jnp.zeros_like(dy)))


def entering(at, x, other_x, dy, other_dy):
    own = dy.shape[0] // 2
    shapes = [(2 * own, D), (own, D), (D, 2 * own)]
    return pl.pallas_call(
        entering_kernel,
        out_shape=[jax.ShapeDtypeStruct(s, BF) for s in shapes],
        in_specs=[SMEM] + [VMEM] * 4,
        out_specs=[VMEM] * len(shapes),
        compiler_params=params(),
        cost_estimate=cost(0, 16 * own * D),
        name="entering",
    )(at, x, other_x, dy, other_dy)


def first_turn_kernel(chunk, m, at, c_ref, wo_ref, wt_ref, s_ref, cot_ref, mine_ref, theirs_ref, delta):
    own = c_ref.shape[1] // 2
    lanes = [pl.ds(pl.multiple_of(side * own + chunk * m, m), m) for side in (at[0], 1 - at[0])]
    cot = jnp.concatenate([c_ref[:, lane] for lane in lanes], axis=1)
    for at_rows in blocks(wo_ref.shape[0]):
        backward = nn(wo_ref[at_rows, :], cot) * out_scale
        slopes = jnp.concatenate([s_ref[at_rows, lane] for lane in lanes], axis=1)
        delta[at_rows, :] = (slopes * backward).astype(BF)
    partial = (nn(wt_ref[...], delta[...]) * in_scale).astype(BF)
    cot_ref[...] = cot[:, :m]
    mine_ref[...] = partial[:, :m]
    theirs_ref[...] = partial[:, m:]


def first_turn(at, chunk, cot, weight_out, weight_in_t, slopes):
    h, tokens = slopes.shape
    m = tokens // 2 // CHUNKS
    return pl.pallas_call(
        lambda *refs: first_turn_kernel(chunk, m, *refs),
        out_shape=[jax.ShapeDtypeStruct((D, m), BF)] * 3,
        in_specs=[SMEM] + [VMEM] * 4,
        out_specs=[VMEM] * 3,
        scratch_shapes=[pltpu.VMEM((h, 2 * m), BF)],
        compiler_params=params(),
        cost_estimate=cost(8 * m * h * D, 4 * h * D + 8 * m * h),
        name="first_turn",
    )(at, cot, weight_out, weight_in_t, slopes)


def both_parts_kernel(c_ref, mine_ref, theirs_ref, o_ref):
    branch = mine_ref[...].astype(F32) + theirs_ref[...].astype(F32)
    o_ref[...] = (c_ref[...].astype(F32) + branch).astype(BF)


def both_parts(cot, mine, theirs):
    return pl.pallas_call(
        both_parts_kernel,
        out_shape=jax.ShapeDtypeStruct(cot.shape, BF),
        in_specs=[VMEM] * 3,
        out_specs=VMEM,
        compiler_params=params(),
        cost_estimate=cost(0, 8 * cot.size),
        name="both_parts",
    )(cot, mine, theirs)


def token_slopes_kernel(x_ref, w_ref, s_ref, t_ref):
    x = x_ref[...]
    for at in blocks(w_ref.shape[0]):
        weight = w_ref[at, :]
        s_ref[at, :] = gelu_parts(nt(weight, x) * in_scale)[1]
        t_ref[:, at] = jnp.transpose(weight)


def token_slopes(x_rows, weight_in):
    m, h = x_rows.shape[0], weight_in.shape[0]
    return pl.pallas_call(
        token_slopes_kernel,
        out_shape=[jax.ShapeDtypeStruct((h, m), F32), jax.ShapeDtypeStruct((D, h), BF)],
        in_specs=[VMEM, VMEM],
        out_specs=[VMEM, VMEM],
        compiler_params=params(),
        cost_estimate=cost(2 * m * h * D, 4 * h * D + 4 * m * h, 2 * m * h),
        name="token_slopes",
    )(x_rows, weight_in)


def kept_kernel(*refs):
    count = len(refs) // 2
    sems = refs[-1]
    copies = [pltpu.make_async_copy(refs[i], refs[count + i], sems.at[i]) for i in range(count)]
    for copy in copies:
        copy.start()
    for copy in copies:
        copy.wait()


def kept(*arrays, mib=20):
    return pl.pallas_call(
        kept_kernel,
        out_shape=[pltpu.VMEM(array.shape, BF) for array in arrays],
        in_specs=[ANY] * len(arrays),
        out_specs=[VMEM] * len(arrays),
        scratch_shapes=[pltpu.SemaphoreType.DMA((len(arrays),))],
        compiler_params=params(mib),
        cost_estimate=cost(0, 4 * sum(array.size for array in arrays)),
        name="kept",
    )(*arrays)


def unit_parts_kernel(core, w_ref, x_ref, a_ref, s_ref, t_ref, own_ref):
    own = own_ref.shape[1]
    x = x_ref[...]
    for at in blocks(w_ref.shape[0]):
        weight = w_ref[at, :]
        values, slopes = gelu_parts(nt(weight, x) * in_scale)
        a_ref[at, :] = values.astype(BF)
        s_ref[at, :] = slopes
        own_ref[at, :] = jnp.where(core[0] == 0, slopes[:, :own], slopes[:, own:])
        t_ref[:, at] = jnp.transpose(weight)


def unit_parts(core, weight_in, x_rows):
    m, h = x_rows.shape[0], weight_in.shape[0]
    return pl.pallas_call(
        unit_parts_kernel,
        out_shape=[
            jax.ShapeDtypeStruct((h, m), BF),
            jax.ShapeDtypeStruct((h, m), F32),
            jax.ShapeDtypeStruct((D, h), BF),
            jax.ShapeDtypeStruct((h, m // 2), F32),
        ],
        in_specs=[SMEM, VMEM, VMEM],
        out_specs=[VMEM] * 4,
        compiler_params=params(),
        cost_estimate=cost(2 * m * h * D, 2 * h * D + 6 * m * h, 2 * m * h),
        name="unit_parts",
    )(core, weight_in, x_rows)


def turn_kernel(col0, c_ref, wo0_ref, wo1_ref, wt0_ref, wt1_ref, s0_ref, s1_ref, after_ref, o_ref, delta):
    cot = c_ref[...]
    m = cot.shape[1]
    branch = None
    for wo_ref, wt_ref, s_ref in ((wo0_ref, wt0_ref, s0_ref), (wo1_ref, wt1_ref, s1_ref)):
        for at in blocks(wo_ref.shape[0]):
            backward = nn(wo_ref[at, :], cot) * out_scale
            delta[at, :] = (s_ref[at, pl.ds(col0, m)] * backward).astype(BF)
        partial = (nn(wt_ref[...], delta[...]) * in_scale).astype(BF).astype(F32)
        branch = partial if branch is None else branch + partial
    o_ref[...] = (cot.astype(F32) + branch).astype(BF)


def turn(cot, wouts, wins_t, slopes, col0, after):
    m = cot.shape[1]
    h = wouts[0].shape[0]
    return pl.pallas_call(
        lambda *refs: turn_kernel(col0, *refs),
        out_shape=jax.ShapeDtypeStruct((D, m), BF),
        in_specs=[VMEM] * 7 + [ANY],
        out_specs=VMEM,
        scratch_shapes=[pltpu.VMEM((h, m), BF)],
        compiler_params=params(),
        cost_estimate=cost(8 * m * h * D, 8 * h * D + 8 * m * h),
        name="turn",
    )(cot, wouts[0], wouts[1], wins_t[0], wins_t[1], slopes[0], slopes[1], after)


def leaving_kernel(core, mine_ref, theirs_ref, o_ref):
    own = mine_ref.shape[1]
    o_ref[pl.ds(pl.multiple_of(core[0] * own, own), own), :] = jnp.transpose(mine_ref[...])
    o_ref[pl.ds(pl.multiple_of((1 - core[0]) * own, own), own), :] = jnp.transpose(theirs_ref[...])


def leaving(core, mine, theirs):
    width, own = mine.shape
    return pl.pallas_call(
        leaving_kernel,
        out_shape=jax.ShapeDtypeStruct((2 * own, width), BF),
        in_specs=[SMEM, VMEM, VMEM],
        out_specs=VMEM,
        compiler_params=params(),
        cost_estimate=cost(0, 8 * own * width),
        name="leaving",
    )(core, mine, theirs)


def copies_out(scratch, o_ref, sems, i):
    at = pl.ds(i * BLOCK, BLOCK)
    return pltpu.make_async_copy(scratch.at[at, :], o_ref.at[at, :], sems.at[i])


def update_out_kernel(a_ref, c_ref, w_ref, o_ref, scratch, sems):
    cot = jnp.transpose(c_ref[...])
    parts = blocks(a_ref.shape[0])
    for i, at in enumerate(parts):
        grad = nn(a_ref[at, :], cot) * out_scale
        scratch[at, :] = (w_ref[at, :].astype(F32) - step_size * grad).astype(BF)
        copies_out(scratch, o_ref, sems, i).start()
    for i in range(len(parts)):
        copies_out(scratch, o_ref, sems, i).wait()


def update_out(act_t, cot, weight_out):
    h, m = act_t.shape
    return pl.pallas_call(
        update_out_kernel,
        out_shape=pltpu.HBM((h, D), BF),
        in_specs=[VMEM] * 3,
        out_specs=HBM,
        scratch_shapes=[pltpu.VMEM((h, D), BF), pltpu.SemaphoreType.DMA((h // BLOCK,))],
        compiler_params=params(),
        cost_estimate=cost(2 * m * h * D, 2 * m * h + 4 * h * D),
        name="update_out",
    )(act_t, cot, weight_out)


def update_in_kernel(s_ref, c_ref, x_ref, wo_ref, wi_ref, o_ref, scratch, sems):
    cot, x = c_ref[...], x_ref[...]
    parts = blocks(s_ref.shape[0])
    for i, at in enumerate(parts):
        backward = nn(wo_ref[at, :], cot) * out_scale
        delta = (s_ref[at, :] * backward).astype(BF)
        grad = nn(delta, x) * in_scale
        scratch[at, :] = (wi_ref[at, :].astype(F32) - step_size * grad).astype(BF)
        copies_out(scratch, o_ref, sems, i).start()
    for i in range(len(parts)):
        copies_out(scratch, o_ref, sems, i).wait()


def update_in(slopes_t, cot, x_rows, weight_out, weight_in):
    h, m = slopes_t.shape
    return pl.pallas_call(
        update_in_kernel,
        out_shape=pltpu.HBM((h, D), BF),
        in_specs=[VMEM] * 5,
        out_specs=HBM,
        scratch_shapes=[pltpu.VMEM((h, D), BF), pltpu.SemaphoreType.DMA((h // BLOCK,))],
        compiler_params=params(),
        cost_estimate=cost(4 * m * h * D, 4 * m * h + 6 * h * D),
        name="update_in",
    )(slopes_t, cot, x_rows, weight_out, weight_in)


def mix_kernel(hi_ref, lo_ref, u_ref, after_ref, o_ref):
    replicas, rows, width = u_ref.shape
    u = u_ref[...].reshape(replicas * rows, width)
    mixed = nn(hi_ref[...], u) + nn(lo_ref[...], u)
    o_ref[...] = mixed.astype(BF).reshape(replicas, rows, width)


def mix(hi, lo, pieces, after):
    replicas, rows, width = pieces.shape
    block = 16
    n = hi.shape[0]
    matrix = pl.BlockSpec((n, n), lambda i: (0, 0))
    piece = pl.BlockSpec((replicas, block, width), lambda i: (0, i, 0))
    return pl.pallas_call(
        mix_kernel,
        grid=(rows // block,),
        out_shape=pltpu.HBM(pieces.shape, BF),
        in_specs=[matrix, matrix, piece, ANY],
        out_specs=piece,
        compiler_params=params(),
        cost_estimate=cost(4 * n * n * width * rows // block, 4 * pieces.size + 4 * n * n),
        name="mix",
    )(hi, lo, pieces, after)


def spread_kernel(m_ref, hi_ref, lo_ref):
    n, replicas = hi_ref.shape[0], m_ref.shape[0]
    narrow = n // replicas

    def chosen(shape, along):
        group = lax.broadcasted_iota(jnp.int32, shape, along) // narrow
        return jnp.where(lax.broadcasted_iota(jnp.int32, shape, 1 - along) == group, 1.0, 0.0).astype(BF)

    rows, columns = chosen((n, replicas), 0), chosen((replicas, n), 1)
    same = lax.broadcasted_iota(jnp.int32, (n, n), 0) % narrow == lax.broadcasted_iota(jnp.int32, (n, n), 1) % narrow
    left = m_ref[...]
    for ref in (hi_ref, lo_ref):
        part = left.astype(BF)
        left = left - part.astype(F32)
        ref[...] = jnp.where(same, nn(nn(rows, part).astype(BF), columns), 0.0).astype(BF)


def spread_matrix(matrix):
    n = 16 * matrix.shape[0]
    return pl.pallas_call(
        spread_kernel,
        out_shape=[jax.ShapeDtypeStruct((n, n), BF)] * 2,
        in_specs=[VMEM],
        out_specs=[VMEM, VMEM],
        compiler_params=params(),
        cost_estimate=cost(2 * n * n * matrix.shape[0], 4 * n * n),
        name="spread",
    )(matrix)


LANDINGS = 6


def landed_kernel(u_ref, after_ref, o_ref, held, into, out_of):
    rows = u_ref.shape[0] // LANDINGS
    at = [pl.ds(i * rows, rows) for i in range(LANDINGS)]
    loads = [pltpu.make_async_copy(u_ref.at[at[i], :], held.at[at[i], :], into.at[i]) for i in range(LANDINGS)]
    stores = [pltpu.make_async_copy(held.at[at[i], :], o_ref.at[at[i], :], out_of.at[i]) for i in range(LANDINGS)]
    for load in loads:
        load.start()
    for load, store in zip(loads, stores):
        load.wait()
        store.start()
    for store in stores:
        store.wait()


def landed(array, after):
    return pl.pallas_call(
        landed_kernel,
        out_shape=pltpu.HBM(array.shape, BF),
        in_specs=[ANY, ANY],
        out_specs=HBM,
        scratch_shapes=[
            pltpu.VMEM(array.shape, BF),
            pltpu.SemaphoreType.DMA((LANDINGS,)),
            pltpu.SemaphoreType.DMA((LANDINGS,)),
        ],
        compiler_params=params(),
        cost_estimate=cost(0, 4 * array.size),
        name="landed",
    )(array, after)


def passed_along(shard):
    length = lax.axis_size("section")
    return lax.ppermute(shard, "section", [(i, i - 1) for i in range(1, length)])


def other_core(shard):
    return lax.ppermute(shard, "tp", [(0, 1), (1, 0)])


def sent_out(block):
    return lax.all_to_all(block, "rep", split_axis=0, concat_axis=0, tiled=True)


def shards(inputs, loss_grad, w_in, w_out, mixing):
    segments = lax.axis_size("section")
    segment_index = lax.axis_index("section")
    core = lax.axis_index("tp")
    replicas = lax.axis_size("rep")
    weight_in = w_in[0, 0]
    weight_out = w_out[0, 0]
    units = weight_in.shape[0]
    tokens = loss_grad.shape[0]
    own = tokens // 2

    core_at = jnp.reshape(core, (1,)).astype(jnp.int32)
    last = (segment_index == segments - 1).astype(jnp.int32)
    other_x = other_core(inputs[0])
    other_dy = other_core(loss_grad)
    own_x, own_dy, own_in, own_out = kept(inputs[0], loss_grad, weight_in, weight_out, mib=54)
    late_in, late_out, other_x, other_dy, own_x = lax.optimization_barrier(
        (weight_in, weight_out, other_x, other_dy, own_x)
    )
    other_in = other_core(late_in)
    other_out = other_core(late_out)
    at = jnp.stack([core.astype(jnp.int32), last])
    x_rows, x_own, cot = entering(at, own_x, other_x, own_dy, other_dy)
    act_t, slopes_t, own_in_t, own_slopes = unit_parts(core_at, own_in, x_rows)
    hi, lo = spread_matrix(mixing)

    columns = own // CHUNKS
    halves = [first_turn(at, c, cot, own_out, own_in_t, slopes_t) for c in range(CHUNKS)]
    kept_cot = [[half[0] for half in halves]]
    kept_result = [[both_parts(half[0], half[1], other_core(half[2])) for half in halves]]
    cots = [passed_along(r) for r in kept_result[0]]

    other_in, other_out = kept(other_in, other_out)
    other_slopes, other_in_t = token_slopes(x_own, other_in)
    slopes, wouts, wins_t = (own_slopes, other_slopes), (own_out, other_out), (own_in_t, other_in_t)
    for turn_index in range(1, segments - 1):
        results = [turn(cots[c], wouts, wins_t, slopes, c * columns, mixing) for c in range(CHUNKS)]
        kept_cot.append(cots)
        kept_result.append(results)
        cots = [passed_along(r) for r in results]
    kept_cot.append(cots)

    def summed(kept):
        parts = []
        for c in range(CHUNKS):
            total = kept[0][c]
            for t in range(1, segments):
                total = total + kept[t][c]
            parts.append(total)
        return jnp.concatenate(parts, axis=1)

    cot_t = lax.all_gather(summed(kept_cot), "tp", axis=1, tiled=True)
    updated_in = update_in(slopes_t, cot_t, x_rows, own_out, own_in)
    pieces_in = sent_out(updated_in.reshape(replicas, units // replicas, D))
    updated_out = update_out(act_t, cot_t, own_out)
    pieces_out = sent_out(updated_out.reshape(replicas, units // replicas, D))
    mixture_in = mix(hi, lo, pieces_in, mixing)
    back_in = sent_out(mixture_in)
    back_out = sent_out(mix(hi, lo, pieces_out, mixture_in))
    mixed_in = landed(back_in.reshape(units, D), mixing)

    kept_result.append([turn(cots[c], wouts, wins_t, slopes, c * columns, mixed_in) for c in range(CHUNKS)])
    result = summed(kept_result)
    width = D // 2
    mine = lax.dynamic_slice_in_dim(result, core * width, width, 0)
    theirs = other_core(lax.dynamic_slice_in_dim(result, (1 - core) * width, width, 0))
    dx = leaving(core_at, mine, theirs)
    mixed_out = landed(back_out.reshape(units, D), dx[:16, :128])
    return dx[None], mixed_in[None, None], mixed_out[None, None]


def solution(mesh):
    in_specs = (
        P("section", "rep", "tp"),
        P("rep", "tp"),
        P("rep", "section", "tp", None),
        P("rep", "section", "tp", None),
        P(),
    )
    out_specs = (
        P("section", "rep", "tp"),
        P("rep", "section", "tp", None),
        P("rep", "section", "tp", None),
    )
    return jax.shard_map(shards, mesh=mesh, in_specs=in_specs, out_specs=out_specs, check_vma=False)
```

```python
import jax
import jax.numpy as jnp
from jax import lax
from jax.experimental import pallas as pl
from jax.experimental.pallas import tpu as pltpu
from jax.sharding import PartitionSpec as P

D = 768
FF = 3072
BF = jnp.bfloat16
F32 = jnp.float32

step_size = 4.0
root_half = 0.7071067811865476
inv_root_two_pi = 0.3989422804014327
in_scale = D ** (-0.5)
out_scale = FF ** (-0.5)

CHUNKS = 2
BLOCK = 512
MIB = 1024 * 1024
VMEM = pl.BlockSpec(memory_space=pltpu.VMEM)
HBM = pl.BlockSpec(memory_space=pltpu.HBM)
ANY = pl.BlockSpec(memory_space=pl.ANY)
SMEM = pl.BlockSpec(memory_space=pltpu.SMEM)


def params(mib=20):
    return pltpu.CompilerParams(vmem_limit_bytes=mib * MIB)


def cost(flops, nbytes, trans=0):
    return pl.CostEstimate(flops=flops, bytes_accessed=nbytes, transcendentals=trans)


def nt(left, right):
    return lax.dot_general(left, right, (((1,), (1,)), ((), ())), preferred_element_type=F32)


def nn(left, right):
    return lax.dot_general(left, right, (((1,), (0,)), ((), ())), preferred_element_type=F32)


def gelu_parts(preact):
    normal_cdf = 0.5 * (1.0 + lax.erf(preact * root_half))
    density = jnp.exp(-0.5 * preact * preact) * inv_root_two_pi
    return preact * normal_cdf, normal_cdf + preact * density


def blocks(h):
    return [pl.ds(i * BLOCK, BLOCK) for i in range(h // BLOCK)]


def joined(core, mine, theirs):
    return jnp.where(core == 0, jnp.concatenate([mine, theirs], axis=1), jnp.concatenate([theirs, mine], axis=1))


def opening_kernel(at, x_hbm, other_x_hbm, dy_hbm, other_dy_hbm, w_hbm, *refs):
    whole_ref, own_x_ref, cot_ref, a_ref, s_ref, own_s_ref, t_ref = refs[:7]
    x_ref, other_x_ref, dy_ref, other_dy_ref, w_ref, sems = refs[7:]
    core = at[0]
    own = own_x_ref.shape[0]
    parts = blocks(w_ref.shape[0])
    pairs = [(x_hbm, x_ref), (other_x_hbm, other_x_ref)]
    pairs += [(w_hbm.at[rows, :], w_ref.at[rows, :]) for rows in parts]
    pairs += [(dy_hbm, dy_ref), (other_dy_hbm, other_dy_ref)]
    copies = [pltpu.make_async_copy(*pair, sems.at[i]) for i, pair in enumerate(pairs)]
    for copy in copies:
        copy.start()
    for copy in copies[:2]:
        copy.wait()
    whole_ref[...] = joined(core, x_ref[...], other_x_ref[...])
    own_x_ref[...] = whole_ref[pl.ds(pl.multiple_of(core * own, own), own), :]
    x = whole_ref[...]
    for i, rows in enumerate(parts):
        copies[2 + i].wait()
        weight = w_ref[rows, :]
        values, slopes = gelu_parts(nt(weight, x) * in_scale)
        a_ref[rows, :] = values.astype(BF)
        s_ref[rows, :] = slopes
        own_s_ref[rows, :] = jnp.where(core == 0, slopes[:, :own], slopes[:, own:])
        t_ref[:, rows] = jnp.transpose(weight)
    for copy in copies[-2:]:
        copy.wait()
    dy = joined(core, dy_ref[...], other_dy_ref[...])
    cot_ref[...] = jnp.transpose(jnp.where(at[1] == 1, dy, jnp.zeros_like(dy)))


def opening(at, x, other_x, dy, other_dy, weight_in):
    m, h = dy.shape[0], weight_in.shape[0]
    own = m // 2
    shapes = [
        ((m, D), BF), ((own, D), BF), ((D, m), BF), ((h, m), BF), ((h, m), F32), ((h, own), F32), ((D, h), BF),
    ]
    return pl.pallas_call(
        opening_kernel,
        out_shape=[pltpu.VMEM(*s) for s in shapes],
        in_specs=[SMEM] + [ANY] * 5,
        out_specs=[VMEM] * len(shapes),
        scratch_shapes=[
            *[pltpu.VMEM(dy.shape, BF)] * 4,
            pltpu.VMEM((h, D), BF),
            pltpu.SemaphoreType.DMA((4 + h // BLOCK,)),
        ],
        compiler_params=params(46),
        cost_estimate=cost(2 * m * h * D, 6 * h * D + 8 * m * h, 2 * m * h),
        name="opening",
    )(at, x, other_x, dy, other_dy, weight_in)


def first_turn_kernel(chunk, m, at, c_ref, wo_ref, wt_ref, s_ref, cot_ref, mine_ref, theirs_ref, delta):
    own = c_ref.shape[1] // 2
    lanes = [pl.ds(pl.multiple_of(side * own + chunk * m, m), m) for side in (at[0], 1 - at[0])]
    cot = jnp.concatenate([c_ref[:, lane] for lane in lanes], axis=1)
    for at_rows in blocks(wo_ref.shape[0]):
        backward = nn(wo_ref[at_rows, :], cot) * out_scale
        slopes = jnp.concatenate([s_ref[at_rows, lane] for lane in lanes], axis=1)
        delta[at_rows, :] = (slopes * backward).astype(BF)
    partial = (nn(wt_ref[...], delta[...]) * in_scale).astype(BF)
    cot_ref[...] = cot[:, :m]
    mine_ref[...] = partial[:, :m]
    theirs_ref[...] = partial[:, m:]


def first_turn(at, chunk, cot, weight_out, weight_in_t, slopes):
    h, tokens = slopes.shape
    m = tokens // 2 // CHUNKS
    return pl.pallas_call(
        lambda *refs: first_turn_kernel(chunk, m, *refs),
        out_shape=[jax.ShapeDtypeStruct((D, m), BF)] * 3,
        in_specs=[SMEM] + [VMEM] * 4,
        out_specs=[VMEM] * 3,
        scratch_shapes=[pltpu.VMEM((h, 2 * m), BF)],
        compiler_params=params(),
        cost_estimate=cost(8 * m * h * D, 4 * h * D + 8 * m * h),
        name="first_turn",
    )(at, cot, weight_out, weight_in_t, slopes)


def both_parts_kernel(c_ref, mine_ref, theirs_ref, o_ref):
    branch = mine_ref[...].astype(F32) + theirs_ref[...].astype(F32)
    o_ref[...] = (c_ref[...].astype(F32) + branch).astype(BF)


def both_parts(cot, mine, theirs):
    return pl.pallas_call(
        both_parts_kernel,
        out_shape=jax.ShapeDtypeStruct(cot.shape, BF),
        in_specs=[VMEM] * 3,
        out_specs=VMEM,
        compiler_params=params(),
        cost_estimate=cost(0, 8 * cot.size),
        name="both_parts",
    )(cot, mine, theirs)


def token_slopes_kernel(x_ref, w_ref, s_ref, t_ref):
    x = x_ref[...]
    for at in blocks(w_ref.shape[0]):
        weight = w_ref[at, :]
        s_ref[at, :] = gelu_parts(nt(weight, x) * in_scale)[1]
        t_ref[:, at] = jnp.transpose(weight)


def token_slopes(x_rows, weight_in):
    m, h = x_rows.shape[0], weight_in.shape[0]
    return pl.pallas_call(
        token_slopes_kernel,
        out_shape=[jax.ShapeDtypeStruct((h, m), F32), jax.ShapeDtypeStruct((D, h), BF)],
        in_specs=[VMEM, VMEM],
        out_specs=[VMEM, VMEM],
        compiler_params=params(),
        cost_estimate=cost(2 * m * h * D, 4 * h * D + 4 * m * h, 2 * m * h),
        name="token_slopes",
    )(x_rows, weight_in)


def kept_kernel(*refs):
    count = len(refs) // 2
    sems = refs[-1]
    copies = [pltpu.make_async_copy(refs[i], refs[count + i], sems.at[i]) for i in range(count)]
    for copy in copies:
        copy.start()
    for copy in copies:
        copy.wait()


def kept(*arrays, mib=20):
    return pl.pallas_call(
        kept_kernel,
        out_shape=[pltpu.VMEM(array.shape, BF) for array in arrays],
        in_specs=[ANY] * len(arrays),
        out_specs=[VMEM] * len(arrays),
        scratch_shapes=[pltpu.SemaphoreType.DMA((len(arrays),))],
        compiler_params=params(mib),
        cost_estimate=cost(0, 4 * sum(array.size for array in arrays)),
        name="kept",
    )(*arrays)


def turn_kernel(col0, c_ref, wo0_ref, wo1_ref, wt0_ref, wt1_ref, s0_ref, s1_ref, after_ref, o_ref, delta):
    cot = c_ref[...]
    m = cot.shape[1]
    branch = None
    for wo_ref, wt_ref, s_ref in ((wo0_ref, wt0_ref, s0_ref), (wo1_ref, wt1_ref, s1_ref)):
        for at in blocks(wo_ref.shape[0]):
            backward = nn(wo_ref[at, :], cot) * out_scale
            delta[at, :] = (s_ref[at, pl.ds(col0, m)] * backward).astype(BF)
        partial = (nn(wt_ref[...], delta[...]) * in_scale).astype(BF).astype(F32)
        branch = partial if branch is None else branch + partial
    o_ref[...] = (cot.astype(F32) + branch).astype(BF)


def turn(cot, wouts, wins_t, slopes, col0, after):
    m = cot.shape[1]
    h = wouts[0].shape[0]
    return pl.pallas_call(
        lambda *refs: turn_kernel(col0, *refs),
        out_shape=jax.ShapeDtypeStruct((D, m), BF),
        in_specs=[VMEM] * 7 + [ANY],
        out_specs=VMEM,
        scratch_shapes=[pltpu.VMEM((h, m), BF)],
        compiler_params=params(),
        cost_estimate=cost(8 * m * h * D, 8 * h * D + 8 * m * h),
        name="turn",
    )(cot, wouts[0], wouts[1], wins_t[0], wins_t[1], slopes[0], slopes[1], after)


def leaving_kernel(core, mine_ref, theirs_ref, o_ref):
    own = mine_ref.shape[1]
    o_ref[pl.ds(pl.multiple_of(core[0] * own, own), own), :] = jnp.transpose(mine_ref[...])
    o_ref[pl.ds(pl.multiple_of((1 - core[0]) * own, own), own), :] = jnp.transpose(theirs_ref[...])


def leaving(core, mine, theirs):
    width, own = mine.shape
    return pl.pallas_call(
        leaving_kernel,
        out_shape=jax.ShapeDtypeStruct((2 * own, width), BF),
        in_specs=[SMEM, VMEM, VMEM],
        out_specs=VMEM,
        compiler_params=params(),
        cost_estimate=cost(0, 8 * own * width),
        name="leaving",
    )(core, mine, theirs)


def all_tokens(core, refs):
    mine, theirs = refs[:CHUNKS], refs[CHUNKS:]
    beside = lambda first, second: jnp.concatenate([ref[...] for ref in first + second], axis=1)
    return jnp.where(core == 0, beside(mine, theirs), beside(theirs, mine))


def copies_out(scratch, o_ref, sems, i):
    at = pl.ds(i * BLOCK, BLOCK)
    return pltpu.make_async_copy(scratch.at[at, :], o_ref.at[at, :], sems.at[i])


def update_out_kernel(core, *refs):
    a_ref, w_ref, o_ref, scratch, sems = refs[2 * CHUNKS :]
    cot = jnp.transpose(all_tokens(core[0], refs[: 2 * CHUNKS]))
    parts = blocks(a_ref.shape[0])
    for i, at in enumerate(parts):
        grad = nn(a_ref[at, :], cot) * out_scale
        scratch[at, :] = (w_ref[at, :].astype(F32) - step_size * grad).astype(BF)
        copies_out(scratch, o_ref, sems, i).start()
    for i in range(len(parts)):
        copies_out(scratch, o_ref, sems, i).wait()


def update_out(core, cots, act_t, weight_out):
    h, m = act_t.shape
    return pl.pallas_call(
        update_out_kernel,
        out_shape=pltpu.HBM((h, D), BF),
        in_specs=[SMEM] + [VMEM] * (2 * CHUNKS + 2),
        out_specs=HBM,
        scratch_shapes=[pltpu.VMEM((h, D), BF), pltpu.SemaphoreType.DMA((h // BLOCK,))],
        compiler_params=params(),
        cost_estimate=cost(2 * m * h * D, 2 * m * h + 4 * h * D),
        name="update_out",
    )(core, *cots, act_t, weight_out)


def update_in_kernel(core, *refs):
    s_ref, x_ref, wo_ref, wi_ref, o_ref, scratch, sems = refs[2 * CHUNKS :]
    cot, x = all_tokens(core[0], refs[: 2 * CHUNKS]), x_ref[...]
    parts = blocks(s_ref.shape[0])
    for i, at in enumerate(parts):
        backward = nn(wo_ref[at, :], cot) * out_scale
        delta = (s_ref[at, :] * backward).astype(BF)
        grad = nn(delta, x) * in_scale
        scratch[at, :] = (wi_ref[at, :].astype(F32) - step_size * grad).astype(BF)
        copies_out(scratch, o_ref, sems, i).start()
    for i in range(len(parts)):
        copies_out(scratch, o_ref, sems, i).wait()


def update_in(core, cots, slopes_t, x_rows, weight_out, weight_in):
    h, m = slopes_t.shape
    return pl.pallas_call(
        update_in_kernel,
        out_shape=pltpu.HBM((h, D), BF),
        in_specs=[SMEM] + [VMEM] * (2 * CHUNKS + 4),
        out_specs=HBM,
        scratch_shapes=[pltpu.VMEM((h, D), BF), pltpu.SemaphoreType.DMA((h // BLOCK,))],
        compiler_params=params(),
        cost_estimate=cost(4 * m * h * D, 4 * m * h + 6 * h * D),
        name="update_in",
    )(core, *cots, slopes_t, x_rows, weight_out, weight_in)


def mix_kernel(hi_ref, lo_ref, u_ref, after_ref, o_ref):
    replicas, rows, width = u_ref.shape
    u = u_ref[...].reshape(replicas * rows, width)
    mixed = nn(hi_ref[...], u) + nn(lo_ref[...], u)
    o_ref[...] = mixed.astype(BF).reshape(replicas, rows, width)


def mix(hi, lo, pieces, after):
    replicas, rows, width = pieces.shape
    block = 16
    n = hi.shape[0]
    matrix = pl.BlockSpec((n, n), lambda i: (0, 0))
    piece = pl.BlockSpec((replicas, block, width), lambda i: (0, i, 0))
    return pl.pallas_call(
        mix_kernel,
        grid=(rows // block,),
        out_shape=pltpu.HBM(pieces.shape, BF),
        in_specs=[matrix, matrix, piece, ANY],
        out_specs=piece,
        compiler_params=params(),
        cost_estimate=cost(4 * n * n * width * rows // block, 4 * pieces.size + 4 * n * n),
        name="mix",
    )(hi, lo, pieces, after)


def spread_kernel(m_ref, hi_ref, lo_ref):
    n, replicas = hi_ref.shape[0], m_ref.shape[0]
    narrow = n // replicas

    def chosen(shape, along):
        group = lax.broadcasted_iota(jnp.int32, shape, along) // narrow
        return jnp.where(lax.broadcasted_iota(jnp.int32, shape, 1 - along) == group, 1.0, 0.0).astype(BF)

    rows, columns = chosen((n, replicas), 0), chosen((replicas, n), 1)
    same = lax.broadcasted_iota(jnp.int32, (n, n), 0) % narrow == lax.broadcasted_iota(jnp.int32, (n, n), 1) % narrow
    left = m_ref[...]
    for ref in (hi_ref, lo_ref):
        part = left.astype(BF)
        left = left - part.astype(F32)
        ref[...] = jnp.where(same, nn(nn(rows, part).astype(BF), columns), 0.0).astype(BF)


def spread_matrix(matrix):
    n = 16 * matrix.shape[0]
    return pl.pallas_call(
        spread_kernel,
        out_shape=[jax.ShapeDtypeStruct((n, n), BF)] * 2,
        in_specs=[VMEM],
        out_specs=[VMEM, VMEM],
        compiler_params=params(),
        cost_estimate=cost(2 * n * n * matrix.shape[0], 4 * n * n),
        name="spread",
    )(matrix)


LANDINGS = 6


def landed_kernel(u_ref, after_ref, o_ref, held, into, out_of):
    rows = u_ref.shape[0] // LANDINGS
    at = [pl.ds(i * rows, rows) for i in range(LANDINGS)]
    loads = [pltpu.make_async_copy(u_ref.at[at[i], :], held.at[at[i], :], into.at[i]) for i in range(LANDINGS)]
    stores = [pltpu.make_async_copy(held.at[at[i], :], o_ref.at[at[i], :], out_of.at[i]) for i in range(LANDINGS)]
    for load in loads:
        load.start()
    for load, store in zip(loads, stores):
        load.wait()
        store.start()
    for store in stores:
        store.wait()


def landed(array, after):
    return pl.pallas_call(
        landed_kernel,
        out_shape=pltpu.HBM(array.shape, BF),
        in_specs=[ANY, ANY],
        out_specs=HBM,
        scratch_shapes=[
            pltpu.VMEM(array.shape, BF),
            pltpu.SemaphoreType.DMA((LANDINGS,)),
            pltpu.SemaphoreType.DMA((LANDINGS,)),
        ],
        compiler_params=params(),
        cost_estimate=cost(0, 4 * array.size),
        name="landed",
    )(array, after)


def passed_along(shard):
    length = lax.axis_size("section")
    return lax.ppermute(shard, "section", [(i, i - 1) for i in range(1, length)])


def other_core(shard):
    return lax.ppermute(shard, "tp", [(0, 1), (1, 0)])


def sent_out(block):
    return lax.all_to_all(block, "rep", split_axis=0, concat_axis=0, tiled=True)


def shards(inputs, loss_grad, w_in, w_out, mixing):
    segments = lax.axis_size("section")
    segment_index = lax.axis_index("section")
    core = lax.axis_index("tp")
    replicas = lax.axis_size("rep")
    weight_in = w_in[0, 0]
    weight_out = w_out[0, 0]
    units = weight_in.shape[0]
    tokens = loss_grad.shape[0]
    own = tokens // 2

    core_at = jnp.reshape(core, (1,)).astype(jnp.int32)
    last = (segment_index == segments - 1).astype(jnp.int32)
    other_x = other_core(inputs[0])
    other_dy = other_core(loss_grad)
    late_in, late_out, other_x, other_dy = lax.optimization_barrier((weight_in, weight_out, other_x, other_dy))
    other_in = other_core(late_in)
    other_out = other_core(late_out)
    at = jnp.stack([core.astype(jnp.int32), last])
    x_rows, x_own, cot, act_t, slopes_t, own_slopes, own_in_t = opening(
        at, inputs[0], other_x, loss_grad, other_dy, weight_in
    )
    hi, lo = spread_matrix(mixing)

    columns = own // CHUNKS
    halves = [first_turn(at, c, cot, weight_out, own_in_t, slopes_t) for c in range(CHUNKS)]
    kept_cot = [[half[0] for half in halves]]
    kept_result = [[both_parts(half[0], half[1], other_core(half[2])) for half in halves]]
    cots = [passed_along(r) for r in kept_result[0]]

    other_in, other_out = kept(other_in, other_out)
    other_slopes, other_in_t = token_slopes(x_own, other_in)
    slopes, wouts, wins_t = (own_slopes, other_slopes), (weight_out, other_out), (own_in_t, other_in_t)
    for turn_index in range(1, segments - 1):
        results = [turn(cots[c], wouts, wins_t, slopes, c * columns, mixing) for c in range(CHUNKS)]
        kept_cot.append(cots)
        kept_result.append(results)
        cots = [passed_along(r) for r in results]
    kept_cot.append(cots)

    def summed(kept):
        parts = []
        for c in range(CHUNKS):
            total = kept[0][c]
            for t in range(1, segments):
                total = total + kept[t][c]
            parts.append(total)
        return parts

    mine = summed(kept_cot)
    all_cots = mine + [other_core(part) for part in mine]
    updated_in = update_in(core_at, all_cots, slopes_t, x_rows, weight_out, weight_in)
    pieces_in = sent_out(updated_in.reshape(replicas, units // replicas, D))
    updated_out = update_out(core_at, all_cots, act_t, weight_out)
    pieces_out = sent_out(updated_out.reshape(replicas, units // replicas, D))
    mixture_in = mix(hi, lo, pieces_in, mixing)
    back_in = sent_out(mixture_in)
    back_out = sent_out(mix(hi, lo, pieces_out, mixture_in))
    mixed_in = landed(back_in.reshape(units, D), mixing)

    kept_result.append([turn(cots[c], wouts, wins_t, slopes, c * columns, mixed_in) for c in range(CHUNKS)])
    result = jnp.concatenate(summed(kept_result), axis=1)
    width = D // 2
    mine = lax.dynamic_slice_in_dim(result, core * width, width, 0)
    theirs = other_core(lax.dynamic_slice_in_dim(result, (1 - core) * width, width, 0))
    dx = leaving(core_at, mine, theirs)
    mixed_out = landed(back_out.reshape(units, D), dx[:16, :128])
    return dx[None], mixed_in[None, None], mixed_out[None, None]


def solution(mesh):
    in_specs = (
        P("section", "rep", "tp"),
        P("rep", "tp"),
        P("rep", "section", "tp", None),
        P("rep", "section", "tp", None),
        P(),
    )
    out_specs = (
        P("section", "rep", "tp"),
        P("rep", "section", "tp", None),
        P("rep", "section", "tp", None),
    )
    return jax.shard_map(shards, mesh=mesh, in_specs=in_specs, out_specs=out_specs, check_vma=False)
```

```python
import jax
import jax.numpy as jnp
from jax import lax
from jax.experimental import pallas as pl
from jax.experimental.pallas import tpu as pltpu
from jax.sharding import PartitionSpec as P

D = 768
FF = 3072
BF = jnp.bfloat16
F32 = jnp.float32

step_size = 4.0
root_half = 0.7071067811865476
inv_root_two_pi = 0.3989422804014327
in_scale = D ** (-0.5)
out_scale = FF ** (-0.5)

CHUNKS = 2
Z = 8
X = 4
WAY = -1
MAIN = 640
BLOCK = 512
MIB = 1024 * 1024
VMEM = pl.BlockSpec(memory_space=pltpu.VMEM)
HBM = pl.BlockSpec(memory_space=pltpu.HBM)
ANY = pl.BlockSpec(memory_space=pl.ANY)
SMEM = pl.BlockSpec(memory_space=pltpu.SMEM)


def params(mib=20):
    return pltpu.CompilerParams(vmem_limit_bytes=mib * MIB)


def cost(flops, nbytes, trans=0):
    return pl.CostEstimate(flops=flops, bytes_accessed=nbytes, transcendentals=trans)


def nt(left, right):
    return lax.dot_general(left, right, (((1,), (1,)), ((), ())), preferred_element_type=F32)


def nn(left, right):
    return lax.dot_general(left, right, (((1,), (0,)), ((), ())), preferred_element_type=F32)


def gelu_parts(preact):
    normal_cdf = 0.5 * (1.0 + lax.erf(preact * root_half))
    density = jnp.exp(-0.5 * preact * preact) * inv_root_two_pi
    return preact * normal_cdf, normal_cdf + preact * density


def blocks(h):
    return [pl.ds(i * BLOCK, BLOCK) for i in range(h // BLOCK)]


def joined(core, mine, theirs):
    return jnp.where(core == 0, jnp.concatenate([mine, theirs], axis=1), jnp.concatenate([theirs, mine], axis=1))


def opening_kernel(at, x_hbm, other_x_hbm, dy_hbm, other_dy_hbm, w_hbm, *refs):
    whole_ref, own_x_ref, cot_ref, a_ref, s_ref, own_s_ref, t_ref = refs[:7]
    x_ref, other_x_ref, dy_ref, other_dy_ref, w_ref, sems = refs[7:]
    core = at[0]
    own = own_x_ref.shape[0]
    parts = blocks(w_ref.shape[0])
    pairs = [(x_hbm, x_ref), (other_x_hbm, other_x_ref)]
    pairs += [(w_hbm.at[rows, :], w_ref.at[rows, :]) for rows in parts]
    pairs += [(dy_hbm, dy_ref), (other_dy_hbm, other_dy_ref)]
    copies = [pltpu.make_async_copy(*pair, sems.at[i]) for i, pair in enumerate(pairs)]
    for copy in copies:
        copy.start()
    for copy in copies[:2]:
        copy.wait()
    whole_ref[...] = joined(core, x_ref[...], other_x_ref[...])
    own_x_ref[...] = whole_ref[pl.ds(pl.multiple_of(core * own, own), own), :]
    x = whole_ref[...]
    for i, rows in enumerate(parts):
        copies[2 + i].wait()
        weight = w_ref[rows, :]
        values, slopes = gelu_parts(nt(weight, x) * in_scale)
        a_ref[rows, :] = values.astype(BF)
        s_ref[rows, :] = slopes
        own_s_ref[rows, :] = jnp.where(core == 0, slopes[:, :own], slopes[:, own:])
        t_ref[:, rows] = jnp.transpose(weight)
    for copy in copies[-2:]:
        copy.wait()
    dy = joined(core, dy_ref[...], other_dy_ref[...])
    cot_ref[...] = jnp.transpose(jnp.where(at[1] == 1, dy, jnp.zeros_like(dy)))


def opening(at, x, other_x, dy, other_dy, weight_in):
    m, h = dy.shape[0], weight_in.shape[0]
    own = m // 2
    shapes = [
        ((m, D), BF), ((own, D), BF), ((D, m), BF), ((h, m), BF), ((h, m), F32), ((h, own), F32), ((D, h), BF),
    ]
    return pl.pallas_call(
        opening_kernel,
        out_shape=[pltpu.VMEM(*s) for s in shapes],
        in_specs=[SMEM] + [ANY] * 5,
        out_specs=[VMEM] * len(shapes),
        scratch_shapes=[
            *[pltpu.VMEM(dy.shape, BF)] * 4,
            pltpu.VMEM((h, D), BF),
            pltpu.SemaphoreType.DMA((4 + h // BLOCK,)),
        ],
        compiler_params=params(46),
        cost_estimate=cost(2 * m * h * D, 6 * h * D + 8 * m * h, 2 * m * h),
        name="opening",
    )(at, x, other_x, dy, other_dy, weight_in)


def first_turn_kernel(chunk, m, at, c_ref, wo_ref, wt_ref, s_ref, cot_ref, mine_ref, theirs_ref, delta):
    own = c_ref.shape[1] // 2
    lanes = [pl.ds(pl.multiple_of(side * own + chunk * m, m), m) for side in (at[0], 1 - at[0])]
    cot = jnp.concatenate([c_ref[:, lane] for lane in lanes], axis=1)
    for at_rows in blocks(wo_ref.shape[0]):
        backward = nn(wo_ref[at_rows, :], cot) * out_scale
        slopes = jnp.concatenate([s_ref[at_rows, lane] for lane in lanes], axis=1)
        delta[at_rows, :] = (slopes * backward).astype(BF)
    partial = (nn(wt_ref[...], delta[...]) * in_scale).astype(BF)
    cot_ref[...] = cot[:, :m]
    mine_ref[...] = partial[:, :m]
    theirs_ref[...] = partial[:, m:]


def first_turn(at, chunk, cot, weight_out, weight_in_t, slopes):
    h, tokens = slopes.shape
    m = tokens // 2 // CHUNKS
    return pl.pallas_call(
        lambda *refs: first_turn_kernel(chunk, m, *refs),
        out_shape=[jax.ShapeDtypeStruct((D, m), BF)] * 3,
        in_specs=[SMEM] + [VMEM] * 4,
        out_specs=[VMEM] * 3,
        scratch_shapes=[pltpu.VMEM((h, 2 * m), BF)],
        compiler_params=params(),
        cost_estimate=cost(8 * m * h * D, 4 * h * D + 8 * m * h),
        name="first_turn",
    )(at, cot, weight_out, weight_in_t, slopes)


def both_parts_kernel(c_ref, mine_ref, theirs_ref, o_ref):
    branch = mine_ref[...].astype(F32) + theirs_ref[...].astype(F32)
    o_ref[...] = (c_ref[...].astype(F32) + branch).astype(BF)


def both_parts(cot, mine, theirs):
    return pl.pallas_call(
        both_parts_kernel,
        out_shape=jax.ShapeDtypeStruct(cot.shape, BF),
        in_specs=[VMEM] * 3,
        out_specs=VMEM,
        compiler_params=params(),
        cost_estimate=cost(0, 8 * cot.size),
        name="both_parts",
    )(cot, mine, theirs)


def token_slopes_kernel(x_ref, w_ref, s_ref, t_ref):
    x = x_ref[...]
    for at in blocks(w_ref.shape[0]):
        weight = w_ref[at, :]
        s_ref[at, :] = gelu_parts(nt(weight, x) * in_scale)[1]
        t_ref[:, at] = jnp.transpose(weight)


def token_slopes(x_rows, weight_in):
    m, h = x_rows.shape[0], weight_in.shape[0]
    return pl.pallas_call(
        token_slopes_kernel,
        out_shape=[jax.ShapeDtypeStruct((h, m), F32), jax.ShapeDtypeStruct((D, h), BF)],
        in_specs=[VMEM, VMEM],
        out_specs=[VMEM, VMEM],
        compiler_params=params(),
        cost_estimate=cost(2 * m * h * D, 4 * h * D + 4 * m * h, 2 * m * h),
        name="token_slopes",
    )(x_rows, weight_in)


def kept_kernel(*refs):
    count = len(refs) // 2
    sems = refs[-1]
    copies = [pltpu.make_async_copy(refs[i], refs[count + i], sems.at[i]) for i in range(count)]
    for copy in copies:
        copy.start()
    for copy in copies:
        copy.wait()


def kept(*arrays, mib=20):
    return pl.pallas_call(
        kept_kernel,
        out_shape=[pltpu.VMEM(array.shape, BF) for array in arrays],
        in_specs=[ANY] * len(arrays),
        out_specs=[VMEM] * len(arrays),
        scratch_shapes=[pltpu.SemaphoreType.DMA((len(arrays),))],
        compiler_params=params(mib),
        cost_estimate=cost(0, 4 * sum(array.size for array in arrays)),
        name="kept",
    )(*arrays)


def turn_kernel(col0, c_ref, wo0_ref, wo1_ref, wt0_ref, wt1_ref, s0_ref, s1_ref, after_ref, o_ref, delta):
    cot = c_ref[...]
    m = cot.shape[1]
    branch = None
    for wo_ref, wt_ref, s_ref in ((wo0_ref, wt0_ref, s0_ref), (wo1_ref, wt1_ref, s1_ref)):
        for at in blocks(wo_ref.shape[0]):
            backward = nn(wo_ref[at, :], cot) * out_scale
            delta[at, :] = (s_ref[at, pl.ds(col0, m)] * backward).astype(BF)
        partial = (nn(wt_ref[...], delta[...]) * in_scale).astype(BF).astype(F32)
        branch = partial if branch is None else branch + partial
    o_ref[...] = (cot.astype(F32) + branch).astype(BF)


def turn(cot, wouts, wins_t, slopes, col0, after):
    m = cot.shape[1]
    h = wouts[0].shape[0]
    return pl.pallas_call(
        lambda *refs: turn_kernel(col0, *refs),
        out_shape=jax.ShapeDtypeStruct((D, m), BF),
        in_specs=[VMEM] * 7 + [ANY],
        out_specs=VMEM,
        scratch_shapes=[pltpu.VMEM((h, m), BF)],
        compiler_params=params(),
        cost_estimate=cost(8 * m * h * D, 8 * h * D + 8 * m * h),
        name="turn",
    )(cot, wouts[0], wouts[1], wins_t[0], wins_t[1], slopes[0], slopes[1], after)


def leaving_kernel(core, mine_ref, theirs_ref, o_ref):
    own = mine_ref.shape[1]
    o_ref[pl.ds(pl.multiple_of(core[0] * own, own), own), :] = jnp.transpose(mine_ref[...])
    o_ref[pl.ds(pl.multiple_of((1 - core[0]) * own, own), own), :] = jnp.transpose(theirs_ref[...])


def leaving(core, mine, theirs):
    width, own = mine.shape
    return pl.pallas_call(
        leaving_kernel,
        out_shape=jax.ShapeDtypeStruct((2 * own, width), BF),
        in_specs=[SMEM, VMEM, VMEM],
        out_specs=VMEM,
        compiler_params=params(),
        cost_estimate=cost(0, 8 * own * width),
        name="leaving",
    )(core, mine, theirs)


def all_tokens(core, refs):
    mine, theirs = refs[:CHUNKS], refs[CHUNKS:]
    beside = lambda first, second: jnp.concatenate([ref[...] for ref in first + second], axis=1)
    return jnp.where(core == 0, beside(mine, theirs), beside(theirs, mine))


def copies_out(scratch, o_ref, sems, i):
    at = pl.ds(i * BLOCK, BLOCK)
    return pltpu.make_async_copy(scratch.at[at, :], o_ref.at[at, :], sems.at[i])


def update_out_kernel(core, *refs):
    a_ref, w_ref, o_ref, scratch, sems = refs[2 * CHUNKS :]
    cot = jnp.transpose(all_tokens(core[0], refs[: 2 * CHUNKS]))
    parts = blocks(a_ref.shape[0])
    for i, at in enumerate(parts):
        grad = nn(a_ref[at, :], cot) * out_scale
        scratch[at, :] = (w_ref[at, :].astype(F32) - step_size * grad).astype(BF)
        copies_out(scratch, o_ref, sems, i).start()
    for i in range(len(parts)):
        copies_out(scratch, o_ref, sems, i).wait()


def update_out(core, cots, act_t, weight_out):
    h, m = act_t.shape
    return pl.pallas_call(
        update_out_kernel,
        out_shape=pltpu.HBM((h, D), BF),
        in_specs=[SMEM] + [VMEM] * (2 * CHUNKS + 2),
        out_specs=HBM,
        scratch_shapes=[pltpu.VMEM((h, D), BF), pltpu.SemaphoreType.DMA((h // BLOCK,))],
        compiler_params=params(),
        cost_estimate=cost(2 * m * h * D, 2 * m * h + 4 * h * D),
        name="update_out",
    )(core, *cots, act_t, weight_out)


def update_in_kernel(core, place, *refs):
    s_ref, x_ref, wo_ref, wi_ref, o_ref, v_ref, scratch, sems = refs[2 * CHUNKS :]
    cot, x = all_tokens(core[0], refs[: 2 * CHUNKS]), x_ref[...]
    rows = v_ref.shape[1]
    copies = []
    for i in range(Z // 2):
        at = pl.ds(2 * i * rows, 2 * rows)
        backward = nn(wo_ref[at, :], cot) * out_scale
        delta = (s_ref[at, :] * backward).astype(BF)
        grad = nn(delta, x) * in_scale
        new = (wi_ref[at, :].astype(F32) - step_size * grad).astype(BF)
        scratch[at, :] = new[:, :MAIN]
        for half in range(2):
            v_ref[lax.rem(WAY * (2 * i + half - place[0]) + 2 * Z, Z)] = new[half * rows : (half + 1) * rows, MAIN:]
        copies.append(pltpu.make_async_copy(scratch.at[at, :], o_ref.at[at, :], sems.at[i]))
        copies[-1].start()
    for copy in copies:
        copy.wait()


def update_in(core, place, cots, slopes_t, x_rows, weight_out, weight_in):
    h, m = slopes_t.shape
    return pl.pallas_call(
        update_in_kernel,
        out_shape=[pltpu.HBM((h, MAIN), BF), jax.ShapeDtypeStruct((Z, h // Z, D - MAIN), BF)],
        in_specs=[SMEM, SMEM] + [VMEM] * (2 * CHUNKS + 4),
        out_specs=[HBM, VMEM],
        scratch_shapes=[pltpu.VMEM((h, MAIN), BF), pltpu.SemaphoreType.DMA((Z // 2,))],
        compiler_params=params(),
        cost_estimate=cost(4 * m * h * D, 4 * m * h + 6 * h * D),
        name="update_in",
    )(core, place, *cots, slopes_t, x_rows, weight_out, weight_in)


def mix_kernel(hi_ref, lo_ref, u_ref, after_ref, o_ref):
    replicas, rows, width = u_ref.shape
    u = u_ref[...].reshape(replicas * rows, width)
    mixed = nn(hi_ref[...], u) + nn(lo_ref[...], u)
    o_ref[...] = mixed.astype(BF).reshape(replicas, rows, width)


def mix(hi, lo, pieces, after):
    replicas, rows, width = pieces.shape
    block = 16
    n = hi.shape[0]
    matrix = pl.BlockSpec((n, n), lambda i: (0, 0))
    piece = pl.BlockSpec((replicas, block, width), lambda i: (0, i, 0))
    return pl.pallas_call(
        mix_kernel,
        grid=(rows // block,),
        out_shape=pltpu.HBM(pieces.shape, BF),
        in_specs=[matrix, matrix, piece, ANY],
        out_specs=piece,
        compiler_params=params(),
        cost_estimate=cost(4 * n * n * width * rows // block, 4 * pieces.size + 4 * n * n),
        name="mix",
    )(hi, lo, pieces, after)


def spread_kernel(m_ref, hi_ref, lo_ref):
    n, replicas = hi_ref.shape[0], m_ref.shape[0]
    narrow = n // replicas

    def chosen(shape, along):
        group = lax.broadcasted_iota(jnp.int32, shape, along) // narrow
        return jnp.where(lax.broadcasted_iota(jnp.int32, shape, 1 - along) == group, 1.0, 0.0).astype(BF)

    rows, columns = chosen((n, replicas), 0), chosen((replicas, n), 1)
    same = lax.broadcasted_iota(jnp.int32, (n, n), 0) % narrow == lax.broadcasted_iota(jnp.int32, (n, n), 1) % narrow
    left = m_ref[...]
    for ref in (hi_ref, lo_ref):
        part = left.astype(BF)
        left = left - part.astype(F32)
        ref[...] = jnp.where(same, nn(nn(rows, part).astype(BF), columns), 0.0).astype(BF)


def spread_matrix(matrix):
    n = 16 * matrix.shape[0]
    return pl.pallas_call(
        spread_kernel,
        out_shape=[jax.ShapeDtypeStruct((n, n), BF)] * 2,
        in_specs=[VMEM],
        out_specs=[VMEM, VMEM],
        compiler_params=params(),
        cost_estimate=cost(2 * n * n * matrix.shape[0], 4 * n * n),
        name="spread",
    )(matrix)


def side_mix_kernel(place, m_ref, own, one, two, three, o_ref):
    groups, rows, width = own.shape
    replicas = Z * X
    z, x = place[0], place[1]
    n, k = 16 * groups, 16 * replicas

    def replica_of(group, sign):
        j, step = group // Z, group % Z
        return (z + 2 * Z + sign * WAY * step) % Z * X + (x + X - j) % X

    def chosen(shape, along, sign):
        group = lax.broadcasted_iota(jnp.int32, shape, along) // 16
        return jnp.where(lax.broadcasted_iota(jnp.int32, shape, 1 - along) == replica_of(group, sign), 1.0, 0.0).astype(BF)

    to, come = chosen((n, replicas), 0, 1), chosen((replicas, k), 1, -1)
    same = lax.broadcasted_iota(jnp.int32, (n, k), 0) % 16 == lax.broadcasted_iota(jnp.int32, (n, k), 1) % 16
    left = m_ref[...]
    spread = []
    for _ in range(2):
        part = left.astype(BF)
        left = left - part.astype(F32)
        spread.append(jnp.where(same, nn(nn(to, part).astype(BF), come), 0.0).astype(BF))
    for i in range(rows // 16):
        at = pl.ds(i * 16, 16)
        u = jnp.concatenate([ref[:, at, :].reshape(groups * 16, width) for ref in (own, one, two, three)], axis=0)
        mixed = nn(spread[0], u) + nn(spread[1], u)
        o_ref[:, at, :] = mixed.astype(BF).reshape(groups, 16, width)


def side_mix(place, matrix, pieces):
    shape = pieces[0].shape
    return pl.pallas_call(
        side_mix_kernel,
        out_shape=jax.ShapeDtypeStruct(shape, BF),
        in_specs=[SMEM] + [VMEM] * 5,
        out_specs=VMEM,
        compiler_params=params(),
        cost_estimate=cost(8 * Z * 512 * 16 * shape[1] * shape[2] // 16, 10 * pieces[0].size),
        name="side_mix",
    )(place, matrix, *pieces)


def shifted(shard, along_z, along_x):
    pairs = []
    for z in range(Z):
        for x in range(X):
            pairs.append((z * X + x, (z + along_z) % Z * X + (x + along_x) % X))
    return lax.ppermute(shard, "rep", pairs)


def first_round(v):
    return shifted(v[3:], 3 * WAY, 0), shifted(v[2], 2 * WAY, 0), shifted(v[1], WAY, 0)


def later_rounds(v, first):
    third, second, next_one = first
    fourth, fifth = shifted(third[1], WAY, 0), shifted(third[2], 2 * WAY, 0)
    sixth = shifted(third[3:], 3 * WAY, 0)
    seventh = shifted(sixth[1], WAY, 0)
    return jnp.stack([v[0], next_one, second, third[0], fourth, fifth, sixth[0], seventh])


LANDINGS = 6


def landed_kernel(u_ref, after_ref, o_ref, held, into, out_of):
    rows = u_ref.shape[0] // LANDINGS
    at = [pl.ds(i * rows, rows) for i in range(LANDINGS)]
    loads = [pltpu.make_async_copy(u_ref.at[at[i], :], held.at[at[i], :], into.at[i]) for i in range(LANDINGS)]
    stores = [pltpu.make_async_copy(held.at[at[i], :], o_ref.at[at[i], :], out_of.at[i]) for i in range(LANDINGS)]
    for load in loads:
        load.start()
    for load, store in zip(loads, stores):
        load.wait()
        store.start()
    for store in stores:
        store.wait()


def landed(array, after):
    return pl.pallas_call(
        landed_kernel,
        out_shape=pltpu.HBM(array.shape, BF),
        in_specs=[ANY, ANY],
        out_specs=HBM,
        scratch_shapes=[
            pltpu.VMEM(array.shape, BF),
            pltpu.SemaphoreType.DMA((LANDINGS,)),
            pltpu.SemaphoreType.DMA((LANDINGS,)),
        ],
        compiler_params=params(),
        cost_estimate=cost(0, 4 * array.size),
        name="landed",
    )(array, after)


def landed_both_kernel(place, u_ref, v_ref, o_ref, main, held, sems):
    rows = v_ref.shape[1]
    load = pltpu.make_async_copy(u_ref, main, sems.at[0])
    load.start()
    for step in range(Z):
        chunk = lax.rem(place[0] - WAY * step + Z, Z)
        held[pl.ds(pl.multiple_of(chunk * rows, 16), rows), MAIN:] = v_ref[step]
    load.wait()
    held[:, :MAIN] = main[...]
    store = pltpu.make_async_copy(held, o_ref, sems.at[1])
    store.start()
    store.wait()


def landed_both(place, array, side):
    h = array.shape[0]
    return pl.pallas_call(
        landed_both_kernel,
        out_shape=pltpu.HBM((h, D), BF),
        in_specs=[SMEM, ANY, VMEM],
        out_specs=HBM,
        scratch_shapes=[pltpu.VMEM(array.shape, BF), pltpu.VMEM((h, D), BF), pltpu.SemaphoreType.DMA((2,))],
        compiler_params=params(),
        cost_estimate=cost(0, 4 * h * D),
        name="landed_both",
    )(place, array, side)


def passed_along(shard):
    length = lax.axis_size("section")
    return lax.ppermute(shard, "section", [(i, i - 1) for i in range(1, length)])


def other_core(shard):
    return lax.ppermute(shard, "tp", [(0, 1), (1, 0)])


def sent_out(block):
    return lax.all_to_all(block, "rep", split_axis=0, concat_axis=0, tiled=True)


def shards(inputs, loss_grad, w_in, w_out, mixing):
    segments = lax.axis_size("section")
    segment_index = lax.axis_index("section")
    core = lax.axis_index("tp")
    replicas = lax.axis_size("rep")
    weight_in = w_in[0, 0]
    weight_out = w_out[0, 0]
    units = weight_in.shape[0]
    tokens = loss_grad.shape[0]
    own = tokens // 2

    core_at = jnp.reshape(core, (1,)).astype(jnp.int32)
    last = (segment_index == segments - 1).astype(jnp.int32)
    other_x = other_core(inputs[0])
    other_dy = other_core(loss_grad)
    late_in, late_out, other_x, other_dy = lax.optimization_barrier((weight_in, weight_out, other_x, other_dy))
    other_in = other_core(late_in)
    other_out = other_core(late_out)
    at = jnp.stack([core.astype(jnp.int32), last])
    x_rows, x_own, cot, act_t, slopes_t, own_slopes, own_in_t = opening(
        at, inputs[0], other_x, loss_grad, other_dy, weight_in
    )
    hi, lo = spread_matrix(mixing)

    columns = own // CHUNKS
    halves = [first_turn(at, c, cot, weight_out, own_in_t, slopes_t) for c in range(CHUNKS)]
    kept_cot = [[half[0] for half in halves]]
    kept_result = [[both_parts(half[0], half[1], other_core(half[2])) for half in halves]]
    cots = [passed_along(r) for r in kept_result[0]]

    other_in, other_out = kept(other_in, other_out)
    other_slopes, other_in_t = token_slopes(x_own, other_in)
    slopes, wouts, wins_t = (own_slopes, other_slopes), (weight_out, other_out), (own_in_t, other_in_t)
    for turn_index in range(1, segments - 1):
        results = [turn(cots[c], wouts, wins_t, slopes, c * columns, mixing) for c in range(CHUNKS)]
        kept_cot.append(cots)
        kept_result.append(results)
        cots = [passed_along(r) for r in results]
    kept_cot.append(cots)

    def summed(kept):
        parts = []
        for c in range(CHUNKS):
            total = kept[0][c]
            for t in range(1, segments):
                total = total + kept[t][c]
            parts.append(total)
        return parts

    mine = summed(kept_cot)
    all_cots = mine + [other_core(part) for part in mine]
    place_in_rep = lax.axis_index("rep")
    place = jnp.stack([place_in_rep // X, place_in_rep % X]).astype(jnp.int32)
    updated_in, side = update_in(core_at, place, all_cots, slopes_t, x_rows, weight_out, weight_in)
    pieces_in = sent_out(updated_in.reshape(replicas, units // replicas, MAIN))
    updated_out = update_out(core_at, all_cots, act_t, weight_out)
    side, updated_out = lax.optimization_barrier((side, updated_out))
    side_first = first_round(side)
    pieces_out = sent_out(updated_out.reshape(replicas, units // replicas, D))
    mixture_in = mix(hi, lo, pieces_in, mixing)
    *side_first, mixture_in = lax.optimization_barrier((*side_first, mixture_in))
    side = later_rounds(side, side_first)
    side = side_mix(place, mixing, [side] + [shifted(side, 0, j) for j in range(1, X)])
    back_in = sent_out(mixture_in)
    mixture_out = mix(hi, lo, pieces_out, mixture_in)
    side, mixture_out = lax.optimization_barrier((side, mixture_out))
    side_first = first_round(side)
    back_out = sent_out(mixture_out)
    kept_result.append([turn(cots[c], wouts, wins_t, slopes, c * columns, back_in) for c in range(CHUNKS)])
    *side_first, kept_result[-1][1] = lax.optimization_barrier((*side_first, kept_result[-1][1]))
    mixed_in = landed_both(place, back_in.reshape(units, MAIN), later_rounds(side, side_first))

    result = jnp.concatenate(summed(kept_result), axis=1)
    width = D // 2
    mine = lax.dynamic_slice_in_dim(result, core * width, width, 0)
    theirs = other_core(lax.dynamic_slice_in_dim(result, (1 - core) * width, width, 0))
    dx = leaving(core_at, mine, theirs)
    mixed_out = landed(back_out.reshape(units, D), dx[:16, :128])
    return dx[None], mixed_in[None, None], mixed_out[None, None]


def solution(mesh):
    in_specs = (
        P("section", "rep", "tp"),
        P("rep", "tp"),
        P("rep", "section", "tp", None),
        P("rep", "section", "tp", None),
        P(),
    )
    out_specs = (
        P("section", "rep", "tp"),
        P("rep", "section", "tp", None),
        P("rep", "section", "tp", None),
    )
    return jax.shard_map(shards, mesh=mesh, in_specs=in_specs, out_specs=out_specs, check_vma=False)
```

```python
import jax
import jax.numpy as jnp
from jax import lax
from jax.experimental import pallas as pl
from jax.experimental.pallas import tpu as pltpu
from jax.sharding import PartitionSpec as P

D = 768
FF = 3072
BF = jnp.bfloat16
F32 = jnp.float32

step_size = 4.0
root_half = 0.7071067811865476
inv_root_two_pi = 0.3989422804014327
in_scale = D ** (-0.5)
out_scale = FF ** (-0.5)

CHUNKS = 2
BLOCK = 512
MIB = 1024 * 1024
VMEM = pl.BlockSpec(memory_space=pltpu.VMEM)
HBM = pl.BlockSpec(memory_space=pltpu.HBM)
ANY = pl.BlockSpec(memory_space=pl.ANY)
SMEM = pl.BlockSpec(memory_space=pltpu.SMEM)


def params(mib=20):
    return pltpu.CompilerParams(vmem_limit_bytes=mib * MIB)


def cost(flops, nbytes, trans=0):
    return pl.CostEstimate(flops=flops, bytes_accessed=nbytes, transcendentals=trans)


def nt(left, right):
    return lax.dot_general(left, right, (((1,), (1,)), ((), ())), preferred_element_type=F32)


def nn(left, right):
    return lax.dot_general(left, right, (((1,), (0,)), ((), ())), preferred_element_type=F32)


def gelu_parts(preact):
    normal_cdf = 0.5 * (1.0 + lax.erf(preact * root_half))
    density = jnp.exp(-0.5 * preact * preact) * inv_root_two_pi
    return preact * normal_cdf, normal_cdf + preact * density


def blocks(h):
    return [pl.ds(i * BLOCK, BLOCK) for i in range(h // BLOCK)]


def joined(core, mine, theirs):
    return jnp.where(core == 0, jnp.concatenate([mine, theirs], axis=1), jnp.concatenate([theirs, mine], axis=1))


def opening_kernel(at, x_hbm, other_x_hbm, dy_hbm, other_dy_hbm, w_hbm, *refs):
    whole_ref, own_x_ref, cot_ref, a_ref, s_ref, own_s_ref, t_ref = refs[:7]
    x_ref, other_x_ref, dy_ref, other_dy_ref, w_ref, sems = refs[7:]
    core = at[0]
    own = own_x_ref.shape[0]
    parts = blocks(w_ref.shape[0])
    pairs = [(x_hbm, x_ref), (other_x_hbm, other_x_ref)]
    pairs += [(w_hbm.at[rows, :], w_ref.at[rows, :]) for rows in parts]
    pairs += [(dy_hbm, dy_ref), (other_dy_hbm, other_dy_ref)]
    copies = [pltpu.make_async_copy(*pair, sems.at[i]) for i, pair in enumerate(pairs)]
    for copy in copies:
        copy.start()
    for copy in copies[:2]:
        copy.wait()
    whole_ref[...] = joined(core, x_ref[...], other_x_ref[...])
    own_x_ref[...] = whole_ref[pl.ds(pl.multiple_of(core * own, own), own), :]
    x = whole_ref[...]
    for i, rows in enumerate(parts):
        copies[2 + i].wait()
        weight = w_ref[rows, :]
        values, slopes = gelu_parts(nt(weight, x) * in_scale)
        a_ref[rows, :] = values.astype(BF)
        s_ref[rows, :] = slopes
        own_s_ref[rows, :] = jnp.where(core == 0, slopes[:, :own], slopes[:, own:])
        t_ref[:, rows] = jnp.transpose(weight)
    for copy in copies[-2:]:
        copy.wait()
    dy = joined(core, dy_ref[...], other_dy_ref[...])
    cot_ref[...] = jnp.transpose(jnp.where(at[1] == 1, dy, jnp.zeros_like(dy)))


def opening(at, x, other_x, dy, other_dy, weight_in):
    m, h = dy.shape[0], weight_in.shape[0]
    own = m // 2
    shapes = [
        ((m, D), BF), ((own, D), BF), ((D, m), BF), ((h, m), BF), ((h, m), F32), ((h, own), F32), ((D, h), BF),
    ]
    return pl.pallas_call(
        opening_kernel,
        out_shape=[pltpu.VMEM(*s) for s in shapes],
        in_specs=[SMEM] + [ANY] * 5,
        out_specs=[VMEM] * len(shapes),
        scratch_shapes=[
            *[pltpu.VMEM(dy.shape, BF)] * 4,
            pltpu.VMEM((h, D), BF),
            pltpu.SemaphoreType.DMA((4 + h // BLOCK,)),
        ],
        compiler_params=params(46),
        cost_estimate=cost(2 * m * h * D, 6 * h * D + 8 * m * h, 2 * m * h),
        name="opening",
    )(at, x, other_x, dy, other_dy, weight_in)


def first_turn_kernel(chunk, m, at, c_ref, wo_ref, wt_ref, s_ref, cot_ref, mine_ref, theirs_ref, delta):
    own = c_ref.shape[1] // 2
    lanes = [pl.ds(pl.multiple_of(side * own + chunk * m, m), m) for side in (at[0], 1 - at[0])]
    cot = jnp.concatenate([c_ref[:, lane] for lane in lanes], axis=1)
    for at_rows in blocks(wo_ref.shape[0]):
        backward = nn(wo_ref[at_rows, :], cot) * out_scale
        slopes = jnp.concatenate([s_ref[at_rows, lane] for lane in lanes], axis=1)
        delta[at_rows, :] = (slopes * backward).astype(BF)
    partial = (nn(wt_ref[...], delta[...]) * in_scale).astype(BF)
    cot_ref[...] = cot[:, :m]
    mine_ref[...] = partial[:, :m]
    theirs_ref[...] = partial[:, m:]


def first_turn(at, chunk, cot, weight_out, weight_in_t, slopes):
    h, tokens = slopes.shape
    m = tokens // 2 // CHUNKS
    return pl.pallas_call(
        lambda *refs: first_turn_kernel(chunk, m, *refs),
        out_shape=[jax.ShapeDtypeStruct((D, m), BF)] * 3,
        in_specs=[SMEM] + [VMEM] * 4,
        out_specs=[VMEM] * 3,
        scratch_shapes=[pltpu.VMEM((h, 2 * m), BF)],
        compiler_params=params(),
        cost_estimate=cost(8 * m * h * D, 4 * h * D + 8 * m * h),
        name="first_turn",
    )(at, cot, weight_out, weight_in_t, slopes)


def both_parts_kernel(c_ref, mine_ref, theirs_ref, o_ref):
    branch = mine_ref[...].astype(F32) + theirs_ref[...].astype(F32)
    o_ref[...] = (c_ref[...].astype(F32) + branch).astype(BF)


def both_parts(cot, mine, theirs):
    return pl.pallas_call(
        both_parts_kernel,
        out_shape=jax.ShapeDtypeStruct(cot.shape, BF),
        in_specs=[VMEM] * 3,
        out_specs=VMEM,
        compiler_params=params(),
        cost_estimate=cost(0, 8 * cot.size),
        name="both_parts",
    )(cot, mine, theirs)


def token_slopes_kernel(x_ref, w_ref, s_ref, t_ref):
    x = x_ref[...]
    for at in blocks(w_ref.shape[0]):
        weight = w_ref[at, :]
        s_ref[at, :] = gelu_parts(nt(weight, x) * in_scale)[1]
        t_ref[:, at] = jnp.transpose(weight)


def token_slopes(x_rows, weight_in):
    m, h = x_rows.shape[0], weight_in.shape[0]
    return pl.pallas_call(
        token_slopes_kernel,
        out_shape=[jax.ShapeDtypeStruct((h, m), F32), jax.ShapeDtypeStruct((D, h), BF)],
        in_specs=[VMEM, VMEM],
        out_specs=[VMEM, VMEM],
        compiler_params=params(),
        cost_estimate=cost(2 * m * h * D, 4 * h * D + 4 * m * h, 2 * m * h),
        name="token_slopes",
    )(x_rows, weight_in)


def kept_kernel(*refs):
    count = len(refs) // 2
    sems = refs[-1]
    copies = [pltpu.make_async_copy(refs[i], refs[count + i], sems.at[i]) for i in range(count)]
    for copy in copies:
        copy.start()
    for copy in copies:
        copy.wait()


def kept(*arrays, mib=20):
    return pl.pallas_call(
        kept_kernel,
        out_shape=[pltpu.VMEM(array.shape, BF) for array in arrays],
        in_specs=[ANY] * len(arrays),
        out_specs=[VMEM] * len(arrays),
        scratch_shapes=[pltpu.SemaphoreType.DMA((len(arrays),))],
        compiler_params=params(mib),
        cost_estimate=cost(0, 4 * sum(array.size for array in arrays)),
        name="kept",
    )(*arrays)


def turn_kernel(col0, c_ref, wo0_ref, wo1_ref, wt0_ref, wt1_ref, s0_ref, s1_ref, after_ref, o_ref, delta):
    cot = c_ref[...]
    m = cot.shape[1]
    branch = None
    for wo_ref, wt_ref, s_ref in ((wo0_ref, wt0_ref, s0_ref), (wo1_ref, wt1_ref, s1_ref)):
        for at in blocks(wo_ref.shape[0]):
            backward = nn(wo_ref[at, :], cot) * out_scale
            delta[at, :] = (s_ref[at, pl.ds(col0, m)] * backward).astype(BF)
        partial = (nn(wt_ref[...], delta[...]) * in_scale).astype(BF).astype(F32)
        branch = partial if branch is None else branch + partial
    o_ref[...] = (cot.astype(F32) + branch).astype(BF)


def turn(cot, wouts, wins_t, slopes, col0, after):
    m = cot.shape[1]
    h = wouts[0].shape[0]
    return pl.pallas_call(
        lambda *refs: turn_kernel(col0, *refs),
        out_shape=jax.ShapeDtypeStruct((D, m), BF),
        in_specs=[VMEM] * 7 + [ANY],
        out_specs=VMEM,
        scratch_shapes=[pltpu.VMEM((h, m), BF)],
        compiler_params=params(),
        cost_estimate=cost(8 * m * h * D, 8 * h * D + 8 * m * h),
        name="turn",
    )(cot, wouts[0], wouts[1], wins_t[0], wins_t[1], slopes[0], slopes[1], after)


def leaving_kernel(core, mine_ref, theirs_ref, o_ref):
    own = mine_ref.shape[1]
    o_ref[pl.ds(pl.multiple_of(core[0] * own, own), own), :] = jnp.transpose(mine_ref[...])
    o_ref[pl.ds(pl.multiple_of((1 - core[0]) * own, own), own), :] = jnp.transpose(theirs_ref[...])


def leaving(core, mine, theirs):
    width, own = mine.shape
    return pl.pallas_call(
        leaving_kernel,
        out_shape=jax.ShapeDtypeStruct((2 * own, width), BF),
        in_specs=[SMEM, VMEM, VMEM],
        out_specs=VMEM,
        compiler_params=params(),
        cost_estimate=cost(0, 8 * own * width),
        name="leaving",
    )(core, mine, theirs)


def all_tokens(core, refs):
    mine, theirs = refs[:CHUNKS], refs[CHUNKS:]
    beside = lambda first, second: jnp.concatenate([ref[...] for ref in first + second], axis=1)
    return jnp.where(core == 0, beside(mine, theirs), beside(theirs, mine))


PARTS = 4


def update_kernel(core, *refs):
    a_ref, s_ref, x_ref, wo_ref, wi_ref, o_ref, scratch, sems = refs[2 * CHUNKS :]
    cot_t, x = all_tokens(core[0], refs[: 2 * CHUNKS]), x_ref[...]
    cot = jnp.transpose(cot_t)
    _, replicas, rows, _ = scratch.shape
    group = replicas // PARTS
    copies = []

    def finish(which, i, weight, grad):
        new = (weight.astype(F32) - step_size * grad).astype(BF)
        at = pl.ds(i * group, group)
        scratch[which, at] = new.reshape(group, rows, D)
        copies.append(pltpu.make_async_copy(scratch.at[which, at], o_ref.at[at, which], sems.at[which, i]))
        copies[-1].start()

    for i in range(PARTS):
        at = pl.ds(i * group * rows, group * rows)
        finish(1, i, wo_ref[at, :], nn(a_ref[at, :], cot) * out_scale)
        backward = nn(wo_ref[at, :], cot_t) * out_scale
        delta = (s_ref[at, :] * backward).astype(BF)
        finish(0, i, wi_ref[at, :], nn(delta, x) * in_scale)
    for copy in copies:
        copy.wait()


def update(replicas, core, cots, act_t, slopes_t, x_rows, weight_out, weight_in):
    h, m = slopes_t.shape
    rows = h // replicas
    return pl.pallas_call(
        update_kernel,
        out_shape=pltpu.HBM((replicas, 2, rows, D), BF),
        in_specs=[SMEM] + [VMEM] * (2 * CHUNKS + 5),
        out_specs=HBM,
        scratch_shapes=[pltpu.VMEM((2, replicas, rows, D), BF), pltpu.SemaphoreType.DMA((2, PARTS))],
        compiler_params=params(24),
        cost_estimate=cost(6 * m * h * D, 6 * m * h + 8 * h * D),
        name="update",
    )(core, *cots, act_t, slopes_t, x_rows, weight_out, weight_in)


def mix_kernel(m_ref, u_ref, o_ref):
    replicas, _, rows, width = u_ref.shape
    mixed = nn(m_ref[...], u_ref[...].reshape(replicas * rows, width))
    o_ref[...] = mixed.astype(BF).reshape(replicas, 1, rows, width)


def mix(spread, pieces):
    replicas, both, rows, width = pieces.shape
    block = 16
    n = spread.shape[0]
    piece = pl.BlockSpec((replicas, 1, block, width), lambda w, i: (0, w, i, 0))
    return pl.pallas_call(
        mix_kernel,
        grid=(both, rows // block),
        out_shape=pltpu.HBM(pieces.shape, BF),
        in_specs=[pl.BlockSpec((n, n), lambda w, i: (0, 0)), piece],
        out_specs=piece,
        compiler_params=params(),
        cost_estimate=cost(2 * n * n * width * both * rows // block, 4 * pieces.size + 2 * n * n),
        name="mix",
    )(spread, pieces)


def spread_kernel(m_ref, o_ref):
    n, replicas = o_ref.shape[0], m_ref.shape[0]
    narrow = n // replicas

    def chosen(shape, along):
        group = lax.broadcasted_iota(jnp.int32, shape, along) // narrow
        return jnp.where(lax.broadcasted_iota(jnp.int32, shape, 1 - along) == group, 1.0, 0.0).astype(BF)

    rows, columns = chosen((n, replicas), 0), chosen((replicas, n), 1)
    same = lax.broadcasted_iota(jnp.int32, (n, n), 0) % narrow == lax.broadcasted_iota(jnp.int32, (n, n), 1) % narrow
    spread = nn(nn(rows, m_ref[...].astype(BF)).astype(BF), columns)
    o_ref[...] = jnp.where(same, spread, 0.0).astype(BF)


def spread_matrix(matrix):
    n = 16 * matrix.shape[0]
    return pl.pallas_call(
        spread_kernel,
        out_shape=jax.ShapeDtypeStruct((n, n), BF),
        in_specs=[VMEM],
        out_specs=VMEM,
        compiler_params=params(),
        cost_estimate=cost(2 * n * n * matrix.shape[0], 4 * n * n),
        name="spread",
    )(matrix)


def landed_kernel(u_ref, after_ref, in_ref, out_ref, held, into, out_of):
    group = u_ref.shape[0] // PARTS
    loads, stores = [], []
    for which, o_ref in enumerate((in_ref, out_ref)):
        for i in range(PARTS):
            at = pl.ds(i * group, group)
            loads.append(pltpu.make_async_copy(u_ref.at[at, which], held.at[which, at], into.at[which, i]))
            stores.append(pltpu.make_async_copy(held.at[which, at], o_ref.at[at], out_of.at[which, i]))
    for load in loads:
        load.start()
    for load, store in zip(loads, stores):
        load.wait()
        store.start()
    for store in stores:
        store.wait()


def landed(array, after):
    replicas, both, rows, width = array.shape
    return pl.pallas_call(
        landed_kernel,
        out_shape=[pltpu.HBM((replicas, rows, width), BF)] * both,
        in_specs=[ANY, ANY],
        out_specs=[HBM] * both,
        scratch_shapes=[
            pltpu.VMEM((both, replicas, rows, width), BF),
            pltpu.SemaphoreType.DMA((both, PARTS)),
            pltpu.SemaphoreType.DMA((both, PARTS)),
        ],
        compiler_params=params(),
        cost_estimate=cost(0, 4 * array.size),
        name="landed",
    )(array, after)


def passed_along(shard):
    length = lax.axis_size("section")
    return lax.ppermute(shard, "section", [(i, i - 1) for i in range(1, length)])


def other_core(shard):
    return lax.ppermute(shard, "tp", [(0, 1), (1, 0)])


def sent_out(block):
    return lax.all_to_all(block, "rep", split_axis=0, concat_axis=0, tiled=True)


def shards(inputs, loss_grad, w_in, w_out, mixing):
    segments = lax.axis_size("section")
    segment_index = lax.axis_index("section")
    core = lax.axis_index("tp")
    replicas = lax.axis_size("rep")
    weight_in = w_in[0, 0]
    weight_out = w_out[0, 0]
    units = weight_in.shape[0]
    tokens = loss_grad.shape[0]
    own = tokens // 2

    core_at = jnp.reshape(core, (1,)).astype(jnp.int32)
    last = (segment_index == segments - 1).astype(jnp.int32)
    at = jnp.stack([core.astype(jnp.int32), last])
    other_x = other_core(inputs[0])
    other_dy = other_core(loss_grad)
    late_in, late_out, other_x, other_dy, at = lax.optimization_barrier(
        (weight_in, weight_out, other_x, other_dy, at)
    )
    other_in = other_core(late_in)
    other_out = other_core(late_out)
    x_rows, x_own, cot, act_t, slopes_t, own_slopes, own_in_t = opening(
        at, inputs[0], other_x, loss_grad, other_dy, weight_in
    )
    spread = spread_matrix(mixing)

    columns = own // CHUNKS
    halves = [first_turn(at, c, cot, weight_out, own_in_t, slopes_t) for c in range(CHUNKS)]
    kept_cot = [[half[0] for half in halves]]
    kept_result = [[both_parts(half[0], half[1], other_core(half[2])) for half in halves]]
    cots = [passed_along(r) for r in kept_result[0]]

    other_in, other_out = kept(other_in, other_out)
    other_slopes, other_in_t = token_slopes(x_own, other_in)
    slopes, wouts, wins_t = (own_slopes, other_slopes), (weight_out, other_out), (own_in_t, other_in_t)
    for turn_index in range(1, segments - 1):
        results = [turn(cots[c], wouts, wins_t, slopes, c * columns, mixing) for c in range(CHUNKS)]
        kept_cot.append(cots)
        kept_result.append(results)
        cots = [passed_along(r) for r in results]
    kept_cot.append(cots)

    def summed(kept):
        parts = []
        for c in range(CHUNKS):
            total = kept[0][c]
            for t in range(1, segments):
                total = total + kept[t][c]
            parts.append(total)
        return parts

    mine = summed(kept_cot)
    all_cots = mine + [other_core(part) for part in mine]
    updated = update(replicas, core_at, all_cots, act_t, slopes_t, x_rows, weight_out, weight_in)
    back = sent_out(mix(spread, sent_out(updated)))

    after = updated[0, 0, :16, :128]
    kept_result.append([turn(cots[c], wouts, wins_t, slopes, c * columns, after) for c in range(CHUNKS)])
    result = jnp.concatenate(summed(kept_result), axis=1)
    width = D // 2
    mine = lax.dynamic_slice_in_dim(result, core * width, width, 0)
    theirs = other_core(lax.dynamic_slice_in_dim(result, (1 - core) * width, width, 0))
    dx = leaving(core_at, mine, theirs)
    mixed_in, mixed_out = landed(back, dx[:16, :128])
    whole = (1, 1, units, D)
    return dx[None], mixed_in.reshape(whole), mixed_out.reshape(whole)


def solution(mesh):
    in_specs = (
        P("section", "rep", "tp"),
        P("rep", "tp"),
        P("rep", "section", "tp", None),
        P("rep", "section", "tp", None),
        P(),
    )
    out_specs = (
        P("section", "rep", "tp"),
        P("rep", "section", "tp", None),
        P("rep", "section", "tp", None),
    )
    return jax.shard_map(shards, mesh=mesh, in_specs=in_specs, out_specs=out_specs, check_vma=False)
```

```python
import jax
import jax.numpy as jnp
from jax import lax
from jax.experimental import pallas as pl
from jax.experimental.pallas import tpu as pltpu
from jax.sharding import PartitionSpec as P

D = 768
FF = 3072
BF = jnp.bfloat16
F32 = jnp.float32

step_size = 4.0
root_half = 0.7071067811865476
inv_root_two_pi = 0.3989422804014327
in_scale = D ** (-0.5)
out_scale = FF ** (-0.5)

CHUNKS = 2
BLOCK = 512
MIB = 1024 * 1024
VMEM = pl.BlockSpec(memory_space=pltpu.VMEM)
HBM = pl.BlockSpec(memory_space=pltpu.HBM)
ANY = pl.BlockSpec(memory_space=pl.ANY)


def params(mib=20):
    return pltpu.CompilerParams(vmem_limit_bytes=mib * MIB)


def cost(flops, nbytes, trans=0):
    return pl.CostEstimate(flops=flops, bytes_accessed=nbytes, transcendentals=trans)


def nt(left, right):
    return lax.dot_general(left, right, (((1,), (1,)), ((), ())), preferred_element_type=F32)


def nn(left, right):
    return lax.dot_general(left, right, (((1,), (0,)), ((), ())), preferred_element_type=F32)


def gelu_parts(preact):
    normal_cdf = 0.5 * (1.0 + lax.erf(preact * root_half))
    density = jnp.exp(-0.5 * preact * preact) * inv_root_two_pi
    return preact * normal_cdf, normal_cdf + preact * density


def blocks(h):
    return [pl.ds(i * BLOCK, BLOCK) for i in range(h // BLOCK)]


def joined(core, mine, theirs):
    return jnp.where(core == 0, jnp.concatenate([mine, theirs], axis=1), jnp.concatenate([theirs, mine], axis=1))


def opening_kernel(x_hbm, other_x_hbm, dy_hbm, other_dy_hbm, w_hbm, *refs):
    whole_ref, own_x_ref, cot_ref, a_ref, s_ref, own_s_ref, t_ref = refs[:7]
    x_ref, other_x_ref, dy_ref, other_dy_ref, w_ref, sems = refs[7:]
    core = lax.axis_index("tp")
    own = own_x_ref.shape[0]
    parts = blocks(w_ref.shape[0])
    pairs = [(x_hbm, x_ref), (other_x_hbm, other_x_ref)]
    pairs += [(w_hbm.at[rows, :], w_ref.at[rows, :]) for rows in parts]
    pairs += [(dy_hbm, dy_ref), (other_dy_hbm, other_dy_ref)]
    copies = [pltpu.make_async_copy(*pair, sems.at[i]) for i, pair in enumerate(pairs)]
    for copy in copies:
        copy.start()
    for copy in copies[:2]:
        copy.wait()
    whole_ref[...] = joined(core, x_ref[...], other_x_ref[...])
    own_x_ref[...] = whole_ref[pl.ds(pl.multiple_of(core * own, own), own), :]
    x = whole_ref[...]
    for i, rows in enumerate(parts):
        copies[2 + i].wait()
        weight = w_ref[rows, :]
        values, slopes = gelu_parts(nt(weight, x) * in_scale)
        a_ref[rows, :] = values.astype(BF)
        s_ref[rows, :] = slopes
        own_s_ref[rows, :] = jnp.where(core == 0, slopes[:, :own], slopes[:, own:])
        t_ref[:, rows] = jnp.transpose(weight)
    for copy in copies[-2:]:
        copy.wait()
    dy = joined(core, dy_ref[...], other_dy_ref[...])
    last = lax.axis_index("section") == lax.axis_size("section") - 1
    cot_ref[...] = jnp.transpose(jnp.where(last, dy, jnp.zeros_like(dy)))


def opening(x, other_x, dy, other_dy, weight_in):
    m, h = dy.shape[0], weight_in.shape[0]
    own = m // 2
    shapes = [
        ((m, D), BF), ((own, D), BF), ((D, m), BF), ((h, m), BF), ((h, m), F32), ((h, own), F32), ((D, h), BF),
    ]
    return pl.pallas_call(
        opening_kernel,
        out_shape=[pltpu.VMEM(*s) for s in shapes],
        in_specs=[ANY] * 5,
        out_specs=[VMEM] * len(shapes),
        scratch_shapes=[
            *[pltpu.VMEM(dy.shape, BF)] * 4,
            pltpu.VMEM((h, D), BF),
            pltpu.SemaphoreType.DMA((4 + h // BLOCK,)),
        ],
        compiler_params=params(46),
        cost_estimate=cost(2 * m * h * D, 6 * h * D + 8 * m * h, 2 * m * h),
        name="opening",
    )(x, other_x, dy, other_dy, weight_in)


def first_turn_kernel(chunk, m, c_ref, wo_ref, wt_ref, s_ref, cot_ref, mine_ref, theirs_ref, delta):
    own = c_ref.shape[1] // 2
    core = lax.axis_index("tp")
    lanes = [pl.ds(pl.multiple_of(side * own + chunk * m, m), m) for side in (core, 1 - core)]
    cot = jnp.concatenate([c_ref[:, lane] for lane in lanes], axis=1)
    for at_rows in blocks(wo_ref.shape[0]):
        backward = nn(wo_ref[at_rows, :], cot) * out_scale
        slopes = jnp.concatenate([s_ref[at_rows, lane] for lane in lanes], axis=1)
        delta[at_rows, :] = (slopes * backward).astype(BF)
    partial = (nn(wt_ref[...], delta[...]) * in_scale).astype(BF)
    cot_ref[...] = cot[:, :m]
    mine_ref[...] = partial[:, :m]
    theirs_ref[...] = partial[:, m:]


def first_turn(chunk, cot, weight_out, weight_in_t, slopes):
    h, tokens = slopes.shape
    m = tokens // 2 // CHUNKS
    return pl.pallas_call(
        lambda *refs: first_turn_kernel(chunk, m, *refs),
        out_shape=[jax.ShapeDtypeStruct((D, m), BF)] * 3,
        in_specs=[VMEM] * 4,
        out_specs=[VMEM] * 3,
        scratch_shapes=[pltpu.VMEM((h, 2 * m), BF)],
        compiler_params=params(),
        cost_estimate=cost(8 * m * h * D, 4 * h * D + 8 * m * h),
        name="first_turn",
    )(cot, weight_out, weight_in_t, slopes)


def both_parts_kernel(c_ref, mine_ref, theirs_ref, o_ref):
    branch = mine_ref[...].astype(F32) + theirs_ref[...].astype(F32)
    o_ref[...] = (c_ref[...].astype(F32) + branch).astype(BF)


def both_parts(cot, mine, theirs):
    return pl.pallas_call(
        both_parts_kernel,
        out_shape=jax.ShapeDtypeStruct(cot.shape, BF),
        in_specs=[VMEM] * 3,
        out_specs=VMEM,
        compiler_params=params(),
        cost_estimate=cost(0, 8 * cot.size),
        name="both_parts",
    )(cot, mine, theirs)


def token_slopes_kernel(x_ref, w_ref, s_ref, t_ref):
    x = x_ref[...]
    for at in blocks(w_ref.shape[0]):
        weight = w_ref[at, :]
        s_ref[at, :] = gelu_parts(nt(weight, x) * in_scale)[1]
        t_ref[:, at] = jnp.transpose(weight)


def token_slopes(x_rows, weight_in):
    m, h = x_rows.shape[0], weight_in.shape[0]
    return pl.pallas_call(
        token_slopes_kernel,
        out_shape=[jax.ShapeDtypeStruct((h, m), F32), jax.ShapeDtypeStruct((D, h), BF)],
        in_specs=[VMEM, VMEM],
        out_specs=[VMEM, VMEM],
        compiler_params=params(),
        cost_estimate=cost(2 * m * h * D, 4 * h * D + 4 * m * h, 2 * m * h),
        name="token_slopes",
    )(x_rows, weight_in)


def kept_kernel(*refs):
    count = len(refs) // 2
    sems = refs[-1]
    copies = [pltpu.make_async_copy(refs[i], refs[count + i], sems.at[i]) for i in range(count)]
    for copy in copies:
        copy.start()
    for copy in copies:
        copy.wait()


def kept(*arrays, mib=20):
    return pl.pallas_call(
        kept_kernel,
        out_shape=[pltpu.VMEM(array.shape, BF) for array in arrays],
        in_specs=[ANY] * len(arrays),
        out_specs=[VMEM] * len(arrays),
        scratch_shapes=[pltpu.SemaphoreType.DMA((len(arrays),))],
        compiler_params=params(mib),
        cost_estimate=cost(0, 4 * sum(array.size for array in arrays)),
        name="kept",
    )(*arrays)


def turn_kernel(col0, c_ref, wo0_ref, wo1_ref, wt0_ref, wt1_ref, s0_ref, s1_ref, after_ref, o_ref, delta):
    cot = c_ref[...]
    m = cot.shape[1]
    branch = None
    for wo_ref, wt_ref, s_ref in ((wo0_ref, wt0_ref, s0_ref), (wo1_ref, wt1_ref, s1_ref)):
        for at in blocks(wo_ref.shape[0]):
            backward = nn(wo_ref[at, :], cot) * out_scale
            delta[at, :] = (s_ref[at, pl.ds(col0, m)] * backward).astype(BF)
        partial = (nn(wt_ref[...], delta[...]) * in_scale).astype(BF).astype(F32)
        branch = partial if branch is None else branch + partial
    o_ref[...] = (cot.astype(F32) + branch).astype(BF)


def turn(cot, wouts, wins_t, slopes, col0, after):
    m = cot.shape[1]
    h = wouts[0].shape[0]
    return pl.pallas_call(
        lambda *refs: turn_kernel(col0, *refs),
        out_shape=jax.ShapeDtypeStruct((D, m), BF),
        in_specs=[VMEM] * 7 + [ANY],
        out_specs=VMEM,
        scratch_shapes=[pltpu.VMEM((h, m), BF)],
        compiler_params=params(),
        cost_estimate=cost(8 * m * h * D, 8 * h * D + 8 * m * h),
        name="turn",
    )(cot, wouts[0], wouts[1], wins_t[0], wins_t[1], slopes[0], slopes[1], after)


def leaving_kernel(mine_ref, theirs_ref, o_ref):
    core = lax.axis_index("tp")
    own = mine_ref.shape[1]
    o_ref[pl.ds(pl.multiple_of(core * own, own), own), :] = jnp.transpose(mine_ref[...])
    o_ref[pl.ds(pl.multiple_of((1 - core) * own, own), own), :] = jnp.transpose(theirs_ref[...])


def leaving(mine, theirs):
    width, own = mine.shape
    return pl.pallas_call(
        leaving_kernel,
        out_shape=jax.ShapeDtypeStruct((2 * own, width), BF),
        in_specs=[VMEM, VMEM],
        out_specs=VMEM,
        compiler_params=params(),
        cost_estimate=cost(0, 8 * own * width),
        name="leaving",
    )(mine, theirs)


def all_tokens(core, refs):
    mine, theirs = refs[:CHUNKS], refs[CHUNKS:]
    beside = lambda first, second: jnp.concatenate([ref[...] for ref in first + second], axis=1)
    return jnp.where(core == 0, beside(mine, theirs), beside(theirs, mine))


PARTS = 4


def update_kernel(*refs):
    a_ref, s_ref, x_ref, wo_ref, wi_ref, o_ref, scratch, sems = refs[2 * CHUNKS :]
    cot_t, x = all_tokens(lax.axis_index("tp"), refs[: 2 * CHUNKS]), x_ref[...]
    cot = jnp.transpose(cot_t)
    _, replicas, rows, _ = scratch.shape
    group = replicas // PARTS
    copies = []

    def finish(which, i, weight, grad):
        new = (weight.astype(F32) - step_size * grad).astype(BF)
        at = pl.ds(i * group, group)
        scratch[which, at] = new.reshape(group, rows, D)
        copies.append(pltpu.make_async_copy(scratch.at[which, at], o_ref.at[at, which], sems.at[which, i]))
        copies[-1].start()

    for i in range(PARTS):
        at = pl.ds(i * group * rows, group * rows)
        finish(1, i, wo_ref[at, :], nn(a_ref[at, :], cot) * out_scale)
        backward = nn(wo_ref[at, :], cot_t) * out_scale
        delta = (s_ref[at, :] * backward).astype(BF)
        finish(0, i, wi_ref[at, :], nn(delta, x) * in_scale)
    for copy in copies:
        copy.wait()


def update(replicas, cots, act_t, slopes_t, x_rows, weight_out, weight_in):
    h, m = slopes_t.shape
    rows = h // replicas
    return pl.pallas_call(
        update_kernel,
        out_shape=pltpu.HBM((replicas, 2, rows, D), BF),
        in_specs=[VMEM] * (2 * CHUNKS + 5),
        out_specs=HBM,
        scratch_shapes=[pltpu.VMEM((2, replicas, rows, D), BF), pltpu.SemaphoreType.DMA((2, PARTS))],
        compiler_params=params(24),
        cost_estimate=cost(6 * m * h * D, 6 * m * h + 8 * h * D),
        name="update",
    )(*cots, act_t, slopes_t, x_rows, weight_out, weight_in)


def mix_kernel(m_ref, u_ref, o_ref, loaded, stored, into, out_of):
    both, parts, replicas, rows, width = loaded.shape
    order = [(which, i) for which in range(both) for i in range(parts)]
    piece = lambda ref, which, i: ref.at[:, which, pl.ds(i * rows, rows), :]
    loads = [pltpu.make_async_copy(piece(u_ref, *at), loaded.at[at], into.at[at]) for at in order]
    stores = [pltpu.make_async_copy(stored.at[at], piece(o_ref, *at), out_of.at[at]) for at in order]
    for load in loads:
        load.start()
    for at, load, store in zip(order, loads, stores):
        load.wait()
        mixed = nn(m_ref[...], loaded[at].reshape(replicas * rows, width))
        stored[at] = mixed.astype(BF).reshape(replicas, rows, width)
        store.start()
    for store in stores:
        store.wait()


def mix(spread, pieces):
    replicas, both, rows, width = pieces.shape
    block = 16
    parts = rows // block
    n = spread.shape[0]
    return pl.pallas_call(
        mix_kernel,
        out_shape=pltpu.HBM(pieces.shape, BF),
        in_specs=[VMEM, ANY],
        out_specs=HBM,
        scratch_shapes=[pltpu.VMEM((both, parts, replicas, block, width), BF)] * 2
        + [pltpu.SemaphoreType.DMA((both, parts))] * 2,
        compiler_params=params(),
        cost_estimate=cost(2 * n * n * width * both * parts, 4 * pieces.size + 2 * n * n),
        name="mix",
    )(spread, pieces)


def spread_kernel(m_ref, o_ref):
    n, replicas = o_ref.shape[0], m_ref.shape[0]
    narrow = n // replicas

    def chosen(shape, along):
        group = lax.broadcasted_iota(jnp.int32, shape, along) // narrow
        return jnp.where(lax.broadcasted_iota(jnp.int32, shape, 1 - along) == group, 1.0, 0.0).astype(BF)

    rows, columns = chosen((n, replicas), 0), chosen((replicas, n), 1)
    same = lax.broadcasted_iota(jnp.int32, (n, n), 0) % narrow == lax.broadcasted_iota(jnp.int32, (n, n), 1) % narrow
    spread = nn(nn(rows, m_ref[...].astype(BF)).astype(BF), columns)
    o_ref[...] = jnp.where(same, spread, 0.0).astype(BF)


def spread_matrix(matrix):
    n = 16 * matrix.shape[0]
    return pl.pallas_call(
        spread_kernel,
        out_shape=jax.ShapeDtypeStruct((n, n), BF),
        in_specs=[VMEM],
        out_specs=VMEM,
        compiler_params=params(),
        cost_estimate=cost(2 * n * n * matrix.shape[0], 4 * n * n),
        name="spread",
    )(matrix)


def landed_kernel(u_ref, after_ref, in_ref, out_ref, held, into, out_of):
    group = u_ref.shape[0] // PARTS
    loads, stores = [], []
    for which, o_ref in enumerate((in_ref, out_ref)):
        for i in range(PARTS):
            at = pl.ds(i * group, group)
            loads.append(pltpu.make_async_copy(u_ref.at[at, which], held.at[which, at], into.at[which, i]))
            stores.append(pltpu.make_async_copy(held.at[which, at], o_ref.at[at], out_of.at[which, i]))
    for load in loads:
        load.start()
    for load, store in zip(loads, stores):
        load.wait()
        store.start()
    for store in stores:
        store.wait()


def landed(array, after):
    replicas, both, rows, width = array.shape
    return pl.pallas_call(
        landed_kernel,
        out_shape=[pltpu.HBM((replicas, rows, width), BF)] * both,
        in_specs=[ANY, ANY],
        out_specs=[HBM] * both,
        scratch_shapes=[
            pltpu.VMEM((both, replicas, rows, width), BF),
            pltpu.SemaphoreType.DMA((both, PARTS)),
            pltpu.SemaphoreType.DMA((both, PARTS)),
        ],
        compiler_params=params(),
        cost_estimate=cost(0, 4 * array.size),
        name="landed",
    )(array, after)


def passed_along(shard):
    length = lax.axis_size("section")
    return lax.ppermute(shard, "section", [(i, i - 1) for i in range(1, length)])


def other_core(shard):
    return lax.ppermute(shard, "tp", [(0, 1), (1, 0)])


def sent_out(block):
    return lax.all_to_all(block, "rep", split_axis=0, concat_axis=0, tiled=True)


def shards(inputs, loss_grad, w_in, w_out, mixing):
    segments = lax.axis_size("section")
    core = lax.axis_index("tp")
    replicas = lax.axis_size("rep")
    weight_in = w_in[0, 0]
    weight_out = w_out[0, 0]
    units = weight_in.shape[0]
    tokens = loss_grad.shape[0]
    own = tokens // 2

    other_x = other_core(inputs[0])
    other_dy = other_core(loss_grad)
    late_in, late_out, other_x, other_dy = lax.optimization_barrier((weight_in, weight_out, other_x, other_dy))
    other_in = other_core(late_in)
    other_out = other_core(late_out)
    x_rows, x_own, cot, act_t, slopes_t, own_slopes, own_in_t = opening(
        inputs[0], other_x, loss_grad, other_dy, weight_in
    )
    spread = spread_matrix(mixing)

    columns = own // CHUNKS
    halves = [first_turn(c, cot, weight_out, own_in_t, slopes_t) for c in range(CHUNKS)]
    kept_cot = [[half[0] for half in halves]]
    kept_result = [[both_parts(half[0], half[1], other_core(half[2])) for half in halves]]
    cots = [passed_along(r) for r in kept_result[0]]

    other_in, other_out = kept(other_in, other_out)
    other_slopes, other_in_t = token_slopes(x_own, other_in)
    slopes, wouts, wins_t = (own_slopes, other_slopes), (weight_out, other_out), (own_in_t, other_in_t)
    for turn_index in range(1, segments - 1):
        results = [turn(cots[c], wouts, wins_t, slopes, c * columns, mixing) for c in range(CHUNKS)]
        kept_cot.append(cots)
        kept_result.append(results)
        cots = [passed_along(r) for r in results]
    kept_cot.append(cots)

    def summed(kept):
        parts = []
        for c in range(CHUNKS):
            total = kept[0][c]
            for t in range(1, segments):
                total = total + kept[t][c]
            parts.append(total)
        return parts

    mine = summed(kept_cot)
    all_cots = mine + [other_core(part) for part in mine]
    updated = update(replicas, all_cots, act_t, slopes_t, x_rows, weight_out, weight_in)
    back = sent_out(mix(spread, sent_out(updated)))

    after = updated[0, 0, :16, :128]
    kept_result.append([turn(cots[c], wouts, wins_t, slopes, c * columns, after) for c in range(CHUNKS)])
    result = jnp.concatenate(summed(kept_result), axis=1)
    width = D // 2
    mine = lax.dynamic_slice_in_dim(result, core * width, width, 0)
    theirs = other_core(lax.dynamic_slice_in_dim(result, (1 - core) * width, width, 0))
    dx = leaving(mine, theirs)
    mixed_in, mixed_out = landed(back, dx[:16, :128])
    whole = (1, 1, units, D)
    return dx[None], mixed_in.reshape(whole), mixed_out.reshape(whole)


def solution(mesh):
    in_specs = (
        P("section", "rep", "tp"),
        P("rep", "tp"),
        P("rep", "section", "tp", None),
        P("rep", "section", "tp", None),
        P(),
    )
    out_specs = (
        P("section", "rep", "tp"),
        P("rep", "section", "tp", None),
        P("rep", "section", "tp", None),
    )
    return jax.shard_map(shards, mesh=mesh, in_specs=in_specs, out_specs=out_specs, check_vma=False)
```

```python
import jax
import jax.numpy as jnp
from jax import lax
from jax.experimental import pallas as pl
from jax.experimental.pallas import tpu as pltpu
from jax.sharding import PartitionSpec as P

D = 768
FF = 3072
BF = jnp.bfloat16
F32 = jnp.float32

step_size = 4.0
root_half = 0.7071067811865476
inv_root_two_pi = 0.3989422804014327
in_scale = D ** (-0.5)
out_scale = FF ** (-0.5)

CHUNKS = 2
BLOCK = 512
MIB = 1024 * 1024
VMEM = pl.BlockSpec(memory_space=pltpu.VMEM)
HBM = pl.BlockSpec(memory_space=pltpu.HBM)
ANY = pl.BlockSpec(memory_space=pl.ANY)


def params(mib=20):
    return pltpu.CompilerParams(vmem_limit_bytes=mib * MIB)


def cost(flops, nbytes, trans=0):
    return pl.CostEstimate(flops=flops, bytes_accessed=nbytes, transcendentals=trans)


def nt(left, right):
    return lax.dot_general(left, right, (((1,), (1,)), ((), ())), preferred_element_type=F32)


def nn(left, right):
    return lax.dot_general(left, right, (((1,), (0,)), ((), ())), preferred_element_type=F32)


def gelu_parts(preact):
    normal_cdf = 0.5 * (1.0 + lax.erf(preact * root_half))
    density = jnp.exp(-0.5 * preact * preact) * inv_root_two_pi
    return preact * normal_cdf, normal_cdf + preact * density


def blocks(h):
    return [pl.ds(i * BLOCK, BLOCK) for i in range(h // BLOCK)]


def joined(core, mine, theirs):
    return jnp.where(core == 0, jnp.concatenate([mine, theirs], axis=1), jnp.concatenate([theirs, mine], axis=1))


def opening_kernel(x_hbm, other_x_hbm, dy_hbm, other_dy_hbm, w_hbm, *refs):
    whole_ref, own_x_ref, cot_ref, a_ref, s_ref, own_s_ref, t_ref = refs[:7]
    x_ref, other_x_ref, dy_ref, other_dy_ref, w_ref, sems = refs[7:]
    core = lax.axis_index("tp")
    own = own_x_ref.shape[0]
    parts = blocks(w_ref.shape[0])
    pairs = [(x_hbm, x_ref), (other_x_hbm, other_x_ref)]
    pairs += [(w_hbm.at[rows, :], w_ref.at[rows, :]) for rows in parts]
    pairs += [(dy_hbm, dy_ref), (other_dy_hbm, other_dy_ref)]
    copies = [pltpu.make_async_copy(*pair, sems.at[i]) for i, pair in enumerate(pairs)]
    for copy in copies:
        copy.start()
    for copy in copies[:2]:
        copy.wait()
    whole_ref[...] = joined(core, x_ref[...], other_x_ref[...])
    own_x_ref[...] = whole_ref[pl.ds(pl.multiple_of(core * own, own), own), :]
    x = whole_ref[...]
    for i, rows in enumerate(parts):
        copies[2 + i].wait()
        weight = w_ref[rows, :]
        values, slopes = gelu_parts(nt(weight, x) * in_scale)
        a_ref[rows, :] = values.astype(BF)
        s_ref[rows, :] = slopes
        own_s_ref[rows, :] = jnp.where(core == 0, slopes[:, :own], slopes[:, own:])
        t_ref[:, rows] = jnp.transpose(weight)
    for copy in copies[-2:]:
        copy.wait()
    dy = joined(core, dy_ref[...], other_dy_ref[...])
    last = lax.axis_index("section") == lax.axis_size("section") - 1
    cot_ref[...] = jnp.transpose(jnp.where(last, dy, jnp.zeros_like(dy)))


def opening(x, other_x, dy, other_dy, weight_in):
    m, h = dy.shape[0], weight_in.shape[0]
    own = m // 2
    shapes = [
        ((m, D), BF), ((own, D), BF), ((D, m), BF), ((h, m), BF), ((h, m), F32), ((h, own), F32), ((D, h), BF),
    ]
    return pl.pallas_call(
        opening_kernel,
        out_shape=[pltpu.VMEM(*s) for s in shapes],
        in_specs=[ANY] * 5,
        out_specs=[VMEM] * len(shapes),
        scratch_shapes=[
            *[pltpu.VMEM(dy.shape, BF)] * 4,
            pltpu.VMEM((h, D), BF),
            pltpu.SemaphoreType.DMA((4 + h // BLOCK,)),
        ],
        compiler_params=params(46),
        cost_estimate=cost(2 * m * h * D, 6 * h * D + 8 * m * h, 2 * m * h),
        name="opening",
    )(x, other_x, dy, other_dy, weight_in)


def first_turn_kernel(chunk, m, c_ref, wo_ref, wt_ref, s_ref, cot_ref, mine_ref, theirs_ref, delta):
    own = c_ref.shape[1] // 2
    core = lax.axis_index("tp")
    lanes = [pl.ds(pl.multiple_of(side * own + chunk * m, m), m) for side in (core, 1 - core)]
    cot = jnp.concatenate([c_ref[:, lane] for lane in lanes], axis=1)
    for at_rows in blocks(wo_ref.shape[0]):
        backward = nn(wo_ref[at_rows, :], cot) * out_scale
        slopes = jnp.concatenate([s_ref[at_rows, lane] for lane in lanes], axis=1)
        delta[at_rows, :] = (slopes * backward).astype(BF)
    partial = (nn(wt_ref[...], delta[...]) * in_scale).astype(BF)
    cot_ref[...] = cot[:, :m]
    mine_ref[...] = partial[:, :m]
    theirs_ref[...] = partial[:, m:]


def first_turn(chunk, cot, weight_out, weight_in_t, slopes):
    h, tokens = slopes.shape
    m = tokens // 2 // CHUNKS
    return pl.pallas_call(
        lambda *refs: first_turn_kernel(chunk, m, *refs),
        out_shape=[jax.ShapeDtypeStruct((D, m), BF)] * 3,
        in_specs=[VMEM] * 4,
        out_specs=[VMEM] * 3,
        scratch_shapes=[pltpu.VMEM((h, 2 * m), BF)],
        compiler_params=params(),
        cost_estimate=cost(8 * m * h * D, 4 * h * D + 8 * m * h),
        name="first_turn",
    )(cot, weight_out, weight_in_t, slopes)


def both_parts_kernel(c_ref, mine_ref, theirs_ref, o_ref):
    branch = mine_ref[...].astype(F32) + theirs_ref[...].astype(F32)
    o_ref[...] = (c_ref[...].astype(F32) + branch).astype(BF)


def both_parts(cot, mine, theirs):
    return pl.pallas_call(
        both_parts_kernel,
        out_shape=jax.ShapeDtypeStruct(cot.shape, BF),
        in_specs=[VMEM] * 3,
        out_specs=VMEM,
        compiler_params=params(),
        cost_estimate=cost(0, 8 * cot.size),
        name="both_parts",
    )(cot, mine, theirs)


def token_slopes_kernel(x_ref, w_ref, s_ref, t_ref):
    x = x_ref[...]
    for at in blocks(w_ref.shape[0]):
        weight = w_ref[at, :]
        s_ref[at, :] = gelu_parts(nt(weight, x) * in_scale)[1]
        t_ref[:, at] = jnp.transpose(weight)


def token_slopes(x_rows, weight_in):
    m, h = x_rows.shape[0], weight_in.shape[0]
    return pl.pallas_call(
        token_slopes_kernel,
        out_shape=[jax.ShapeDtypeStruct((h, m), F32), jax.ShapeDtypeStruct((D, h), BF)],
        in_specs=[VMEM, VMEM],
        out_specs=[VMEM, VMEM],
        compiler_params=params(),
        cost_estimate=cost(2 * m * h * D, 4 * h * D + 4 * m * h, 2 * m * h),
        name="token_slopes",
    )(x_rows, weight_in)


def kept_kernel(*refs):
    count = len(refs) // 2
    sems = refs[-1]
    copies = [pltpu.make_async_copy(refs[i], refs[count + i], sems.at[i]) for i in range(count)]
    for copy in copies:
        copy.start()
    for copy in copies:
        copy.wait()


def kept(*arrays, mib=20):
    return pl.pallas_call(
        kept_kernel,
        out_shape=[pltpu.VMEM(array.shape, BF) for array in arrays],
        in_specs=[ANY] * len(arrays),
        out_specs=[VMEM] * len(arrays),
        scratch_shapes=[pltpu.SemaphoreType.DMA((len(arrays),))],
        compiler_params=params(mib),
        cost_estimate=cost(0, 4 * sum(array.size for array in arrays)),
        name="kept",
    )(*arrays)


def turn_kernel(col0, c_ref, wo0_ref, wo1_ref, wt0_ref, wt1_ref, s0_ref, s1_ref, after_ref, o_ref, delta):
    cot = c_ref[...]
    m = cot.shape[1]
    branch = None
    for wo_ref, wt_ref, s_ref in ((wo0_ref, wt0_ref, s0_ref), (wo1_ref, wt1_ref, s1_ref)):
        for at in blocks(wo_ref.shape[0]):
            backward = nn(wo_ref[at, :], cot) * out_scale
            delta[at, :] = (s_ref[at, pl.ds(col0, m)] * backward).astype(BF)
        partial = (nn(wt_ref[...], delta[...]) * in_scale).astype(BF).astype(F32)
        branch = partial if branch is None else branch + partial
    o_ref[...] = (cot.astype(F32) + branch).astype(BF)


def turn(cot, wouts, wins_t, slopes, col0, after):
    m = cot.shape[1]
    h = wouts[0].shape[0]
    return pl.pallas_call(
        lambda *refs: turn_kernel(col0, *refs),
        out_shape=jax.ShapeDtypeStruct((D, m), BF),
        in_specs=[VMEM] * 7 + [ANY],
        out_specs=VMEM,
        scratch_shapes=[pltpu.VMEM((h, m), BF)],
        compiler_params=params(),
        cost_estimate=cost(8 * m * h * D, 8 * h * D + 8 * m * h),
        name="turn",
    )(cot, wouts[0], wouts[1], wins_t[0], wins_t[1], slopes[0], slopes[1], after)


def leaving_kernel(mine_ref, theirs_ref, o_ref):
    core = lax.axis_index("tp")
    own = mine_ref.shape[1]
    o_ref[pl.ds(pl.multiple_of(core * own, own), own), :] = jnp.transpose(mine_ref[...])
    o_ref[pl.ds(pl.multiple_of((1 - core) * own, own), own), :] = jnp.transpose(theirs_ref[...])


def leaving(mine, theirs):
    width, own = mine.shape
    return pl.pallas_call(
        leaving_kernel,
        out_shape=jax.ShapeDtypeStruct((2 * own, width), BF),
        in_specs=[VMEM, VMEM],
        out_specs=VMEM,
        compiler_params=params(),
        cost_estimate=cost(0, 8 * own * width),
        name="leaving",
    )(mine, theirs)


def all_tokens(core, refs):
    mine, theirs = refs[:CHUNKS], refs[CHUNKS:]
    beside = lambda first, second: jnp.concatenate([ref[...] for ref in first + second], axis=1)
    return jnp.where(core == 0, beside(mine, theirs), beside(theirs, mine))


PARTS = 4


def update_kernel(*refs):
    a_ref, s_ref, x_ref, wo_ref, wi_ref, o_ref, scratch, sems = refs[2 * CHUNKS :]
    cot_t, x = all_tokens(lax.axis_index("tp"), refs[: 2 * CHUNKS]), x_ref[...]
    cot = jnp.transpose(cot_t)
    _, replicas, rows, _ = scratch.shape
    group = replicas // PARTS
    copies = []

    def finish(which, i, weight, grad):
        new = (weight.astype(F32) - step_size * grad).astype(BF)
        at = pl.ds(i * group, group)
        scratch[which, at] = new.reshape(group, rows, D)
        copies.append(pltpu.make_async_copy(scratch.at[which, at], o_ref.at[at, which], sems.at[which, i]))
        copies[-1].start()

    for i in range(PARTS):
        at = pl.ds(i * group * rows, group * rows)
        finish(1, i, wo_ref[at, :], nn(a_ref[at, :], cot) * out_scale)
        backward = nn(wo_ref[at, :], cot_t) * out_scale
        delta = (s_ref[at, :] * backward).astype(BF)
        finish(0, i, wi_ref[at, :], nn(delta, x) * in_scale)
    for copy in copies:
        copy.wait()


def update(replicas, cots, act_t, slopes_t, x_rows, weight_out, weight_in):
    h, m = slopes_t.shape
    rows = h // replicas
    return pl.pallas_call(
        update_kernel,
        out_shape=pltpu.HBM((replicas, 2, rows, D), BF),
        in_specs=[VMEM] * (2 * CHUNKS + 5),
        out_specs=HBM,
        scratch_shapes=[pltpu.VMEM((2, replicas, rows, D), BF), pltpu.SemaphoreType.DMA((2, PARTS))],
        compiler_params=params(24),
        cost_estimate=cost(6 * m * h * D, 6 * m * h + 8 * h * D),
        name="update",
    )(*cots, act_t, slopes_t, x_rows, weight_out, weight_in)


def mix_kernel(m_ref, u_ref, o_ref, loaded, stored, into, out_of):
    both, parts, replicas, rows, width = loaded.shape
    order = [(which, i) for which in range(both) for i in range(parts)]
    piece = lambda ref, which, i: ref.at[:, which, pl.ds(i * rows, rows), :]
    loads = [pltpu.make_async_copy(piece(u_ref, *at), loaded.at[at], into.at[at]) for at in order]
    stores = [pltpu.make_async_copy(stored.at[at], piece(o_ref, *at), out_of.at[at]) for at in order]
    for load in loads:
        load.start()
    for at, load, store in zip(order, loads, stores):
        load.wait()
        mixed = nn(m_ref[...], loaded[at].reshape(replicas * rows, width))
        stored[at] = mixed.astype(BF).reshape(replicas, rows, width)
        store.start()
    for store in stores:
        store.wait()


def mix(spread, pieces):
    replicas, both, rows, width = pieces.shape
    block = 16
    parts = rows // block
    n = spread.shape[0]
    return pl.pallas_call(
        mix_kernel,
        out_shape=pltpu.HBM(pieces.shape, BF),
        in_specs=[VMEM, ANY],
        out_specs=HBM,
        scratch_shapes=[pltpu.VMEM((both, parts, replicas, block, width), BF)] * 2
        + [pltpu.SemaphoreType.DMA((both, parts))] * 2,
        compiler_params=params(),
        cost_estimate=cost(2 * n * n * width * both * parts, 4 * pieces.size + 2 * n * n),
        name="mix",
    )(spread, pieces)


def spread_kernel(m_ref, o_ref):
    n, replicas = o_ref.shape[0], m_ref.shape[0]
    narrow = n // replicas

    def chosen(shape, along):
        group = lax.broadcasted_iota(jnp.int32, shape, along) // narrow
        return jnp.where(lax.broadcasted_iota(jnp.int32, shape, 1 - along) == group, 1.0, 0.0).astype(BF)

    rows, columns = chosen((n, replicas), 0), chosen((replicas, n), 1)
    same = lax.broadcasted_iota(jnp.int32, (n, n), 0) % narrow == lax.broadcasted_iota(jnp.int32, (n, n), 1) % narrow
    spread = nn(nn(rows, m_ref[...].astype(BF)).astype(BF), columns)
    o_ref[...] = jnp.where(same, spread, 0.0).astype(BF)


def spread_matrix(matrix):
    n = 16 * matrix.shape[0]
    return pl.pallas_call(
        spread_kernel,
        out_shape=jax.ShapeDtypeStruct((n, n), BF),
        in_specs=[VMEM],
        out_specs=VMEM,
        compiler_params=params(),
        cost_estimate=cost(2 * n * n * matrix.shape[0], 4 * n * n),
        name="spread",
    )(matrix)


def landed_kernel(u_ref, after_ref, in_ref, out_ref, held, into, out_of):
    group = u_ref.shape[0] // PARTS
    loads, stores = [], []
    for which, o_ref in enumerate((in_ref, out_ref)):
        for i in range(PARTS):
            at = pl.ds(i * group, group)
            loads.append(pltpu.make_async_copy(u_ref.at[at, which], held.at[which, at], into.at[which, i]))
            stores.append(pltpu.make_async_copy(held.at[which, at], o_ref.at[at], out_of.at[which, i]))
    for load in loads:
        load.start()
    for load, store in zip(loads, stores):
        load.wait()
        store.start()
    for store in stores:
        store.wait()


def landed(array, after):
    replicas, both, rows, width = array.shape
    return pl.pallas_call(
        landed_kernel,
        out_shape=[pltpu.HBM((replicas, rows, width), BF)] * both,
        in_specs=[ANY, ANY],
        out_specs=[HBM] * both,
        scratch_shapes=[
            pltpu.VMEM((both, replicas, rows, width), BF),
            pltpu.SemaphoreType.DMA((both, PARTS)),
            pltpu.SemaphoreType.DMA((both, PARTS)),
        ],
        compiler_params=params(),
        cost_estimate=cost(0, 4 * array.size),
        name="landed",
    )(array, after)


def passed_along(shard):
    length = lax.axis_size("section")
    return lax.ppermute(shard, "section", [(i, i - 1) for i in range(1, length)])


def other_core(shard):
    return lax.ppermute(shard, "tp", [(0, 1), (1, 0)])


def sent_out(block):
    return lax.all_to_all(block, "rep", split_axis=0, concat_axis=0, tiled=True)


def shards(inputs, loss_grad, w_in, w_out, mixing):
    segments = lax.axis_size("section")
    core = lax.axis_index("tp")
    replicas = lax.axis_size("rep")
    weight_in = w_in[0, 0]
    weight_out = w_out[0, 0]
    units = weight_in.shape[0]
    tokens = loss_grad.shape[0]
    own = tokens // 2

    other_x = other_core(inputs[0])
    other_dy = other_core(loss_grad)
    late_in, late_out, other_x, other_dy = lax.optimization_barrier((weight_in, weight_out, other_x, other_dy))
    other_in = other_core(late_in)
    other_out = other_core(late_out)
    x_rows, x_own, cot, act_t, slopes_t, own_slopes, own_in_t = opening(
        inputs[0], other_x, loss_grad, other_dy, weight_in
    )
    spread = spread_matrix(mixing)

    columns = own // CHUNKS
    halves = [first_turn(c, cot, weight_out, own_in_t, slopes_t) for c in range(CHUNKS)]
    kept_cot = [[half[0] for half in halves]]
    kept_result = [[both_parts(half[0], half[1], other_core(half[2])) for half in halves]]
    cots = [passed_along(r) for r in kept_result[0]]

    (other_out,) = kept(other_out)
    other_slopes, other_in_t = token_slopes(x_own, other_in)
    slopes, wouts, wins_t = (own_slopes, other_slopes), (weight_out, other_out), (own_in_t, other_in_t)
    for turn_index in range(1, segments - 1):
        results = [turn(cots[c], wouts, wins_t, slopes, c * columns, mixing) for c in range(CHUNKS)]
        kept_cot.append(cots)
        kept_result.append(results)
        cots = [passed_along(r) for r in results]
    kept_cot.append(cots)

    def summed(kept):
        parts = []
        for c in range(CHUNKS):
            total = kept[0][c]
            for t in range(1, segments):
                total = total + kept[t][c]
            parts.append(total)
        return parts

    mine = summed(kept_cot)
    all_cots = mine + [other_core(part) for part in mine]
    updated = update(replicas, all_cots, act_t, slopes_t, x_rows, weight_out, weight_in)
    back = sent_out(mix(spread, sent_out(updated)))

    after = updated[0, 0, :16, :128]
    kept_result.append([turn(cots[c], wouts, wins_t, slopes, c * columns, after) for c in range(CHUNKS)])
    result = jnp.concatenate(summed(kept_result), axis=1)
    width = D // 2
    mine = lax.dynamic_slice_in_dim(result, core * width, width, 0)
    theirs = other_core(lax.dynamic_slice_in_dim(result, (1 - core) * width, width, 0))
    dx = leaving(mine, theirs)
    mixed_in, mixed_out = landed(back, dx[:16, :128])
    whole = (1, 1, units, D)
    return dx[None], mixed_in.reshape(whole), mixed_out.reshape(whole)


def solution(mesh):
    in_specs = (
        P("section", "rep", "tp"),
        P("rep", "tp"),
        P("rep", "section", "tp", None),
        P("rep", "section", "tp", None),
        P(),
    )
    out_specs = (
        P("section", "rep", "tp"),
        P("rep", "section", "tp", None),
        P("rep", "section", "tp", None),
    )
    return jax.shard_map(shards, mesh=mesh, in_specs=in_specs, out_specs=out_specs, check_vma=False)
```

```python
import jax
import jax.numpy as jnp
from jax import lax
from jax.experimental import pallas as pl
from jax.experimental.pallas import tpu as pltpu
from jax.sharding import PartitionSpec as P

D = 768
FF = 3072
BF = jnp.bfloat16
F32 = jnp.float32

step_size = 4.0
root_half = 0.7071067811865476
inv_root_two_pi = 0.3989422804014327
in_scale = D ** (-0.5)
out_scale = FF ** (-0.5)

CHUNKS = 2
BLOCK = 512
MIB = 1024 * 1024
VMEM = pl.BlockSpec(memory_space=pltpu.VMEM)
HBM = pl.BlockSpec(memory_space=pltpu.HBM)
ANY = pl.BlockSpec(memory_space=pl.ANY)


def params(mib=20):
    return pltpu.CompilerParams(vmem_limit_bytes=mib * MIB)


def cost(flops, nbytes, trans=0):
    return pl.CostEstimate(flops=flops, bytes_accessed=nbytes, transcendentals=trans)


def nt(left, right):
    return lax.dot_general(left, right, (((1,), (1,)), ((), ())), preferred_element_type=F32)


def nn(left, right):
    return lax.dot_general(left, right, (((1,), (0,)), ((), ())), preferred_element_type=F32)


def gelu_parts(preact):
    normal_cdf = 0.5 * (1.0 + lax.erf(preact * root_half))
    density = jnp.exp(-0.5 * preact * preact) * inv_root_two_pi
    return preact * normal_cdf, normal_cdf + preact * density


def blocks(h):
    return [pl.ds(i * BLOCK, BLOCK) for i in range(h // BLOCK)]


def joined(core, mine, theirs):
    return jnp.where(core == 0, jnp.concatenate([mine, theirs], axis=1), jnp.concatenate([theirs, mine], axis=1))


def opening_kernel(x_hbm, other_x_hbm, dy_hbm, other_dy_hbm, w_hbm, *refs):
    whole_ref, own_x_ref, cot_ref, a_ref, s_ref, own_s_ref, t_ref = refs[:7]
    x_ref, other_x_ref, dy_ref, other_dy_ref, w_ref, sems = refs[7:]
    core = lax.axis_index("tp")
    own = own_x_ref.shape[0]
    parts = blocks(w_ref.shape[0])
    pairs = [(x_hbm, x_ref), (other_x_hbm, other_x_ref)]
    pairs += [(w_hbm.at[rows, :], w_ref.at[rows, :]) for rows in parts]
    pairs += [(dy_hbm, dy_ref), (other_dy_hbm, other_dy_ref)]
    copies = [pltpu.make_async_copy(*pair, sems.at[i]) for i, pair in enumerate(pairs)]
    for copy in copies:
        copy.start()
    for copy in copies[:2]:
        copy.wait()
    whole_ref[...] = joined(core, x_ref[...], other_x_ref[...])
    own_x_ref[...] = whole_ref[pl.ds(pl.multiple_of(core * own, own), own), :]
    x = whole_ref[...]
    for i, rows in enumerate(parts):
        copies[2 + i].wait()
        weight = w_ref[rows, :]
        values, slopes = gelu_parts(nt(weight, x) * in_scale)
        a_ref[rows, :] = values.astype(BF)
        s_ref[rows, :] = slopes
        own_s_ref[rows, :] = jnp.where(core == 0, slopes[:, :own], slopes[:, own:])
        t_ref[:, rows] = jnp.transpose(weight)
    for copy in copies[-2:]:
        copy.wait()
    dy = joined(core, dy_ref[...], other_dy_ref[...])
    last = lax.axis_index("section") == lax.axis_size("section") - 1
    cot_ref[...] = jnp.transpose(jnp.where(last, dy, jnp.zeros_like(dy)))


def opening(x, other_x, dy, other_dy, weight_in):
    m, h = dy.shape[0], weight_in.shape[0]
    own = m // 2
    shapes = [
        ((m, D), BF), ((own, D), BF), ((D, m), BF), ((h, m), BF), ((h, m), F32), ((h, own), F32), ((D, h), BF),
    ]
    return pl.pallas_call(
        opening_kernel,
        out_shape=[pltpu.VMEM(*s) for s in shapes],
        in_specs=[ANY] * 5,
        out_specs=[VMEM] * len(shapes),
        scratch_shapes=[
            *[pltpu.VMEM(dy.shape, BF)] * 4,
            pltpu.VMEM((h, D), BF),
            pltpu.SemaphoreType.DMA((4 + h // BLOCK,)),
        ],
        compiler_params=params(46),
        cost_estimate=cost(2 * m * h * D, 6 * h * D + 8 * m * h, 2 * m * h),
        name="opening",
    )(x, other_x, dy, other_dy, weight_in)


def first_turn_kernel(chunk, m, c_ref, wo_ref, wt_ref, s_ref, cot_ref, mine_ref, theirs_ref, delta):
    own = c_ref.shape[1] // 2
    core = lax.axis_index("tp")
    lanes = [pl.ds(pl.multiple_of(side * own + chunk * m, m), m) for side in (core, 1 - core)]
    cot = jnp.concatenate([c_ref[:, lane] for lane in lanes], axis=1)
    for at_rows in blocks(wo_ref.shape[0]):
        backward = nn(wo_ref[at_rows, :], cot) * out_scale
        slopes = jnp.concatenate([s_ref[at_rows, lane] for lane in lanes], axis=1)
        delta[at_rows, :] = (slopes * backward).astype(BF)
    partial = (nn(wt_ref[...], delta[...]) * in_scale).astype(BF)
    cot_ref[...] = cot[:, :m]
    mine_ref[...] = partial[:, :m]
    theirs_ref[...] = partial[:, m:]


def first_turn(chunk, cot, weight_out, weight_in_t, slopes):
    h, tokens = slopes.shape
    m = tokens // 2 // CHUNKS
    return pl.pallas_call(
        lambda *refs: first_turn_kernel(chunk, m, *refs),
        out_shape=[jax.ShapeDtypeStruct((D, m), BF)] * 3,
        in_specs=[VMEM] * 4,
        out_specs=[VMEM] * 3,
        scratch_shapes=[pltpu.VMEM((h, 2 * m), BF)],
        compiler_params=params(),
        cost_estimate=cost(8 * m * h * D, 4 * h * D + 8 * m * h),
        name="first_turn",
    )(cot, weight_out, weight_in_t, slopes)


def both_parts_kernel(c_ref, mine_ref, theirs_ref, o_ref):
    branch = mine_ref[...].astype(F32) + theirs_ref[...].astype(F32)
    o_ref[...] = (c_ref[...].astype(F32) + branch).astype(BF)


def both_parts(cot, mine, theirs):
    return pl.pallas_call(
        both_parts_kernel,
        out_shape=jax.ShapeDtypeStruct(cot.shape, BF),
        in_specs=[VMEM] * 3,
        out_specs=VMEM,
        compiler_params=params(),
        cost_estimate=cost(0, 8 * cot.size),
        name="both_parts",
    )(cot, mine, theirs)


def token_slopes_kernel(x_ref, w_ref, s_ref, t_ref):
    x = x_ref[...]
    for at in blocks(w_ref.shape[0]):
        weight = w_ref[at, :]
        s_ref[at, :] = gelu_parts(nt(weight, x) * in_scale)[1]
        t_ref[:, at] = jnp.transpose(weight)


def token_slopes(x_rows, weight_in):
    m, h = x_rows.shape[0], weight_in.shape[0]
    return pl.pallas_call(
        token_slopes_kernel,
        out_shape=[jax.ShapeDtypeStruct((h, m), F32), jax.ShapeDtypeStruct((D, h), BF)],
        in_specs=[VMEM, VMEM],
        out_specs=[VMEM, VMEM],
        compiler_params=params(),
        cost_estimate=cost(2 * m * h * D, 4 * h * D + 4 * m * h, 2 * m * h),
        name="token_slopes",
    )(x_rows, weight_in)


def kept_kernel(*refs):
    count = len(refs) // 2
    for i in range(count):
        refs[count + i][...] = refs[i][...]


def kept(*arrays, mib=20):
    return pl.pallas_call(
        kept_kernel,
        out_shape=[pltpu.VMEM(array.shape, BF) for array in arrays],
        in_specs=[VMEM] * len(arrays),
        out_specs=[VMEM] * len(arrays),
        compiler_params=params(mib),
        cost_estimate=cost(0, 4 * sum(array.size for array in arrays)),
        name="kept",
    )(*arrays)


def turn_kernel(col0, c_ref, wo0_ref, wo1_ref, wt0_ref, wt1_ref, s0_ref, s1_ref, after_ref, o_ref, delta):
    cot = c_ref[...]
    m = cot.shape[1]
    branch = None
    for wo_ref, wt_ref, s_ref in ((wo0_ref, wt0_ref, s0_ref), (wo1_ref, wt1_ref, s1_ref)):
        for at in blocks(wo_ref.shape[0]):
            backward = nn(wo_ref[at, :], cot) * out_scale
            delta[at, :] = (s_ref[at, pl.ds(col0, m)] * backward).astype(BF)
        partial = (nn(wt_ref[...], delta[...]) * in_scale).astype(BF).astype(F32)
        branch = partial if branch is None else branch + partial
    o_ref[...] = (cot.astype(F32) + branch).astype(BF)


def turn(cot, wouts, wins_t, slopes, col0, after):
    m = cot.shape[1]
    h = wouts[0].shape[0]
    return pl.pallas_call(
        lambda *refs: turn_kernel(col0, *refs),
        out_shape=jax.ShapeDtypeStruct((D, m), BF),
        in_specs=[VMEM] * 7 + [ANY],
        out_specs=VMEM,
        scratch_shapes=[pltpu.VMEM((h, m), BF)],
        compiler_params=params(),
        cost_estimate=cost(8 * m * h * D, 8 * h * D + 8 * m * h),
        name="turn",
    )(cot, wouts[0], wouts[1], wins_t[0], wins_t[1], slopes[0], slopes[1], after)


def leaving_kernel(mine_ref, theirs_ref, o_ref):
    core = lax.axis_index("tp")
    own = mine_ref.shape[1]
    o_ref[pl.ds(pl.multiple_of(core * own, own), own), :] = jnp.transpose(mine_ref[...])
    o_ref[pl.ds(pl.multiple_of((1 - core) * own, own), own), :] = jnp.transpose(theirs_ref[...])


def leaving(mine, theirs):
    width, own = mine.shape
    return pl.pallas_call(
        leaving_kernel,
        out_shape=jax.ShapeDtypeStruct((2 * own, width), BF),
        in_specs=[VMEM, VMEM],
        out_specs=VMEM,
        compiler_params=params(),
        cost_estimate=cost(0, 8 * own * width),
        name="leaving",
    )(mine, theirs)


def all_tokens(core, refs):
    mine, theirs = refs[:CHUNKS], refs[CHUNKS:]
    beside = lambda first, second: jnp.concatenate([ref[...] for ref in first + second], axis=1)
    return jnp.where(core == 0, beside(mine, theirs), beside(theirs, mine))


PARTS = 4


def update_kernel(*refs):
    a_ref, s_ref, x_ref, wo_ref, wi_ref, o_ref, scratch, sems = refs[2 * CHUNKS :]
    cot_t, x = all_tokens(lax.axis_index("tp"), refs[: 2 * CHUNKS]), x_ref[...]
    cot = jnp.transpose(cot_t)
    _, replicas, rows, _ = scratch.shape
    group = replicas // PARTS
    copies = []

    def finish(which, i, weight, grad):
        new = (weight.astype(F32) - step_size * grad).astype(BF)
        at = pl.ds(i * group, group)
        scratch[which, at] = new.reshape(group, rows, D)
        copies.append(pltpu.make_async_copy(scratch.at[which, at], o_ref.at[at, which], sems.at[which, i]))
        copies[-1].start()

    for i in range(PARTS):
        at = pl.ds(i * group * rows, group * rows)
        finish(1, i, wo_ref[at, :], nn(a_ref[at, :], cot) * out_scale)
        backward = nn(wo_ref[at, :], cot_t) * out_scale
        delta = (s_ref[at, :] * backward).astype(BF)
        finish(0, i, wi_ref[at, :], nn(delta, x) * in_scale)
    for copy in copies:
        copy.wait()


def update(replicas, cots, act_t, slopes_t, x_rows, weight_out, weight_in):
    h, m = slopes_t.shape
    rows = h // replicas
    return pl.pallas_call(
        update_kernel,
        out_shape=pltpu.HBM((replicas, 2, rows, D), BF),
        in_specs=[VMEM] * (2 * CHUNKS + 5),
        out_specs=HBM,
        scratch_shapes=[pltpu.VMEM((2, replicas, rows, D), BF), pltpu.SemaphoreType.DMA((2, PARTS))],
        compiler_params=params(24),
        cost_estimate=cost(6 * m * h * D, 6 * m * h + 8 * h * D),
        name="update",
    )(*cots, act_t, slopes_t, x_rows, weight_out, weight_in)


def mix_kernel(m_ref, u_ref, o_ref, loaded, stored, into, out_of):
    both, parts, replicas, rows, width = loaded.shape
    order = [(which, i) for which in range(both) for i in range(parts)]
    piece = lambda ref, which, i: ref.at[:, which, pl.ds(i * rows, rows), :]
    loads = [pltpu.make_async_copy(piece(u_ref, *at), loaded.at[at], into.at[at]) for at in order]
    stores = [pltpu.make_async_copy(stored.at[at], piece(o_ref, *at), out_of.at[at]) for at in order]
    for load in loads:
        load.start()
    for at, load, store in zip(order, loads, stores):
        load.wait()
        mixed = nn(m_ref[...], loaded[at].reshape(replicas * rows, width))
        stored[at] = mixed.astype(BF).reshape(replicas, rows, width)
        store.start()
    for store in stores:
        store.wait()


def mix(spread, pieces):
    replicas, both, rows, width = pieces.shape
    block = 16
    parts = rows // block
    n = spread.shape[0]
    return pl.pallas_call(
        mix_kernel,
        out_shape=pltpu.HBM(pieces.shape, BF),
        in_specs=[VMEM, ANY],
        out_specs=HBM,
        scratch_shapes=[pltpu.VMEM((both, parts, replicas, block, width), BF)] * 2
        + [pltpu.SemaphoreType.DMA((both, parts))] * 2,
        compiler_params=params(),
        cost_estimate=cost(2 * n * n * width * both * parts, 4 * pieces.size + 2 * n * n),
        name="mix",
    )(spread, pieces)


def spread_kernel(m_ref, o_ref):
    n, replicas = o_ref.shape[0], m_ref.shape[0]
    narrow = n // replicas

    def chosen(shape, along):
        group = lax.broadcasted_iota(jnp.int32, shape, along) // narrow
        return jnp.where(lax.broadcasted_iota(jnp.int32, shape, 1 - along) == group, 1.0, 0.0).astype(BF)

    rows, columns = chosen((n, replicas), 0), chosen((replicas, n), 1)
    same = lax.broadcasted_iota(jnp.int32, (n, n), 0) % narrow == lax.broadcasted_iota(jnp.int32, (n, n), 1) % narrow
    spread = nn(nn(rows, m_ref[...].astype(BF)).astype(BF), columns)
    o_ref[...] = jnp.where(same, spread, 0.0).astype(BF)


def spread_matrix(matrix):
    n = 16 * matrix.shape[0]
    return pl.pallas_call(
        spread_kernel,
        out_shape=jax.ShapeDtypeStruct((n, n), BF),
        in_specs=[VMEM],
        out_specs=VMEM,
        compiler_params=params(),
        cost_estimate=cost(2 * n * n * matrix.shape[0], 4 * n * n),
        name="spread",
    )(matrix)


def landed_kernel(u_ref, after_ref, in_ref, out_ref, held, into, out_of):
    group = u_ref.shape[0] // PARTS
    loads, stores = [], []
    for which, o_ref in enumerate((in_ref, out_ref)):
        for i in range(PARTS):
            at = pl.ds(i * group, group)
            loads.append(pltpu.make_async_copy(u_ref.at[at, which], held.at[which, at], into.at[which, i]))
            stores.append(pltpu.make_async_copy(held.at[which, at], o_ref.at[at], out_of.at[which, i]))
    for load in loads:
        load.start()
    for load, store in zip(loads, stores):
        load.wait()
        store.start()
    for store in stores:
        store.wait()


def landed(array, after):
    replicas, both, rows, width = array.shape
    return pl.pallas_call(
        landed_kernel,
        out_shape=[pltpu.HBM((replicas, rows, width), BF)] * both,
        in_specs=[ANY, ANY],
        out_specs=[HBM] * both,
        scratch_shapes=[
            pltpu.VMEM((both, replicas, rows, width), BF),
            pltpu.SemaphoreType.DMA((both, PARTS)),
            pltpu.SemaphoreType.DMA((both, PARTS)),
        ],
        compiler_params=params(),
        cost_estimate=cost(0, 4 * array.size),
        name="landed",
    )(array, after)


def passed_along(shard):
    length = lax.axis_size("section")
    return lax.ppermute(shard, "section", [(i, i - 1) for i in range(1, length)])


def other_core(shard):
    return lax.ppermute(shard, "tp", [(0, 1), (1, 0)])


def sent_out(block):
    return lax.all_to_all(block, "rep", split_axis=0, concat_axis=0, tiled=True)


def shards(inputs, loss_grad, w_in, w_out, mixing):
    segments = lax.axis_size("section")
    core = lax.axis_index("tp")
    replicas = lax.axis_size("rep")
    weight_in = w_in[0, 0]
    weight_out = w_out[0, 0]
    units = weight_in.shape[0]
    tokens = loss_grad.shape[0]
    own = tokens // 2

    other_x = other_core(inputs[0])
    other_dy = other_core(loss_grad)
    late_in, late_out, other_x, other_dy = lax.optimization_barrier((weight_in, weight_out, other_x, other_dy))
    other_in = other_core(late_in)
    other_out = other_core(late_out)
    x_rows, x_own, cot, act_t, slopes_t, own_slopes, own_in_t = opening(
        inputs[0], other_x, loss_grad, other_dy, weight_in
    )
    spread = spread_matrix(mixing)

    columns = own // CHUNKS
    halves = [first_turn(c, cot, weight_out, own_in_t, slopes_t) for c in range(CHUNKS)]
    kept_cot = [[half[0] for half in halves]]
    kept_result = [[both_parts(half[0], half[1], other_core(half[2])) for half in halves]]
    cots = [passed_along(r) for r in kept_result[0]]

    other_in, other_out = kept(other_in, other_out)
    other_slopes, other_in_t = token_slopes(x_own, other_in)
    slopes, wouts, wins_t = (own_slopes, other_slopes), (weight_out, other_out), (own_in_t, other_in_t)
    for turn_index in range(1, segments - 1):
        results = [turn(cots[c], wouts, wins_t, slopes, c * columns, mixing) for c in range(CHUNKS)]
        kept_cot.append(cots)
        kept_result.append(results)
        cots = [passed_along(r) for r in results]
    kept_cot.append(cots)

    def summed(kept):
        parts = []
        for c in range(CHUNKS):
            total = kept[0][c]
            for t in range(1, segments):
                total = total + kept[t][c]
            parts.append(total)
        return parts

    mine = summed(kept_cot)
    all_cots = mine + [other_core(part) for part in mine]
    updated = update(replicas, all_cots, act_t, slopes_t, x_rows, weight_out, weight_in)
    back = sent_out(mix(spread, sent_out(updated)))

    after = updated[0, 0, :16, :128]
    kept_result.append([turn(cots[c], wouts, wins_t, slopes, c * columns, after) for c in range(CHUNKS)])
    result = jnp.concatenate(summed(kept_result), axis=1)
    width = D // 2
    mine = lax.dynamic_slice_in_dim(result, core * width, width, 0)
    theirs = other_core(lax.dynamic_slice_in_dim(result, (1 - core) * width, width, 0))
    dx = leaving(mine, theirs)
    mixed_in, mixed_out = landed(back, dx[:16, :128])
    whole = (1, 1, units, D)
    return dx[None], mixed_in.reshape(whole), mixed_out.reshape(whole)


def solution(mesh):
    in_specs = (
        P("section", "rep", "tp"),
        P("rep", "tp"),
        P("rep", "section", "tp", None),
        P("rep", "section", "tp", None),
        P(),
    )
    out_specs = (
        P("section", "rep", "tp"),
        P("rep", "section", "tp", None),
        P("rep", "section", "tp", None),
    )
    return jax.shard_map(shards, mesh=mesh, in_specs=in_specs, out_specs=out_specs, check_vma=False)
```
